32 devices in a mesh: rep: 4 (over y, x), fsdp: 8 (over z, core).
Axes of the slice: x: 2, y: 2, z: 4, core: 2. Of those that a mesh axis runs over, the one named last changes fastest.
Arguments:
- tokens: bfloat16 [65536, 768], P(('rep', 'fsdp')), may hold values from -6 to 6
- segment_ids: int32 [64, 1024], P(('rep', 'fsdp')), may hold values from 0 to 5, as said below
- valid_mask: int32 [64, 1024], P(('rep', 'fsdp')), may hold values from 0 to 1, as said below
- cotangent: bfloat16 [65536, 768], P(('rep', 'fsdp')), may hold values from -6 to 6
- norm1_gain: bfloat16 [768], P('fsdp'), may hold values from 0.099609375 to 1.8984375
- norm1_bias: bfloat16 [768], P('fsdp'), may hold values from -1.5 to 1.5
- qkv_weight: bfloat16 [768, 2304], P('fsdp'), may hold values from -0.21875 to 0.21875
- query_bias: bfloat16 [768], P('fsdp'), may hold values from -1.5 to 1.5
- value_bias: bfloat16 [768], P('fsdp'), may hold values from -1.5 to 1.5
- proj_weight: bfloat16 [768, 768], P('fsdp'), may hold values from -1.75 to 1.75
- proj_bias: bfloat16 [768], P('fsdp'), may hold values from -1.5 to 1.5
- norm2_gain: bfloat16 [768], P('fsdp'), may hold values from 0.099609375 to 1.8984375
- norm2_bias: bfloat16 [768], P('fsdp'), may hold values from -1.5 to 1.5
- expand_weight: bfloat16 [768, 3072], P('fsdp'), may hold values from -0.21875 to 0.21875
- expand_bias: bfloat16 [3072], P('fsdp'), may hold values from -1.5 to 1.5
- reduce_weight: bfloat16 [3072, 768], P('fsdp'), may hold values from -0.109375 to 0.109375
- reduce_bias: bfloat16 [768], P('fsdp'), may hold values from -1.5 to 1.5
Outputs:
- output: bfloat16 [65536, 768], P(('rep', 'fsdp'))
- input_grad: bfloat16 [65536, 768], P(('rep', 'fsdp'))
- grad_norm1_gain: float32 [768], P('fsdp')
- grad_norm1_bias: float32 [768], P('fsdp')
- grad_qkv_weight: float32 [768, 2304], P('fsdp')
- grad_query_bias: float32 [768], P('fsdp')
- grad_value_bias: float32 [768], P('fsdp')
- grad_proj_weight: float32 [768, 768], P('fsdp')
- grad_proj_bias: float32 [768], P('fsdp')
- grad_norm2_gain: float32 [768], P('fsdp')
- grad_norm2_bias: float32 [768], P('fsdp')
- grad_expand_weight: float32 [768, 3072], P('fsdp')
- grad_expand_bias: float32 [3072], P('fsdp')
- grad_reduce_weight: float32 [3072, 768], P('fsdp')
- grad_reduce_bias: float32 [768], P('fsdp')
The draws below stay inside these ranges and needn't reach their ends.
Inputs may be any that keep to these rules, and one draw needn't show every extreme that they name: `segment_ids`: clip number of each row; along a sequence it never falls, each of the 6 clips holds one contiguous run of rows, and every clip of every sequence is present. `valid_mask`: inside each clip's rows the valid rows come first and padding rows follow; every clip has valid rows, and the last clip of every sequence ends in padding.
All inputs are finite; a program needn't handle non-finite values.
Results may differ from the reference program's by a relative error of at most 0.019.
Values may be sent and summed in bfloat16 or wider, within the bound.
No kernel may reach another device: no remote copies, remote signals or barrier semaphores. Data moves between devices by JAX's collectives and lax.ppermute only.
A program may use at most 448 MiB of HBM per device.

```python
import jax
import jax.numpy as jnp
from jax import lax

D = 768
HEADS = 12
FF = 3072
LENGTH = 1024
CLIPS = 6
SEQS = 64
TOKENS = 65536


def clip_table(key):
    size_key, pad_key = jax.random.split(key)
    lowest = LENGTH // CLIPS - LENGTH // 48
    sizes = jax.random.randint(size_key, (SEQS, CLIPS - 1), lowest, lowest + LENGTH // 24 + 1)
    remainder = LENGTH - jnp.sum(sizes, axis=1, keepdims=True)
    sizes = jnp.concatenate([sizes, remainder], axis=1).astype(jnp.int32)
    padding = jax.random.randint(pad_key, (SEQS, CLIPS), 0, LENGTH // 48 + 1).astype(jnp.int32)
    last_clip = (jnp.arange(CLIPS) == CLIPS - 1).astype(jnp.int32)
    padding = padding + last_clip[None, :] * (padding == 0).astype(jnp.int32)
    clip_ends = jnp.cumsum(sizes, axis=1)
    position = jnp.arange(LENGTH, dtype=jnp.int32)
    segments = jnp.sum((position[None, :, None] >= clip_ends[:, None, :]).astype(jnp.int32), axis=2).astype(jnp.int32)
    starts = clip_ends - sizes
    clip_start = jnp.take_along_axis(starts, segments, axis=1)
    clip_valid = jnp.take_along_axis(sizes - padding, segments, axis=1)
    validity = (position[None, :] - clip_start < clip_valid).astype(jnp.int32)
    return (segments, validity)


def draw_segment_ids(key, part):
    table = clip_table(key)
    return table[0]


def draw_valid_mask(key, part):
    table = clip_table(key)
    return table[1]


def levels(stream_key, extent, pieces, least, high):
    gain = 1.0
    for dim, parts in pieces:
        steps = jax.random.uniform(jax.random.fold_in(jax.random.fold_in(stream_key, 6), dim), (parts,), jnp.float32, least / len(pieces), high / len(pieces))
        gain = gain * jnp.repeat(jnp.exp(steps), extent[dim] // parts).reshape((-1,) + (1,) * (len(extent) - 1 - dim))
    return gain


def normal_values(key, extent, scale, most, shards=(), held_as=jnp.bfloat16):
    factor_of = levels(key, extent, shards, -0.22, 0.18) if shards else 1.0
    entries = jax.random.normal(key, extent, jnp.float32) * scale * factor_of
    return jnp.minimum(jnp.maximum(entries, -most), most).astype(held_as)


def setup_inputs(seed: int = 0) -> dict:
    keys = jax.random.split(jax.random.key(seed), 18)
    return {
        "tokens": normal_values(keys[0], (TOKENS, D), 1.0, 6.0, ((0, 32),)),
        "segment_ids": draw_segment_ids(jax.random.fold_in(keys[17], 71), 0),
        "valid_mask": draw_valid_mask(jax.random.fold_in(keys[17], 71), 0),
        "cotangent": normal_values(keys[3], (TOKENS, D), 1.0, 6.0, ((0, 32),)),
        "norm1_gain": jnp.clip(1.0 + 0.18 * jax.random.normal(keys[4], (D,), jnp.float32), 0.099609375, 1.8984375).astype(jnp.bfloat16),
        "norm1_bias": normal_values(keys[5], (D,), 0.3, 1.5, ((0, 8),)),
        "qkv_weight": normal_values(keys[6], (D, 3 * D), D ** -0.5, 0.21875, ((0, 8),)),
        "query_bias": normal_values(keys[7], (D,), 0.3, 1.5, ((0, 8),)),
        "value_bias": normal_values(keys[8], (D,), 0.3, 1.5, ((0, 8),)),
        "proj_weight": normal_values(keys[9], (D, D), (D // 64) ** -0.5, 1.75, ((0, 8),)),
        "proj_bias": normal_values(keys[10], (D,), 0.3, 1.5, ((0, 8),)),
        "norm2_gain": jnp.clip(1.0 + 0.18 * jax.random.normal(keys[11], (D,), jnp.float32), 0.099609375, 1.8984375).astype(jnp.bfloat16),
        "norm2_bias": normal_values(keys[12], (D,), 0.3, 1.5, ((0, 8),)),
        "expand_weight": normal_values(keys[13], (D, FF), D ** -0.5, 0.21875, ((0, 8),)),
        "expand_bias": normal_values(keys[14], (FF,), 0.3, 1.5, ((0, 8),)),
        "reduce_weight": normal_values(keys[15], (FF, D), FF ** -0.5, 0.109375, ((0, 8),)),
        "reduce_bias": normal_values(keys[16], (D,), 0.3, 1.5, ((0, 8),)),
    }


@jax.custom_vjp
def low(v):
    return lax.optimization_barrier(v.astype(jnp.bfloat16)).astype(jnp.float32)

@jax.custom_vjp
def low_back(v):
    return v

def low_keep(v):
    return (low(v), None)

def low_pass(kept, grad):
    return (grad,)

def back_keep(v):
    return (v, None)

def back_low(kept, grad):
    return (low(grad),)
low.defvjp(low_keep, low_pass)
low_back.defvjp(back_keep, back_low)
epsilon = 1e-06
exact_mode = lax.Precision.HIGHEST

def layer_norm(inputs, norm_gain, norm_shift):
    row_mean = lax.optimization_barrier(jnp.mean(inputs, axis=-1, keepdims=True))
    centred = inputs - row_mean
    row_var = lax.optimization_barrier(jnp.mean(centred * centred, axis=-1, keepdims=True))
    return centred * lax.rsqrt(row_var + epsilon) * norm_gain + norm_shift

def sequence_layer(params, inputs, segments, validity):
    gain_one, shift_one, qkv_matrix, query_shift, value_shift, proj_matrix, proj_shift, gain_two, shift_two, expand_matrix, expand_shift, reduce_matrix, reduce_shift = params
    seq_len = inputs.shape[0]
    model_width = inputs.shape[1]
    head_size = model_width // HEADS
    score_scale = head_size ** (-0.5)
    normed1 = low(layer_norm(inputs, gain_one, shift_one))
    projected = jnp.dot(normed1, qkv_matrix, precision=exact_mode)
    queries = low(low_back(projected[:, :model_width] + query_shift))
    key_rows = low(low_back(projected[:, model_width:2 * model_width]))
    value_rows = low(low_back(projected[:, 2 * model_width:] + value_shift))
    query_heads = queries.reshape(seq_len, HEADS, head_size)
    key_heads = key_rows.reshape(seq_len, HEADS, head_size)
    value_heads = value_rows.reshape(seq_len, HEADS, head_size)
    scores = low_back(jnp.einsum('qhd,khd->hqk', query_heads, key_heads, precision=exact_mode) * score_scale)
    allowed = (segments[:, None] == segments[None, :]) & (validity[None, :] == 1)
    masked = jnp.where(allowed[None], scores, -1e+30)
    highest = lax.optimization_barrier(jnp.max(masked, axis=-1, keepdims=True))
    exponent = jnp.where(allowed[None], jnp.exp(masked - highest), 0.0)
    attn_weights = low(exponent / lax.optimization_barrier(jnp.sum(exponent, axis=-1, keepdims=True)))
    mixed = jnp.einsum('hqk,khd->qhd', attn_weights, value_heads, precision=exact_mode).reshape(seq_len, model_width)
    mixed = low(low_back(mixed))
    attended = low_back(jnp.dot(mixed, proj_matrix, precision=exact_mode) + proj_shift)
    middle = inputs + attended
    normed2 = low(layer_norm(middle, gain_two, shift_two))
    preact = low_back(jnp.dot(normed2, expand_matrix, precision=exact_mode) + expand_shift)
    activated = low(jax.nn.gelu(preact, approximate=False))
    branch = low_back(jnp.dot(activated, reduce_matrix, precision=exact_mode) + reduce_shift)
    return middle + branch

def reference(tokens, segment_ids, valid_mask, cotangent, norm1_gain, norm1_bias, qkv_weight, query_bias, value_bias, proj_weight, proj_bias, norm2_gain, norm2_bias, expand_weight, expand_bias, reduce_weight, reduce_bias):
    params = tuple((entry.astype(jnp.float32) for entry in (norm1_gain, norm1_bias, qkv_weight, query_bias, value_bias, proj_weight, proj_bias, norm2_gain, norm2_bias, expand_weight, expand_bias, reduce_weight, reduce_bias)))

    def forward(weights, inputs):
        blocks = inputs.reshape(SEQS, LENGTH, D)
        seq_step = jax.checkpoint(sequence_layer)

        def per_sequence(packed):
            return seq_step(weights, packed[0], packed[1], packed[2])
        results = lax.map(per_sequence, (blocks, segment_ids, valid_mask))
        return results.reshape(SEQS * LENGTH, D)
    output, pullback = jax.vjp(forward, params, tokens.astype(jnp.float32))
    param_grads, input_grad = pullback(cotangent.astype(jnp.float32))
    grad_norm1_gain, grad_norm1_bias, grad_qkv_weight, grad_query_bias, grad_value_bias, grad_proj_weight, grad_proj_bias, grad_norm2_gain, grad_norm2_bias, grad_expand_weight, grad_expand_bias, grad_reduce_weight, grad_reduce_bias = param_grads
    return (output.astype(jnp.bfloat16), input_grad.astype(jnp.bfloat16), grad_norm1_gain, grad_norm1_bias, grad_qkv_weight, grad_query_bias, grad_value_bias, grad_proj_weight, grad_proj_bias, grad_norm2_gain, grad_norm2_bias, grad_expand_weight, grad_expand_bias, grad_reduce_weight, grad_reduce_bias)
```

```python
import functools

import jax
import jax.numpy as jnp
from jax import lax
from jax.experimental import pallas as pl
from jax.experimental.pallas import tpu as pltpu
from jax.sharding import PartitionSpec as P

HEADS = 12
CLIPS = 6
EPSILON = 1e-06
WINDOW = 256
FIELDS = 5
BF16 = jnp.bfloat16
F32 = jnp.float32
MEBI = 1024 * 1024
NEGATIVE = -1e30


def dot(left, right):
    return lax.dot_general(left, right, (((1,), (0,)), ((), ())), preferred_element_type=F32)


def dot_nt(left, right):
    return lax.dot_general(left, right, (((1,), (1,)), ((), ())), preferred_element_type=F32)


def dot_tn(left, right):
    return lax.dot_general(left, right, (((0,), (0,)), ((), ())), preferred_element_type=F32)


def resident(shape):
    zeros = (0,) * len(shape)
    return pl.BlockSpec(shape, lambda *_: zeros, pipeline_mode=pl.Buffered(1))


def params(limit, count=1):
    return pltpu.CompilerParams(
        vmem_limit_bytes=limit * MEBI, dimension_semantics=("arbitrary",) * count
    )


def normalise(values):
    row_mean = jnp.mean(values, axis=-1, keepdims=True)
    centred = values - row_mean
    row_var = jnp.mean(centred * centred, axis=-1, keepdims=True)
    scale = lax.rsqrt(row_var + EPSILON)
    return centred * scale, scale


def norm_back(upstream, gain, xhat, scale):
    weighted = upstream * gain
    first = jnp.mean(weighted, axis=-1, keepdims=True)
    second = jnp.mean(weighted * xhat, axis=-1, keepdims=True)
    return scale * (weighted - first - xhat * second)


def qkv_kernel(tokens, vecs, weight, qkv, normed):
    width = tokens.shape[1]
    xhat, _ = normalise(tokens[...].astype(F32))
    rows = (xhat * vecs[0:1, :] + vecs[1:2, :]).astype(BF16)
    normed[...] = rows
    query = dot(rows, weight[:, :width]) + vecs[2:3, :]
    qkv[:, :width] = query.astype(BF16) * jnp.asarray(0.125, BF16)
    qkv[:, width : 2 * width] = dot(rows, weight[:, width : 2 * width]).astype(BF16)
    value = dot(rows, weight[:, 2 * width :]) + vecs[3:4, :]
    qkv[:, 2 * width :] = value.astype(BF16)


def qkv_forward(tokens, vecs, weight, block=512):
    rows, width = tokens.shape
    return pl.pallas_call(
        qkv_kernel,
        grid=(rows // block,),
        in_specs=[
            pl.BlockSpec((block, width), lambda i: (i, 0)),
            resident(vecs.shape),
            resident(weight.shape),
        ],
        out_specs=[
            pl.BlockSpec((block, 3 * width), lambda i: (i, 0)),
            pl.BlockSpec((block, width), lambda i: (i, 0)),
        ],
        out_shape=[
            jax.ShapeDtypeStruct((rows, 3 * width), BF16),
            jax.ShapeDtypeStruct((rows, width), BF16),
        ],
        compiler_params=params(40),
    )(tokens, vecs, weight)


def clip_table(segment_ids, valid_mask):
    seq_len = segment_ids.shape[1]
    clips = jnp.arange(CLIPS, dtype=jnp.int32)[None, :, None]
    segments = segment_ids[:, None, :]
    start = jnp.sum((segments < clips).astype(jnp.int32), axis=2)
    end = jnp.sum((segments <= clips).astype(jnp.int32), axis=2)
    valid = jnp.sum(((segments == clips) & (valid_mask[:, None, :] == 1)).astype(jnp.int32), axis=2)
    aligned = start // 16 * 16
    need = end - aligned
    path = (need > WINDOW).astype(jnp.int32) + (need > 2 * WINDOW).astype(jnp.int32)
    window = jnp.where(path == 0, WINDOW, jnp.where(path == 1, 2 * WINDOW, seq_len))
    base = jnp.minimum(aligned, seq_len - window)
    return jnp.stack([base, path, start - base, end - base, start + valid - base], axis=2).reshape(
        -1
    )


def lane_low(rows):
    return lax.broadcasted_iota(jnp.int32, (rows, 128), 1) < 64


def flag_lane(rows):
    return lax.broadcasted_iota(jnp.int32, (rows, 128), 1) % 64 == 0


def row_mask(rows, offset, first, last):
    index = lax.broadcasted_iota(jnp.int32, (rows, 128), 0) + offset
    return (index >= first) & (index < last)


def key_extra(rows, first, last):
    bias = jnp.where(row_mask(rows, 0, first, last), 0.0, NEGATIVE)
    return jnp.where(flag_lane(rows), bias, 0.0).astype(BF16)


def query_extra(rows):
    return jnp.where(flag_lane(rows), 1.0, 0.0).astype(BF16)


def weights_of(query, keys, extra_query, extra_keys, low, low_keys, head):
    if head == 0:
        left = jnp.where(low, query, extra_query)
        right = jnp.where(low_keys, keys, extra_keys)
    else:
        left = jnp.where(low, extra_query, query)
        right = jnp.where(low_keys, extra_keys, keys)
    scores = dot_nt(left, right)
    return jnp.exp(scores - jnp.max(scores, axis=1, keepdims=True)).astype(BF16)


def attend_window(refs, base, first, last, valid_end, window, pairs, exps, clip):
    queries, keys_ref, values_ref, mixed, inverse = refs
    chunk = WINDOW
    low = lane_low(chunk)
    low_keys = lane_low(window)
    extra_keys = key_extra(window, first, valid_end)
    extra_query = query_extra(chunk)
    ones = jnp.ones((window, 128), BF16)
    key_rows = pl.ds(base, window)

    def one_chunk(offset, row_start):
        rows = pl.ds(row_start, chunk)
        keep = row_mask(chunk, offset, first, last)
        for pair in range(pairs):
            lanes = pl.ds(128 * pair, 128)
            query = queries[rows, lanes]
            keys = keys_ref[key_rows, lanes]
            stack = jnp.concatenate([values_ref[key_rows, lanes], ones], axis=1)
            sums = []
            for head in range(2):
                weights = weights_of(query, keys, extra_query, extra_keys, low, low_keys, head)
                if exps is not None:
                    exps[0, 2 * pair + head, pl.ds(clip * WINDOW, WINDOW), :] = weights
                sums.append(dot(weights, stack))
            total = jnp.where(low, sums[0][:, 128:], sums[1][:, 128:])
            weighted = jnp.where(low, sums[0][:, :128], sums[1][:, :128])
            reciprocal = 1.0 / total
            mixed[rows, lanes] = jnp.where(
                keep, (weighted * reciprocal), mixed[rows, lanes].astype(F32)
            ).astype(BF16)
            inverse[rows, lanes] = jnp.where(keep, reciprocal, inverse[rows, lanes])

    if window == chunk:
        one_chunk(0, base)
    else:

        def step(index, carry):
            offset = index * chunk
            one_chunk(offset, pl.multiple_of(base + offset, 16))
            return carry

        lax.fori_loop(0, window // chunk, step, 0)


def clip_fields(table, sequence, clip):
    at = (sequence * CLIPS + clip) * FIELDS
    base = pl.multiple_of(table[at], 16)
    return base, table[at + 1], table[at + 2], table[at + 3], table[at + 4]


def attend_kernel(pairs, table, queries, keys, values, mixed, inverse, exps):
    sequence = pl.program_id(0)
    seq_len = queries.shape[0]
    mixed[...] = jnp.zeros_like(mixed)
    inverse[...] = jnp.zeros_like(inverse)
    refs = (queries, keys, values, mixed, inverse)

    def one_clip(clip, carry):
        base, path, first, last, valid_end = clip_fields(table, sequence, clip)
        for number, window in enumerate((WINDOW, 2 * WINDOW, seq_len)):

            @pl.when(path == number)
            def _():
                attend_window(
                    refs,
                    base,
                    first,
                    last,
                    valid_end,
                    window,
                    pairs,
                    exps if number == 0 else None,
                    clip,
                )

        return carry

    lax.fori_loop(0, CLIPS, one_clip, 0)


def attend_forward(table, qkv, seq_len, pairs=2):
    rows = qkv.shape[0]
    width = qkv.shape[1] // 3
    seqs = rows // seq_len
    lanes = 128 * pairs
    groups = width // lanes
    block = (seq_len, lanes)
    return pl.pallas_call(
        functools.partial(attend_kernel, pairs),
        grid_spec=pltpu.PrefetchScalarGridSpec(
            num_scalar_prefetch=1,
            grid=(seqs, groups),
            in_specs=[
                pl.BlockSpec(block, lambda s, g, t: (s, g)),
                pl.BlockSpec(block, lambda s, g, t: (s, groups + g)),
                pl.BlockSpec(block, lambda s, g, t: (s, 2 * groups + g)),
            ],
            out_specs=[
                pl.BlockSpec(block, lambda s, g, t: (s, g)),
                pl.BlockSpec(block, lambda s, g, t: (s, g)),
                pl.BlockSpec((1, 2 * pairs, CLIPS * WINDOW, WINDOW), lambda s, g, t: (s, g, 0, 0)),
            ],
        ),
        out_shape=[
            jax.ShapeDtypeStruct((rows, width), BF16),
            jax.ShapeDtypeStruct((rows, width), F32),
            jax.ShapeDtypeStruct((seqs, HEADS, CLIPS * WINDOW, WINDOW), BF16),
        ],
        compiler_params=params(48, 2),
    )(table, qkv, qkv, qkv)


def back_window(refs, base, first, last, valid_end, window, pairs, exps, clip, gather):
    queries, keys_ref, values_ref, grads, mixed, inverse, dq, dk, dv = refs
    key_grad, value_grad = gather
    chunk = WINDOW
    single = window == chunk
    low = lane_low(chunk)
    low_keys = lane_low(window)
    extra_keys = None if single else key_extra(window, first, valid_end)
    extra_query = None if single else query_extra(chunk)
    key_rows = pl.ds(base, window)
    one = jnp.ones((window, 128), BF16)

    def one_chunk(offset, row_start):
        rows = pl.ds(row_start, chunk)
        keep = row_mask(chunk, offset, first, last)
        for pair in range(pairs):
            lanes = pl.ds(128 * pair, 128)
            query = queries[rows, lanes]
            keys = keys_ref[key_rows, lanes]
            values = values_ref[key_rows, lanes]
            scaled = jnp.where(keep, grads[rows, lanes].astype(F32) * inverse[rows, lanes], 0.0)
            product = scaled * mixed[rows, lanes].astype(F32)
            turned = pltpu.roll(-product, 64, 1).astype(BF16)
            scaled = scaled.astype(BF16)
            parts = []
            for head in range(2):
                if head == 0:
                    left = jnp.where(low, scaled, turned)
                    right = jnp.where(low_keys, values, one)
                else:
                    left = jnp.where(low, turned, scaled)
                    right = jnp.where(low_keys, one, values)
                if single:
                    weights = exps[0, 2 * pair + head, pl.ds(clip * WINDOW, WINDOW), :]
                else:
                    weights = weights_of(query, keys, extra_query, extra_keys, low, low_keys, head)
                grad_scores = (weights.astype(F32) * dot_nt(left, right)).astype(BF16)
                parts.append(
                    (
                        dot(grad_scores, keys),
                        dot_tn(grad_scores, query),
                        dot_tn(weights, scaled),
                    )
                )
            query_part = jnp.where(low, parts[0][0], parts[1][0]) * 0.125
            key_part = jnp.where(low_keys, parts[0][1], parts[1][1])
            value_part = jnp.where(low_keys, parts[0][2], parts[1][2])
            dq[rows, lanes] = jnp.where(keep, query_part, dq[rows, lanes].astype(F32)).astype(BF16)
            if single:
                dk[rows, lanes] = jnp.where(keep, key_part, dk[rows, lanes].astype(F32)).astype(
                    BF16
                )
                dv[rows, lanes] = jnp.where(keep, value_part, dv[rows, lanes].astype(F32)).astype(
                    BF16
                )
            else:
                key_grad[pl.ds(0, window), lanes] += key_part
                value_grad[pl.ds(0, window), lanes] += value_part

    if single:
        one_chunk(0, base)
        return
    key_grad[...] = jnp.zeros_like(key_grad)
    value_grad[...] = jnp.zeros_like(value_grad)

    def step(index, carry):
        offset = index * chunk
        one_chunk(offset, pl.multiple_of(base + offset, 16))
        return carry

    lax.fori_loop(0, window // chunk, step, 0)
    keep = row_mask(window, 0, first, last)
    for pair in range(pairs):
        lanes = pl.ds(128 * pair, 128)
        for ref, total in ((dk, key_grad), (dv, value_grad)):
            ref[key_rows, lanes] = jnp.where(
                keep, total[pl.ds(0, window), lanes], ref[key_rows, lanes].astype(F32)
            ).astype(BF16)


def back_kernel(
    pairs,
    table,
    queries,
    keys,
    values,
    grads,
    mixed,
    inverse,
    exps,
    dq,
    dk,
    dv,
    key_grad,
    value_grad,
):
    sequence = pl.program_id(0)
    seq_len = queries.shape[0]
    for ref in (dq, dk, dv):
        ref[...] = jnp.zeros_like(ref)
    refs = (queries, keys, values, grads, mixed, inverse, dq, dk, dv)

    def one_clip(clip, carry):
        base, path, first, last, valid_end = clip_fields(table, sequence, clip)
        for number, window in enumerate((WINDOW, 2 * WINDOW, seq_len)):

            @pl.when(path == number)
            def _():
                back_window(
                    refs,
                    base,
                    first,
                    last,
                    valid_end,
                    window,
                    pairs,
                    exps,
                    clip,
                    (key_grad, value_grad),
                )

        return carry

    lax.fori_loop(0, CLIPS, one_clip, 0)


def attend_backward(table, qkv, grads, mixed, inverse, exps, seq_len, pairs=2):
    rows, width = mixed.shape
    seqs = rows // seq_len
    lanes = 128 * pairs
    groups = width // lanes
    block = (seq_len, lanes)
    own = pl.BlockSpec(block, lambda s, g, t: (s, g))
    shape = jax.ShapeDtypeStruct((rows, width), BF16)
    return pl.pallas_call(
        functools.partial(back_kernel, pairs),
        grid_spec=pltpu.PrefetchScalarGridSpec(
            num_scalar_prefetch=1,
            grid=(seqs, groups),
            in_specs=[
                own,
                pl.BlockSpec(block, lambda s, g, t: (s, groups + g)),
                pl.BlockSpec(block, lambda s, g, t: (s, 2 * groups + g)),
                own,
                own,
                own,
                pl.BlockSpec((1, 2 * pairs, CLIPS * WINDOW, WINDOW), lambda s, g, t: (s, g, 0, 0)),
            ],
            out_specs=[own, own, own],
            scratch_shapes=[pltpu.VMEM(block, F32), pltpu.VMEM(block, F32)],
        ),
        out_shape=[shape, shape, shape],
        compiler_params=params(48, 2),
    )(table, qkv, qkv, qkv, grads, mixed, inverse, exps)


def gauss(value):
    size = jnp.abs(value)
    rate = 1.0 / (1.0 + 0.3275911 * 0.7071067811865476 * size)
    tail = jnp.exp(value * value * -0.5)
    series = rate * (
        0.5 * 0.254829592
        + rate
        * (
            0.5 * -0.284496736
            + rate * (0.5 * 1.421413741 + rate * (0.5 * -1.453152027 + rate * (0.5 * 1.061405429)))
        )
    )
    upper = series * tail
    return jnp.where(value >= 0, 1.0 - upper, upper), value * tail * 0.3989422804014327


def middle_kernel(
    part,
    tokens,
    mixed,
    cotangent,
    vecs,
    ebias,
    proj,
    expand,
    reduce,
    output,
    grad_middle,
    grad_mixed,
    grad_proj,
    grad_expand,
    grad_reduce,
    grad_ebias,
    grad_vecs,
    sum_proj,
    sum_expand,
    sum_reduce,
):
    step = pl.program_id(0)
    hidden = expand.shape[1]

    @pl.when(step == 0)
    def _():
        sum_proj[...] = jnp.zeros_like(sum_proj)
        sum_expand[...] = jnp.zeros_like(sum_expand)
        sum_reduce[...] = jnp.zeros_like(sum_reduce)
        grad_ebias[...] = jnp.zeros_like(grad_ebias)
        grad_vecs[...] = jnp.zeros_like(grad_vecs)

    mixed_rows = mixed[...]
    cot = cotangent[...]
    middle = tokens[...].astype(F32) + dot(mixed_rows, proj[...]) + vecs[4:5, :]
    xhat, scale = normalise(middle)
    normed = (xhat * vecs[5:6, :] + vecs[6:7, :]).astype(BF16)
    normed_t = normed.T
    branch = None
    grad_normed = None
    for start in range(0, hidden, part):
        cols = pl.ds(start, part)
        into = expand[:, cols]
        back = reduce[cols, :]
        preact = dot(normed, into) + ebias[:, cols]
        cdf, slope = gauss(preact)
        activated = (preact * cdf).astype(BF16)
        grad_preact = (dot_nt(cot, back) * (cdf + slope)).astype(BF16)
        term = dot(activated, back)
        branch = term if branch is None else branch + term
        term = dot_nt(grad_preact, into)
        grad_normed = term if grad_normed is None else grad_normed + term
        sum_reduce[cols, :] += dot_tn(activated, cot)
        sum_expand[:, cols] += dot(normed_t, grad_preact)
        grad_ebias[:, cols] += jnp.sum(grad_preact.astype(F32), axis=0, keepdims=True)
    output[...] = (middle + branch + vecs[7:8, :]).astype(BF16)
    cot32 = cot.astype(F32)
    grads = cot32 + norm_back(grad_normed, vecs[5:6, :], xhat, scale)
    attended = grads.astype(BF16)
    grad_middle[...] = attended
    grad_mixed[...] = dot_nt(attended, proj[...]).astype(BF16)
    sum_proj[...] += dot_tn(mixed_rows, attended)
    grad_vecs[0:1, :] += jnp.sum(attended.astype(F32), axis=0, keepdims=True)
    grad_vecs[1:2, :] += jnp.sum(grad_normed * xhat, axis=0, keepdims=True)
    grad_vecs[2:3, :] += jnp.sum(grad_normed, axis=0, keepdims=True)
    grad_vecs[3:4, :] += jnp.sum(cot32, axis=0, keepdims=True)

    @pl.when(step == pl.num_programs(0) - 1)
    def _():
        grad_proj[...] = sum_proj[...].astype(BF16)
        grad_expand[...] = sum_expand[...].astype(BF16)
        grad_reduce[...] = sum_reduce[...].astype(BF16)


def middle_all(tokens, mixed, cotangent, vecs, ebias, proj, expand, reduce, block=512, part=512):
    rows, width = tokens.shape
    row_block = pl.BlockSpec((block, width), lambda i: (i, 0))
    row_shape = jax.ShapeDtypeStruct((rows, width), BF16)
    return pl.pallas_call(
        functools.partial(middle_kernel, part),
        grid=(rows // block,),
        in_specs=[
            row_block,
            row_block,
            row_block,
            resident(vecs.shape),
            resident(ebias.shape),
            resident(proj.shape),
            resident(expand.shape),
            resident(reduce.shape),
        ],
        out_specs=[
            row_block,
            row_block,
            row_block,
            resident(proj.shape),
            resident(expand.shape),
            resident(reduce.shape),
            resident(ebias.shape),
            resident((8, width)),
        ],
        out_shape=[
            row_shape,
            row_shape,
            row_shape,
            jax.ShapeDtypeStruct(proj.shape, BF16),
            jax.ShapeDtypeStruct(expand.shape, BF16),
            jax.ShapeDtypeStruct(reduce.shape, BF16),
            jax.ShapeDtypeStruct(ebias.shape, F32),
            jax.ShapeDtypeStruct((8, width), F32),
        ],
        scratch_shapes=[
            pltpu.VMEM(proj.shape, F32),
            pltpu.VMEM(expand.shape, F32),
            pltpu.VMEM(reduce.shape, F32),
        ],
        compiler_params=params(63),
    )(tokens, mixed, cotangent, vecs, ebias, proj, expand, reduce)


def weight_kernel(normed, dq, dk, dv, grad_weight, grad_vecs, total):
    step = pl.program_id(0)
    width = normed.shape[1]

    @pl.when(step == 0)
    def _():
        total[...] = jnp.zeros_like(total)
        grad_vecs[...] = jnp.zeros_like(grad_vecs)

    rows_t = normed[...].T
    for index, part in enumerate((dq, dk, dv)):
        total[:, index * width : (index + 1) * width] += dot(rows_t, part[...])
    grad_vecs[0:1, :] += jnp.sum(dq[...].astype(F32), axis=0, keepdims=True)
    grad_vecs[1:2, :] += jnp.sum(dv[...].astype(F32), axis=0, keepdims=True)

    @pl.when(step == pl.num_programs(0) - 1)
    def _():
        grad_weight[...] = total[...].astype(BF16)


def qkv_weight_grad(normed, dq, dk, dv, block=512):
    rows, width = normed.shape
    row_block = pl.BlockSpec((block, width), lambda i: (i, 0))
    return pl.pallas_call(
        weight_kernel,
        grid=(rows // block,),
        in_specs=[row_block] * 4,
        out_specs=[resident((width, 3 * width)), resident((8, width))],
        out_shape=[
            jax.ShapeDtypeStruct((width, 3 * width), BF16),
            jax.ShapeDtypeStruct((8, width), F32),
        ],
        scratch_shapes=[pltpu.VMEM((width, 3 * width), F32)],
        compiler_params=params(40),
    )(normed, dq, dk, dv)


def input_kernel(tokens, grad_middle, dq, dk, dv, vecs, weight, input_grad, grad_vecs):
    step = pl.program_id(0)
    width = tokens.shape[1]

    @pl.when(step == 0)
    def _():
        grad_vecs[...] = jnp.zeros_like(grad_vecs)

    xhat, scale = normalise(tokens[...].astype(F32))
    upstream = (
        dot_nt(dq[...], weight[:, :width])
        + dot_nt(dk[...], weight[:, width : 2 * width])
        + dot_nt(dv[...], weight[:, 2 * width :])
    )
    grads = norm_back(upstream, vecs[0:1, :], xhat, scale)
    input_grad[...] = (grad_middle[...].astype(F32) + grads).astype(BF16)
    grad_vecs[0:1, :] += jnp.sum(upstream * xhat, axis=0, keepdims=True)
    grad_vecs[1:2, :] += jnp.sum(upstream, axis=0, keepdims=True)


def input_backward(tokens, grad_middle, dq, dk, dv, vecs, weight, block=512):
    rows, width = tokens.shape
    row_block = pl.BlockSpec((block, width), lambda i: (i, 0))
    return pl.pallas_call(
        input_kernel,
        grid=(rows // block,),
        in_specs=[row_block] * 5 + [resident(vecs.shape), resident(weight.shape)],
        out_specs=[row_block, resident((8, width))],
        out_shape=[
            jax.ShapeDtypeStruct((rows, width), BF16),
            jax.ShapeDtypeStruct((8, width), F32),
        ],
        compiler_params=params(40),
    )(tokens, grad_middle, dq, dk, dv, vecs, weight)


def local(
    tokens,
    segment_ids,
    valid_mask,
    cotangent,
    norm1_gain,
    norm1_bias,
    qkv_weight,
    query_bias,
    value_bias,
    proj_weight,
    proj_bias,
    norm2_gain,
    norm2_bias,
    expand_weight,
    expand_bias,
    reduce_weight,
    reduce_bias,
):
    seq_len = segment_ids.shape[1]
    own = norm1_gain.shape[0]
    per = expand_bias.shape[0] // own
    small = jnp.stack(
        [
            norm1_gain,
            norm1_bias,
            query_bias,
            value_bias,
            proj_bias,
            norm2_gain,
            norm2_bias,
            reduce_bias,
            *jnp.split(expand_bias, per),
        ]
    )
    small = lax.all_gather(small, "fsdp", axis=0)
    shards = small.shape[0]
    vecs = small[:, :8].swapaxes(0, 1).reshape(8, shards * own).astype(F32)
    ebias = small[:, 8:].reshape(1, shards * own * per).astype(F32)
    qkv_full = lax.all_gather(qkv_weight, "fsdp", axis=0, tiled=True)
    proj_full = lax.all_gather(proj_weight, "fsdp", axis=0, tiled=True)
    expand_full = lax.all_gather(expand_weight, "fsdp", axis=0, tiled=True)
    reduce_full = lax.all_gather(reduce_weight, "fsdp", axis=0, tiled=True)

    table = clip_table(segment_ids, valid_mask)
    qkv, normed1 = qkv_forward(tokens, vecs, qkv_full)
    mixed, inverse, exps = attend_forward(table, qkv, seq_len)
    (
        output,
        grad_middle,
        grad_mixed,
        grad_proj,
        grad_expand,
        grad_reduce,
        grad_ebias,
        middle_vecs,
    ) = middle_all(tokens, mixed, cotangent, vecs, ebias, proj_full, expand_full, reduce_full)

    def shard(grad):
        part = lax.psum_scatter(grad, "fsdp", scatter_dimension=0, tiled=True)
        return lax.psum(part, "rep").astype(F32)

    sum_reduce = shard(grad_reduce)
    sum_expand = shard(grad_expand)
    sum_proj = shard(grad_proj)
    dq, dk, dv = attend_backward(table, qkv, grad_mixed, mixed, inverse, exps, seq_len)
    grad_qkv, qkv_vecs = qkv_weight_grad(normed1, dq, dk, dv)
    sum_qkv = shard(grad_qkv)
    input_grad, input_vecs = input_backward(tokens, grad_middle, dq, dk, dv, vecs, qkv_full)

    vec_rows = jnp.concatenate([input_vecs[:2], qkv_vecs[:2], middle_vecs[:4]], axis=0)
    vec_rows = vec_rows.reshape(8, shards, own).swapaxes(0, 1)
    bias_rows = grad_ebias.reshape(shards, per, own)
    small_grads = jnp.concatenate([vec_rows, bias_rows], axis=1)
    small_grads = lax.psum(small_grads, "rep")
    small_grads = lax.psum_scatter(small_grads, "fsdp", scatter_dimension=0)
    return (
        output,
        input_grad,
        small_grads[0],
        small_grads[1],
        sum_qkv,
        small_grads[2],
        small_grads[3],
        sum_proj,
        small_grads[4],
        small_grads[5],
        small_grads[6],
        sum_expand,
        small_grads[8:].reshape(-1),
        sum_reduce,
        small_grads[7],
    )


def solution(mesh):
    rows = P(("rep", "fsdp"), None)
    vector = P("fsdp")
    matrix = P("fsdp", None)
    params_specs = (
        vector,
        vector,
        matrix,
        vector,
        vector,
        matrix,
        vector,
        vector,
        vector,
        matrix,
        vector,
        matrix,
        vector,
    )
    return jax.shard_map(
        local,
        mesh=mesh,
        in_specs=(rows, rows, rows, rows) + params_specs,
        out_specs=(rows, rows) + params_specs,
        check_vma=False,
    )
```

```python
import functools
import math

import jax
import jax.numpy as jnp
from jax import lax
from jax.experimental import pallas as pl
from jax.experimental.pallas import tpu as pltpu
from jax.sharding import PartitionSpec as P

HEADS = 12
CLIPS = 6
EPSILON = 1e-06
WINDOW = 256
FIELDS = 5
BF16 = jnp.bfloat16
F32 = jnp.float32
MEBI = 1024 * 1024
NEGATIVE = -1e30


def dot(left, right):
    return lax.dot_general(left, right, (((1,), (0,)), ((), ())), preferred_element_type=F32)


def dot_nt(left, right):
    return lax.dot_general(left, right, (((1,), (1,)), ((), ())), preferred_element_type=F32)


def dot_tn(left, right):
    return lax.dot_general(left, right, (((0,), (0,)), ((), ())), preferred_element_type=F32)


def resident(shape):
    zeros = (0,) * len(shape)
    return pl.BlockSpec(shape, lambda *_: zeros, pipeline_mode=pl.Buffered(1))


def params(limit, count=1):
    return pltpu.CompilerParams(
        vmem_limit_bytes=limit * MEBI, dimension_semantics=("arbitrary",) * count
    )


def normalise(values):
    row_mean = jnp.mean(values, axis=-1, keepdims=True)
    centred = values - row_mean
    row_var = jnp.mean(centred * centred, axis=-1, keepdims=True)
    scale = lax.rsqrt(row_var + EPSILON)
    return centred * scale, scale


def norm_back(upstream, gain, xhat, scale):
    weighted = upstream * gain
    first = jnp.mean(weighted, axis=-1, keepdims=True)
    second = jnp.mean(weighted * xhat, axis=-1, keepdims=True)
    return scale * (weighted - first - xhat * second)


def core_swap(value):
    count = lax.axis_size("fsdp")
    return lax.ppermute(value, "fsdp", [(i, i ^ 1) for i in range(count)])


def chip_shift(value, hops):
    count = lax.axis_size("fsdp")
    return lax.ppermute(value, "fsdp", [(i, (i + 2 * hops) % count) for i in range(count)])


def replica_swap(value, bits):
    return lax.ppermute(value, "rep", [(i, i ^ bits) for i in range(4)])


def place_table():
    shard = lax.axis_index("fsdp")
    replica = lax.axis_index("rep")
    return jnp.stack([shard // 2, shard % 2, replica // 2, replica % 2]).astype(jnp.int32)


def gather_pieces(piece, split):
    chips = lax.axis_size("fsdp") // 2
    along = jnp.concatenate([chip_shift(piece, hop) for hop in range(1, chips)], axis=0)
    from_x = replica_swap(along, 1)
    from_y = replica_swap(along, 2)
    low = replica_swap(from_x[:, :split], 2)
    high = replica_swap(from_y[:, split:], 1)
    here = (along, from_x, from_y, low, high)
    return here, tuple(core_swap(part) for part in here)


def fetch_copies(place, targets, owns, pieces, split, chips, sems):
    chip, core, row_bit, col_bit = (place[i] for i in range(4))
    count = 0
    made = []

    def add(source, target):
        nonlocal count
        made.append(pltpu.make_async_copy(source, target, sems.at[count]))
        count += 1

    for other in range(2):
        side = core ^ other
        along, from_x, from_y, low, high = pieces[other]
        height = along.shape[0] // (chips - 1)
        step = math.gcd(height, 16)
        for number, (target, stacked, column) in enumerate(targets):
            rows = target.shape[0] // (2 * chips)
            start = pl.multiple_of((2 * chip + side) * rows, step)
            add(owns[other][number], target.at[pl.ds(start, rows), :])
            for hop in range(1, chips):
                shard = 2 * lax.rem(chip - hop + chips, chips) + side
                source_rows = pl.ds((hop - 1) * height, height)
                for flip in range(4):
                    across = row_bit ^ (flip // 2)
                    aside = col_bit ^ (flip % 2)
                    if stacked:
                        width = target.shape[1]
                        spans = []
                        for half in range(rows // (4 * height)):
                            at = shard * rows + (across * 2 + aside) * (rows // 4) + half * height
                            spans.append((column + half * width, width, at, 0))
                    else:
                        width = target.shape[1] // 2
                        spans = [(column, width, shard * rows + across * height, aside * width)]
                    for first, size, row, col in spans:
                        row = pl.multiple_of(row, step)
                        cuts = [(first, size, 0)]
                        if flip == 3 and first < split < first + size:
                            cuts = [
                                (first, split - first, 0),
                                (split, first + size - split, split - first),
                            ]
                        for begin, length, extra in cuts:
                            origin = (along, from_x, from_y, low)[flip]
                            if flip == 3 and begin >= split:
                                origin = high
                                begin = begin - split
                            to = col if isinstance(col, int) else pl.multiple_of(col + extra, 128)
                            add(
                                origin.at[source_rows, pl.ds(begin, length)],
                                target.at[pl.ds(row, height), pl.ds(to, length)],
                            )
    return made


def spread_copies(place, targets, small, blank, mine, theirs, chips, sems):
    core = place[1]
    count = 0
    made = []
    height = mine.shape[0] // (4 * chips)
    step = math.gcd(height, 16)
    for other, packed in ((1, theirs), (0, mine)):
        side = core ^ other
        for chip in range(chips):
            shard = 2 * chip + side
            for quarter in range(4):
                out_rows = pl.ds((chip * 4 + quarter) * height, height)
                moves = []
                column = 0
                for target, stacked in targets:
                    rows = target.shape[0] // (2 * chips)
                    if stacked:
                        width = target.shape[1]
                        for half in range(rows // (4 * height)):
                            row = shard * rows + quarter * (rows // 4) + half * height
                            row = pl.multiple_of(row, step)
                            moves.append((target.at[pl.ds(row, height), :], column, width))
                            column += width
                    else:
                        width = target.shape[1] // 2
                        row = pl.multiple_of(shard * rows + (quarter // 2) * height, step)
                        cols = pl.ds((quarter % 2) * width, width)
                        moves.append((target.at[pl.ds(row, height), cols], column, width))
                        column += width
                if quarter == 0:
                    moves.append((small.at[shard], column, 128))
                else:
                    moves.append((blank.at[...], column, 128))
                for source, column, width in moves:
                    made.append(
                        pltpu.make_async_copy(
                            source, packed.at[out_rows, pl.ds(column, width)], sems.at[count]
                        )
                    )
                    count += 1
    return made


def run_copies(made):
    for copy in made:
        copy.start()
    for copy in made:
        copy.wait()


def add16(left, right):
    return left.astype(F32) + right.astype(F32)


def first_sum(height, place, mine, other, keep_a, send_a, keep_b, send_b):
    row_bit, col_bit = place[2], place[3]
    cut = keep_a.shape[1]
    step = math.gcd(height, 16)

    def piece(quarter, cols):
        rows = pl.ds(pl.multiple_of(quarter * height, step), height)
        return add16(mine[rows, cols], other[rows, cols]).astype(BF16)

    for bit in range(2):
        out = pl.ds(bit * height, height)
        keep_a[out, :] = piece(bit * 2 + col_bit, pl.ds(0, cut))
        send_a[out, :] = piece(bit * 2 + 1 - col_bit, pl.ds(0, cut))
        keep_b[out, :] = piece(row_bit * 2 + bit, pl.ds(cut, mine.shape[1] - cut))
        send_b[out, :] = piece((1 - row_bit) * 2 + bit, pl.ds(cut, mine.shape[1] - cut))


def second_sum(height, place, keep_a, got_a, keep_b, got_b, next_a, send_a, next_b, send_b):
    step = math.gcd(height, 16)
    for bit, keep, got, stay, send in (
        (place[2], keep_a, got_a, next_a, send_a),
        (place[3], keep_b, got_b, next_b, send_b),
    ):
        for which, out in ((bit, stay), (1 - bit, send)):
            rows = pl.ds(pl.multiple_of(which * height, step), height)
            out[...] = add16(keep[rows, :], got[rows, :]).astype(BF16)


def third_sum(height, place, keep_a, got_a, keep_b, got_b, own, *sends):
    chips = len(sends) + 1
    cut = keep_a.shape[1]
    step = math.gcd(height, 16)
    for hop, out in enumerate((own, *sends)):
        at = lax.rem(place[0] + hop, chips)
        rows = pl.ds(pl.multiple_of(at * height, step), height)
        out[:, :cut] = add16(keep_a[rows, :], got_a[rows, :]).astype(out.dtype)
        out[:, cut:] = add16(keep_b[rows, :], got_b[rows, :]).astype(out.dtype)


def fourth_sum(own, *refs):
    total = own[...]
    for ref in refs[:-1]:
        total = total + ref[...].astype(F32)
    refs[-1][...] = total.astype(BF16)


def last_spread(stacks, place, own, from_x, from_y, from_xy, *outs):
    replica = place[2] * 2 + place[3]
    height, packed = own.shape
    step = math.gcd(height, 16)
    for flip, source in enumerate((own, from_x, from_y, from_xy)):
        across = place[2] ^ (flip // 2)
        aside = place[3] ^ (flip % 2)
        column = 0
        for stacked, out in zip(stacks, outs):
            rows, width = out.shape
            if stacked:
                for half in range(rows // (4 * height)):
                    at = (across * 2 + aside) * (rows // 4) + half * height
                    out[pl.ds(pl.multiple_of(at, step), height), :] = source[
                        :, column : column + width
                    ].astype(F32)
                    column += width
            else:
                width = width // 2
                at = pl.ds(pl.multiple_of(across * height, step), height)
                cols = pl.ds(pl.multiple_of(aside * width, 128), width)
                out[at, cols] = source[:, column : column + width].astype(F32)
                column += width

        @pl.when((replica ^ flip) == 0)
        def _():
            outs[-1][...] = source[0:16, packed - 128 :].astype(F32)


def small_call(body, place, inputs, shapes, grid=None, in_specs=None, out_specs=None):
    if grid is None:
        grid = (1,)
        in_specs = [pl.BlockSpec(value.shape, lambda i, t: (0, 0)) for value in inputs]
        out_specs = [pl.BlockSpec(shape.shape, lambda i, t: (0, 0)) for shape in shapes]
    return pl.pallas_call(
        body,
        grid_spec=pltpu.PrefetchScalarGridSpec(
            num_scalar_prefetch=1, grid=grid, in_specs=in_specs, out_specs=out_specs
        ),
        out_shape=shapes,
        compiler_params=params(40),
    )(place, *inputs)


def sum_pieces(place, mine, theirs, cut, stacks, out_shapes):
    chips = lax.axis_size("fsdp") // 2
    height = mine.shape[0] // (4 * chips)
    packed = mine.shape[1]
    other = core_swap(theirs)

    def shape(rows, cols, dtype=BF16):
        return jax.ShapeDtypeStruct((rows, cols), dtype)

    def rows_of(count, cols):
        return pl.BlockSpec((count * height, cols), lambda i, t: (i, 0))

    keep_a, send_a, keep_b, send_b = small_call(
        functools.partial(first_sum, height),
        place,
        (mine, other),
        [shape(2 * chips * height, cut)] * 2 + [shape(2 * chips * height, packed - cut)] * 2,
        (chips,),
        [rows_of(4, packed)] * 2,
        [rows_of(2, cut)] * 2 + [rows_of(2, packed - cut)] * 2,
    )
    got_a = replica_swap(send_a, 1)
    got_b = replica_swap(send_b, 2)
    keep_a, send_a, keep_b, send_b = small_call(
        functools.partial(second_sum, height),
        place,
        (keep_a, got_a, keep_b, got_b),
        [shape(chips * height, cut)] * 2 + [shape(chips * height, packed - cut)] * 2,
        (chips,),
        [rows_of(2, cut)] * 2 + [rows_of(2, packed - cut)] * 2,
        [rows_of(1, cut)] * 2 + [rows_of(1, packed - cut)] * 2,
    )
    got_a = replica_swap(send_a, 2)
    got_b = replica_swap(send_b, 1)
    own, *sends = small_call(
        functools.partial(third_sum, height),
        place,
        (keep_a, got_a, keep_b, got_b),
        [shape(height, packed, F32)] + [shape(height, packed)] * (chips - 1),
    )
    got = [chip_shift(send, hop + 1) for hop, send in enumerate(sends)]
    (total,) = small_call(
        lambda table, *refs: fourth_sum(*refs), place, (own, *got), [shape(height, packed)]
    )
    quarters = (total, replica_swap(total, 1), replica_swap(total, 2), replica_swap(total, 3))
    return small_call(
        functools.partial(last_spread, stacks),
        place,
        quarters,
        [jax.ShapeDtypeStruct(s, F32) for s in out_shapes] + [shape(16, 128, F32)],
    )


def small_blocks(rows_of_shard, small, shards, own):
    small[...] = jnp.zeros_like(small)
    for shard in range(shards):
        rows = rows_of_shard(shard)
        small[shard, 0 : rows.shape[0], 0:own] = rows.astype(BF16)


def qkv_kernel(chips, split, place, tokens, vecs, *refs):
    owns = (refs[0:1], refs[1:2])
    pieces = (refs[2:7], refs[7:12])
    qkv, unit, weight, sems = refs[12:]
    width = tokens.shape[1]

    @pl.when(pl.program_id(0) == 0)
    def _():
        run_copies(fetch_copies(place, [(weight, False, 0)], owns, pieces, split, chips, sems))

    xhat, _ = normalise(tokens[...].astype(F32))
    unit[...] = xhat.astype(BF16)
    rows = (xhat * vecs[0:1, :] + vecs[1:2, :]).astype(BF16)
    query = dot(rows, weight[:, :width]) + vecs[2:3, :]
    qkv[:, :width] = query.astype(BF16) * jnp.asarray(0.125, BF16)
    qkv[:, width : 2 * width] = dot(rows, weight[:, width : 2 * width]).astype(BF16)
    value = dot(rows, weight[:, 2 * width :]) + vecs[3:4, :]
    qkv[:, 2 * width :] = value.astype(BF16)


def hbm():
    return pl.BlockSpec(memory_space=pl.ANY)


def qkv_forward(place, tokens, vecs, own, pieces, split, block=512):
    rows, width = tokens.shape
    chips = lax.axis_size("fsdp") // 2
    sources = [own, core_swap(own), *pieces[0], *pieces[1]]
    zero = lambda i, t: (0, 0)
    return pl.pallas_call(
        functools.partial(qkv_kernel, chips, split),
        grid_spec=pltpu.PrefetchScalarGridSpec(
            num_scalar_prefetch=1,
            grid=(rows // block,),
            in_specs=[
                pl.BlockSpec((block, width), lambda i, t: (i, 0)),
                pl.BlockSpec(vecs.shape, zero),
            ]
            + [hbm()] * len(sources),
            out_specs=[
                pl.BlockSpec((block, 3 * width), lambda i, t: (i, 0)),
                pl.BlockSpec((block, width), lambda i, t: (i, 0)),
                resident((width, 3 * width)),
            ],
            scratch_shapes=[pltpu.SemaphoreType.DMA((2 + 10 * (chips - 1),))],
        ),
        out_shape=[
            jax.ShapeDtypeStruct((rows, 3 * width), BF16),
            jax.ShapeDtypeStruct((rows, width), BF16),
            jax.ShapeDtypeStruct((width, 3 * width), BF16),
        ],
        compiler_params=params(40),
        cost_estimate=pl.CostEstimate(
            flops=6 * rows * width * width, bytes_accessed=20_000_000, transcendentals=0
        ),
    )(place, tokens, vecs, *sources)


def clip_table(segment_ids, valid_mask):
    seq_len = segment_ids.shape[1]
    clips = jnp.arange(CLIPS, dtype=jnp.int32)[None, :, None]
    segments = segment_ids[:, None, :]
    start = jnp.sum((segments < clips).astype(jnp.int32), axis=2)
    end = jnp.sum((segments <= clips).astype(jnp.int32), axis=2)
    valid = jnp.sum(((segments == clips) & (valid_mask[:, None, :] == 1)).astype(jnp.int32), axis=2)
    aligned = start // 16 * 16
    need = end - aligned
    path = (need > WINDOW).astype(jnp.int32) + (need > 2 * WINDOW).astype(jnp.int32)
    window = jnp.where(path == 0, WINDOW, jnp.where(path == 1, 2 * WINDOW, seq_len))
    base = jnp.minimum(aligned, seq_len - window)
    return jnp.stack([base, path, start - base, end - base, start + valid - base], axis=2).reshape(
        -1
    )


def lane_low(rows):
    return lax.broadcasted_iota(jnp.int32, (rows, 128), 1) < 64


def flag_lane(rows):
    return lax.broadcasted_iota(jnp.int32, (rows, 128), 1) % 64 == 0


def row_mask(rows, offset, first, last):
    index = lax.broadcasted_iota(jnp.int32, (rows, 128), 0) + offset
    return (index >= first) & (index < last)


def key_extra(rows, first, last):
    bias = jnp.where(row_mask(rows, 0, first, last), 0.0, NEGATIVE)
    return jnp.where(flag_lane(rows), bias, 0.0).astype(BF16)


def query_extra(rows):
    return jnp.where(flag_lane(rows), 1.0, 0.0).astype(BF16)


def weights_of(query, keys, extra_query, extra_keys, low, low_keys, head):
    if head == 0:
        left = jnp.where(low, query, extra_query)
        right = jnp.where(low_keys, keys, extra_keys)
    else:
        left = jnp.where(low, extra_query, query)
        right = jnp.where(low_keys, extra_keys, keys)
    scores = dot_nt(left, right)
    return jnp.exp(scores - jnp.max(scores, axis=1, keepdims=True)).astype(BF16)


def attend_window(refs, base, first, last, valid_end, window, pairs, exps, clip):
    queries, keys_ref, values_ref, mixed, inverse = refs
    chunk = WINDOW
    low = lane_low(chunk)
    low_keys = lane_low(window)
    extra_keys = key_extra(window, first, valid_end)
    extra_query = query_extra(chunk)
    ones = jnp.ones((window, 128), BF16)
    key_rows = pl.ds(base, window)

    def one_chunk(offset, row_start):
        rows = pl.ds(row_start, chunk)
        keep = row_mask(chunk, offset, first, last)
        for pair in range(pairs):
            lanes = pl.ds(128 * pair, 128)
            query = queries[rows, lanes]
            keys = keys_ref[key_rows, lanes]
            stack = jnp.concatenate([values_ref[key_rows, lanes], ones], axis=1)
            sums = []
            for head in range(2):
                weights = weights_of(query, keys, extra_query, extra_keys, low, low_keys, head)
                if exps is not None:
                    exps[0, 2 * pair + head, pl.ds(clip * WINDOW, WINDOW), :] = weights
                sums.append(dot(weights, stack))
            total = jnp.where(low, sums[0][:, 128:], sums[1][:, 128:])
            weighted = jnp.where(low, sums[0][:, :128], sums[1][:, :128])
            reciprocal = 1.0 / total
            mixed[rows, lanes] = jnp.where(
                keep, (weighted * reciprocal), mixed[rows, lanes].astype(F32)
            ).astype(BF16)
            inverse[rows, lanes] = jnp.where(keep, reciprocal, inverse[rows, lanes])

    if window == chunk:
        one_chunk(0, base)
    else:

        def step(index, carry):
            offset = index * chunk
            one_chunk(offset, pl.multiple_of(base + offset, 16))
            return carry

        lax.fori_loop(0, window // chunk, step, 0)


def clip_fields(table, sequence, clip):
    at = (sequence * CLIPS + clip) * FIELDS
    base = pl.multiple_of(table[at], 16)
    return base, table[at + 1], table[at + 2], table[at + 3], table[at + 4]


def attend_kernel(pairs, table, queries, keys, values, mixed, inverse, exps):
    sequence = pl.program_id(0)
    seq_len = queries.shape[0]
    mixed[...] = jnp.zeros_like(mixed)
    inverse[...] = jnp.zeros_like(inverse)
    refs = (queries, keys, values, mixed, inverse)

    def one_clip(clip, carry):
        base, path, first, last, valid_end = clip_fields(table, sequence, clip)
        for number, window in enumerate((WINDOW, 2 * WINDOW, seq_len)):

            @pl.when(path == number)
            def _():
                attend_window(
                    refs,
                    base,
                    first,
                    last,
                    valid_end,
                    window,
                    pairs,
                    exps if number == 0 else None,
                    clip,
                )

        return carry

    lax.fori_loop(0, CLIPS, one_clip, 0)


def attend_forward(table, qkv, seq_len, pairs=2):
    rows = qkv.shape[0]
    width = qkv.shape[1] // 3
    seqs = rows // seq_len
    lanes = 128 * pairs
    groups = width // lanes
    block = (seq_len, lanes)
    return pl.pallas_call(
        functools.partial(attend_kernel, pairs),
        grid_spec=pltpu.PrefetchScalarGridSpec(
            num_scalar_prefetch=1,
            grid=(seqs, groups),
            in_specs=[
                pl.BlockSpec(block, lambda s, g, t: (s, g)),
                pl.BlockSpec(block, lambda s, g, t: (s, groups + g)),
                pl.BlockSpec(block, lambda s, g, t: (s, 2 * groups + g)),
            ],
            out_specs=[
                pl.BlockSpec(block, lambda s, g, t: (s, g)),
                pl.BlockSpec(block, lambda s, g, t: (s, g)),
                pl.BlockSpec((1, 2 * pairs, CLIPS * WINDOW, WINDOW), lambda s, g, t: (s, g, 0, 0)),
            ],
        ),
        out_shape=[
            jax.ShapeDtypeStruct((rows, width), BF16),
            jax.ShapeDtypeStruct((rows, width), F32),
            jax.ShapeDtypeStruct((seqs, HEADS, CLIPS * WINDOW, WINDOW), BF16),
        ],
        compiler_params=params(48, 2),
    )(table, qkv, qkv, qkv)


def back_window(refs, base, first, last, valid_end, window, pairs, exps, clip, gather):
    queries, keys_ref, values_ref, grads, mixed, inverse, dq, dk, dv = refs
    key_grad, value_grad = gather
    chunk = WINDOW
    single = window == chunk
    low = lane_low(chunk)
    low_keys = lane_low(window)
    extra_keys = None if single else key_extra(window, first, valid_end)
    extra_query = None if single else query_extra(chunk)
    key_rows = pl.ds(base, window)
    one = jnp.ones((window, 128), BF16)

    def one_chunk(offset, row_start):
        rows = pl.ds(row_start, chunk)
        keep = row_mask(chunk, offset, first, last)
        for pair in range(pairs):
            lanes = pl.ds(128 * pair, 128)
            query = queries[rows, lanes]
            keys = keys_ref[key_rows, lanes]
            values = values_ref[key_rows, lanes]
            scaled = jnp.where(keep, grads[rows, lanes].astype(F32) * inverse[rows, lanes], 0.0)
            product = scaled * mixed[rows, lanes].astype(F32)
            turned = pltpu.roll(-product, 64, 1).astype(BF16)
            scaled = scaled.astype(BF16)
            parts = []
            for head in range(2):
                if head == 0:
                    left = jnp.where(low, scaled, turned)
                    right = jnp.where(low_keys, values, one)
                else:
                    left = jnp.where(low, turned, scaled)
                    right = jnp.where(low_keys, one, values)
                if single:
                    weights = exps[0, 2 * pair + head, pl.ds(clip * WINDOW, WINDOW), :]
                else:
                    weights = weights_of(query, keys, extra_query, extra_keys, low, low_keys, head)
                grad_scores = (weights.astype(F32) * dot_nt(left, right)).astype(BF16)
                parts.append(
                    (
                        dot(grad_scores, keys),
                        dot_tn(grad_scores, query),
                        dot_tn(weights, scaled),
                    )
                )
            query_part = jnp.where(low, parts[0][0], parts[1][0]) * 0.125
            key_part = jnp.where(low_keys, parts[0][1], parts[1][1])
            value_part = jnp.where(low_keys, parts[0][2], parts[1][2])
            dq[rows, lanes] = jnp.where(keep, query_part, dq[rows, lanes].astype(F32)).astype(BF16)
            if single:
                dk[rows, lanes] = jnp.where(keep, key_part, dk[rows, lanes].astype(F32)).astype(
                    BF16
                )
                dv[rows, lanes] = jnp.where(keep, value_part, dv[rows, lanes].astype(F32)).astype(
                    BF16
                )
            else:
                key_grad[pl.ds(0, window), lanes] += key_part
                value_grad[pl.ds(0, window), lanes] += value_part

    if single:
        one_chunk(0, base)
        return
    key_grad[...] = jnp.zeros_like(key_grad)
    value_grad[...] = jnp.zeros_like(value_grad)

    def step(index, carry):
        offset = index * chunk
        one_chunk(offset, pl.multiple_of(base + offset, 16))
        return carry

    lax.fori_loop(0, window // chunk, step, 0)
    keep = row_mask(window, 0, first, last)
    for pair in range(pairs):
        lanes = pl.ds(128 * pair, 128)
        for ref, total in ((dk, key_grad), (dv, value_grad)):
            ref[key_rows, lanes] = jnp.where(
                keep, total[pl.ds(0, window), lanes], ref[key_rows, lanes].astype(F32)
            ).astype(BF16)


def back_kernel(
    pairs,
    table,
    queries,
    keys,
    values,
    grads,
    mixed,
    inverse,
    exps,
    dq,
    dk,
    dv,
    key_grad,
    value_grad,
):
    sequence = pl.program_id(0)
    seq_len = queries.shape[0]
    for ref in (dq, dk, dv):
        ref[...] = jnp.zeros_like(ref)
    refs = (queries, keys, values, grads, mixed, inverse, dq, dk, dv)

    def one_clip(clip, carry):
        base, path, first, last, valid_end = clip_fields(table, sequence, clip)
        for number, window in enumerate((WINDOW, 2 * WINDOW, seq_len)):

            @pl.when(path == number)
            def _():
                back_window(
                    refs,
                    base,
                    first,
                    last,
                    valid_end,
                    window,
                    pairs,
                    exps,
                    clip,
                    (key_grad, value_grad),
                )

        return carry

    lax.fori_loop(0, CLIPS, one_clip, 0)


def attend_backward(table, qkv, grads, mixed, inverse, exps, seq_len, pairs=2):
    rows, width = mixed.shape
    seqs = rows // seq_len
    lanes = 128 * pairs
    groups = width // lanes
    block = (seq_len, lanes)
    own = pl.BlockSpec(block, lambda s, g, t: (s, g))
    shape = jax.ShapeDtypeStruct((rows, width), BF16)
    return pl.pallas_call(
        functools.partial(back_kernel, pairs),
        grid_spec=pltpu.PrefetchScalarGridSpec(
            num_scalar_prefetch=1,
            grid=(seqs, groups),
            in_specs=[
                own,
                pl.BlockSpec(block, lambda s, g, t: (s, groups + g)),
                pl.BlockSpec(block, lambda s, g, t: (s, 2 * groups + g)),
                own,
                own,
                own,
                pl.BlockSpec((1, 2 * pairs, CLIPS * WINDOW, WINDOW), lambda s, g, t: (s, g, 0, 0)),
            ],
            out_specs=[own, own, own],
            scratch_shapes=[pltpu.VMEM(block, F32), pltpu.VMEM(block, F32)],
        ),
        out_shape=[shape, shape, shape],
        compiler_params=params(48, 2),
    )(table, qkv, qkv, qkv, grads, mixed, inverse, exps)


def gauss(value):
    size = jnp.abs(value)
    rate = 1.0 / (1.0 + 0.3275911 * 0.7071067811865476 * size)
    tail = jnp.exp(value * value * -0.5)
    series = rate * (
        0.5 * 0.254829592
        + rate
        * (
            0.5 * -0.284496736
            + rate * (0.5 * 1.421413741 + rate * (0.5 * -1.453152027 + rate * (0.5 * 1.061405429)))
        )
    )
    upper = series * tail
    return jnp.where(value >= 0, 1.0 - upper, upper), value * tail * 0.3989422804014327


def middle_kernel(
    part,
    chips,
    split,
    place,
    tokens,
    mixed,
    cotangent,
    vecs,
    ebias,
    *refs,
):
    owns = (refs[0:3], refs[3:6])
    pieces = (refs[6:11], refs[11:16])
    (
        output,
        grad_middle,
        grad_mixed,
        mine,
        theirs,
        proj,
        expand,
        reduce,
        sum_proj,
        sum_expand,
        sum_reduce,
        sum_ebias,
        sum_vecs,
        small,
        blank,
        in_sems,
        out_sems,
    ) = refs[16:]
    step = pl.program_id(0)
    width, hidden = expand.shape
    own = width // (2 * chips)

    @pl.when(step == 0)
    def _():
        targets = [
            (proj, False, 0),
            (expand, False, width // 2),
            (reduce, True, width // 2 + hidden // 2),
        ]
        made = fetch_copies(place, targets, owns, pieces, split, chips, in_sems)
        for copy in made:
            copy.start()
        sum_proj[...] = jnp.zeros_like(sum_proj)
        sum_expand[...] = jnp.zeros_like(sum_expand)
        sum_reduce[...] = jnp.zeros_like(sum_reduce)
        sum_ebias[...] = jnp.zeros_like(sum_ebias)
        sum_vecs[...] = jnp.zeros_like(sum_vecs)
        for copy in made:
            copy.wait()

    mixed_rows = mixed[...]
    cot = cotangent[...]
    middle = tokens[...].astype(F32) + dot(mixed_rows, proj[...]) + vecs[4:5, :]
    xhat, scale = normalise(middle)
    normed = (xhat * vecs[5:6, :] + vecs[6:7, :]).astype(BF16)
    normed_t = normed.T
    branch = None
    grad_normed = None
    for start in range(0, hidden, part):
        cols = pl.ds(start, part)
        into = expand[:, cols]
        back = reduce[cols, :]
        preact = dot(normed, into) + ebias[:, cols]
        cdf, slope = gauss(preact)
        activated = (preact * cdf).astype(BF16)
        grad_preact = (dot_nt(cot, back) * (cdf + slope)).astype(BF16)
        term = dot(activated, back)
        branch = term if branch is None else branch + term
        term = dot_nt(grad_preact, into)
        grad_normed = term if grad_normed is None else grad_normed + term
        sum_reduce[cols, :] += dot_tn(activated, cot)
        sum_expand[:, cols] += dot(normed_t, grad_preact)
        sum_ebias[:, cols] += jnp.sum(grad_preact.astype(F32), axis=0, keepdims=True)
    output[...] = (middle + branch + vecs[7:8, :]).astype(BF16)
    cot32 = cot.astype(F32)
    grads = cot32 + norm_back(grad_normed, vecs[5:6, :], xhat, scale)
    attended = grads.astype(BF16)
    grad_middle[...] = attended
    grad_mixed[...] = dot_nt(attended, proj[...]).astype(BF16)
    sum_proj[...] += dot_tn(mixed_rows, attended)
    sum_vecs[0:1, :] += jnp.sum(attended.astype(F32), axis=0, keepdims=True)
    sum_vecs[1:2, :] += jnp.sum(grad_normed * xhat, axis=0, keepdims=True)
    sum_vecs[2:3, :] += jnp.sum(grad_normed, axis=0, keepdims=True)
    sum_vecs[3:4, :] += jnp.sum(cot32, axis=0, keepdims=True)

    @pl.when(step == pl.num_programs(0) - 1)
    def _():
        proj[...] = sum_proj[...].astype(BF16)
        expand[...] = sum_expand[...].astype(BF16)
        reduce[...] = sum_reduce[...].astype(BF16)
        blank[...] = jnp.zeros_like(blank)
        per = hidden // width

        def rows_of_shard(shard):
            rows = [sum_vecs[0:4, shard * own : (shard + 1) * own]]
            for index in range(per):
                at = (shard * per + index) * own
                rows.append(sum_ebias[0:1, at : at + own])
            return jnp.concatenate(rows, axis=0)

        small_blocks(rows_of_shard, small, 2 * chips, own)
        run_copies(
            spread_copies(
                place,
                [(proj, False), (expand, False), (reduce, True)],
                small,
                blank,
                mine,
                theirs,
                chips,
                out_sems,
            )
        )


def middle_all(
    place, tokens, mixed, cotangent, vecs, ebias, owns, pieces, split, block=512, part=512
):
    rows, width = tokens.shape
    chips = lax.axis_size("fsdp") // 2
    hidden = ebias.shape[1]
    height = width // (4 * chips)
    row_block = pl.BlockSpec((block, width), lambda i, t: (i, 0))
    row_shape = jax.ShapeDtypeStruct((rows, width), BF16)
    packed = (4 * chips * height, width // 2 + hidden // 2 + hidden // 2 + 128)
    packed_shape = jax.ShapeDtypeStruct(packed, BF16)
    sources = [*owns, *(core_swap(own) for own in owns), *pieces[0], *pieces[1]]
    halves = hidden // width // 2
    return pl.pallas_call(
        functools.partial(middle_kernel, part, chips, split),
        grid_spec=pltpu.PrefetchScalarGridSpec(
            num_scalar_prefetch=1,
            grid=(rows // block,),
            in_specs=[row_block] * 3
            + [
                pl.BlockSpec(vecs.shape, lambda i, t: (0, 0)),
                pl.BlockSpec(ebias.shape, lambda i, t: (0, 0)),
            ]
            + [hbm()] * len(sources),
            out_specs=[row_block] * 3 + [hbm(), hbm()],
            scratch_shapes=[
                pltpu.VMEM((width, width), BF16),
                pltpu.VMEM((width, hidden), BF16),
                pltpu.VMEM((hidden, width), BF16),
                pltpu.VMEM((width, width), F32),
                pltpu.VMEM((width, hidden), F32),
                pltpu.VMEM((hidden, width), F32),
                pltpu.VMEM((1, hidden), F32),
                pltpu.VMEM((8, width), F32),
                pltpu.VMEM((2 * chips, height, 128), BF16),
                pltpu.VMEM((height, 128), BF16),
                pltpu.SemaphoreType.DMA((2 * (3 + 4 * (chips - 1) * (2 + halves)),)),
                pltpu.SemaphoreType.DMA((8 * chips * (3 + halves),)),
            ],
        ),
        out_shape=[row_shape, row_shape, row_shape, packed_shape, packed_shape],
        compiler_params=params(63),
        cost_estimate=pl.CostEstimate(
            flops=6 * rows * width * (width + 2 * hidden),
            bytes_accessed=40_000_000,
            transcendentals=rows * hidden * 2,
        ),
    )(place, tokens, mixed, cotangent, vecs, ebias, *sources)


def weight_kernel(
    chips, place, unit, dq, dk, dv, vecs, weight, mine, theirs, total, sums, low, small, blank, sems
):
    step = pl.program_id(0)
    width = unit.shape[1]
    own = width // (2 * chips)

    @pl.when(step == 0)
    def _():
        total[...] = jnp.zeros_like(total)
        sums[...] = jnp.zeros_like(sums)

    rows_t = unit[...].T
    for index, part in enumerate((dq, dk, dv)):
        cols = slice(index * width, (index + 1) * width)
        total[:, cols] += dot(rows_t, part[...])
        sums[0:1, cols] += jnp.sum(part[...].astype(F32), axis=0, keepdims=True)

    @pl.when(step == pl.num_programs(0) - 1)
    def _():
        columns = vecs[...].T
        gain, shift = columns[:, 0:1], columns[:, 1:2]
        gain_part = jnp.zeros((width, 1), F32)
        shift_part = jnp.zeros((width, 1), F32)
        for index in range(3):
            cols = slice(index * width, (index + 1) * width)
            raw = total[:, cols]
            sides = weight[:, cols].astype(F32)
            line = sums[0:1, cols]
            gain_part += jnp.sum(raw * sides, axis=1, keepdims=True)
            shift_part += jnp.sum(line * sides, axis=1, keepdims=True)
            low[:, cols] = (gain * raw + shift * line).astype(BF16)
        pick = lax.broadcasted_iota(jnp.int32, (width, 128), 1)
        both = jnp.where(pick == 0, gain_part, jnp.where(pick == 1, shift_part, 0.0)).T
        blank[...] = jnp.zeros_like(blank)

        def rows_of_shard(shard):
            cols = slice(shard * own, (shard + 1) * own)
            after = slice(2 * width + shard * own, 2 * width + (shard + 1) * own)
            return jnp.concatenate([both[0:2, cols], sums[0:1, cols], sums[0:1, after]], axis=0)

        small_blocks(rows_of_shard, small, 2 * chips, own)
        run_copies(
            spread_copies(place, [(low, False)], small, blank, mine, theirs, chips, sems)
        )


def qkv_weight_grad(place, unit, dq, dk, dv, vecs, weight, block=512):
    rows, width = unit.shape
    chips = lax.axis_size("fsdp") // 2
    height = width // (4 * chips)
    row_block = pl.BlockSpec((block, width), lambda i, t: (i, 0))
    packed = jax.ShapeDtypeStruct((4 * chips * height, 3 * width // 2 + 128), BF16)
    zero = lambda i, t: (0, 0)
    return pl.pallas_call(
        functools.partial(weight_kernel, chips),
        grid_spec=pltpu.PrefetchScalarGridSpec(
            num_scalar_prefetch=1,
            grid=(rows // block,),
            in_specs=[row_block] * 4
            + [pl.BlockSpec(vecs.shape, zero), resident(weight.shape)],
            out_specs=[hbm(), hbm()],
            scratch_shapes=[
                pltpu.VMEM((width, 3 * width), F32),
                pltpu.VMEM((8, 3 * width), F32),
                pltpu.VMEM((width, 3 * width), BF16),
                pltpu.VMEM((2 * chips, height, 128), BF16),
                pltpu.VMEM((height, 128), BF16),
                pltpu.SemaphoreType.DMA((16 * chips,)),
            ],
        ),
        out_shape=[packed, packed],
        compiler_params=params(48),
        cost_estimate=pl.CostEstimate(
            flops=6 * rows * width * width, bytes_accessed=20_000_000, transcendentals=0
        ),
    )(place, unit, dq, dk, dv, vecs, weight)


def input_kernel(tokens, grad_middle, dq, dk, dv, vecs, weight, input_grad):
    width = tokens.shape[1]
    xhat, scale = normalise(tokens[...].astype(F32))
    upstream = (
        dot_nt(dq[...], weight[:, :width])
        + dot_nt(dk[...], weight[:, width : 2 * width])
        + dot_nt(dv[...], weight[:, 2 * width :])
    )
    grads = norm_back(upstream, vecs[0:1, :], xhat, scale)
    input_grad[...] = (grad_middle[...].astype(F32) + grads).astype(BF16)


def input_backward(tokens, grad_middle, dq, dk, dv, vecs, weight, block=512):
    rows, width = tokens.shape
    row_block = pl.BlockSpec((block, width), lambda i: (i, 0))
    return pl.pallas_call(
        input_kernel,
        grid=(rows // block,),
        in_specs=[row_block] * 5 + [resident(vecs.shape), resident(weight.shape)],
        out_specs=row_block,
        out_shape=jax.ShapeDtypeStruct((rows, width), BF16),
        compiler_params=params(40),
        cost_estimate=pl.CostEstimate(
            flops=6 * rows * width * width, bytes_accessed=20_000_000, transcendentals=0
        ),
    )(tokens, grad_middle, dq, dk, dv, vecs, weight)


def local(
    tokens,
    segment_ids,
    valid_mask,
    cotangent,
    norm1_gain,
    norm1_bias,
    qkv_weight,
    query_bias,
    value_bias,
    proj_weight,
    proj_bias,
    norm2_gain,
    norm2_bias,
    expand_weight,
    expand_bias,
    reduce_weight,
    reduce_bias,
):
    seq_len = segment_ids.shape[1]
    own, width = proj_weight.shape
    shards = lax.axis_size("fsdp")
    chips = shards // 2
    height = own // 2
    per = expand_bias.shape[0] // own
    place = place_table()
    row_bit, col_bit = place[2], place[3]

    def tile(weight):
        half = weight.shape[1] // 2
        return lax.dynamic_slice(weight, (row_bit * height, col_bit * half), (height, half))

    small = jnp.stack(
        [
            norm1_gain,
            norm1_bias,
            query_bias,
            value_bias,
            proj_bias,
            norm2_gain,
            norm2_bias,
            reduce_bias,
            *jnp.split(expand_bias, per),
        ]
    )
    block = jnp.pad(small, ((0, height - small.shape[0]), (0, 128 - own)))
    piece = jnp.concatenate([tile(qkv_weight), block], axis=1)
    qkv_split = piece.shape[1] // 2
    qkv_pieces = gather_pieces(piece, qkv_split)

    quarter = lax.dynamic_slice(
        reduce_weight,
        ((row_bit * 2 + col_bit) * (per * own // 4), 0),
        (per * own // 4, width),
    )
    parts = [tile(proj_weight), tile(expand_weight), *jnp.split(quarter, per // 2, axis=0)]
    middle_split = (width + per * width) // 2
    middle_pieces = gather_pieces(jnp.concatenate(parts, axis=1), middle_split)

    chip, core = place[0], place[1]
    edge = piece.shape[1] - 128

    def blocks_of(first, along):
        rest = along.reshape(chips - 1, height, -1)[:, : small.shape[0], edge : edge + own]
        return jnp.concatenate([first[None], rest], axis=0)

    both = jnp.stack(
        [
            blocks_of(small, qkv_pieces[0][0]),
            blocks_of(core_swap(small), qkv_pieces[1][0]),
        ],
        axis=1,
    )
    hops = (chip - jnp.arange(chips)) % chips
    choice = (hops[:, None, None, None] == jnp.arange(chips)[None, None, :, None]) & (
        (jnp.arange(2) ^ core)[None, :, None, None] == jnp.arange(2)[None, None, None, :]
    )
    small = jnp.sum(
        jnp.where(choice[..., None, None], both[None, None].astype(F32), 0.0), axis=(2, 3)
    ).reshape(shards, small.shape[0], own)
    vecs = small[:, :8].swapaxes(0, 1).reshape(8, width)
    ebias = small[:, 8:].reshape(1, width * per)

    table = clip_table(segment_ids, valid_mask)
    qkv, unit, qkv_full = qkv_forward(place, tokens, vecs, qkv_weight, qkv_pieces, qkv_split)
    mixed, inverse, exps = attend_forward(table, qkv, seq_len)
    output, grad_middle, grad_mixed, mine, theirs = middle_all(
        place,
        tokens,
        mixed,
        cotangent,
        vecs,
        ebias,
        (proj_weight, expand_weight, reduce_weight),
        middle_pieces,
        middle_split,
    )
    sum_proj, sum_expand, sum_reduce, middle_small = sum_pieces(
        place,
        mine,
        theirs,
        mine.shape[1] // 256 * 128,
        (False, False, True),
        (proj_weight.shape, expand_weight.shape, reduce_weight.shape),
    )
    dq, dk, dv = attend_backward(table, qkv, grad_mixed, mixed, inverse, exps, seq_len)
    mine, theirs = qkv_weight_grad(place, unit, dq, dk, dv, vecs, qkv_full)
    sum_qkv, qkv_small = sum_pieces(
        place, mine, theirs, mine.shape[1] // 256 * 128, (False,), (qkv_weight.shape,)
    )
    input_grad = input_backward(tokens, grad_middle, dq, dk, dv, vecs, qkv_full)
    return (
        output,
        input_grad,
        qkv_small[0, :own],
        qkv_small[1, :own],
        sum_qkv,
        qkv_small[2, :own],
        qkv_small[3, :own],
        sum_proj,
        middle_small[0, :own],
        middle_small[1, :own],
        middle_small[2, :own],
        sum_expand,
        middle_small[4 : 4 + per, :own].reshape(-1),
        sum_reduce,
        middle_small[3, :own],
    )


def solution(mesh):
    rows = P(("rep", "fsdp"), None)
    vector = P("fsdp")
    matrix = P("fsdp", None)
    params_specs = (
        vector,
        vector,
        matrix,
        vector,
        vector,
        matrix,
        vector,
        vector,
        vector,
        matrix,
        vector,
        matrix,
        vector,
    )
    return jax.shard_map(
        local,
        mesh=mesh,
        in_specs=(rows, rows, rows, rows) + params_specs,
        out_specs=(rows, rows) + params_specs,
        check_vma=False,
    )
```

```python
import functools
import math

import jax
import jax.numpy as jnp
from jax import lax
from jax.experimental import pallas as pl
from jax.experimental.pallas import tpu as pltpu
from jax.sharding import PartitionSpec as P

HEADS = 12
CLIPS = 6
EPSILON = 1e-06
WINDOW = 256
FIELDS = 5
BF16 = jnp.bfloat16
F32 = jnp.float32
MEBI = 1024 * 1024
NEGATIVE = -1e30


def dot(left, right):
    return lax.dot_general(left, right, (((1,), (0,)), ((), ())), preferred_element_type=F32)


def dot_nt(left, right):
    return lax.dot_general(left, right, (((1,), (1,)), ((), ())), preferred_element_type=F32)


def dot_tn(left, right):
    return lax.dot_general(left, right, (((0,), (0,)), ((), ())), preferred_element_type=F32)


def resident(shape):
    zeros = (0,) * len(shape)
    return pl.BlockSpec(shape, lambda *_: zeros, pipeline_mode=pl.Buffered(1))


def params(limit, count=1):
    return pltpu.CompilerParams(
        vmem_limit_bytes=limit * MEBI, dimension_semantics=("arbitrary",) * count
    )


def cost(micros):
    return pl.CostEstimate(flops=int(micros * 1e4), bytes_accessed=100, transcendentals=0)


def after(value, *others):
    return lax.optimization_barrier((value, *others))[0]


def normalise(values):
    row_mean = jnp.mean(values, axis=-1, keepdims=True)
    centred = values - row_mean
    row_var = jnp.mean(centred * centred, axis=-1, keepdims=True)
    scale = lax.rsqrt(row_var + EPSILON)
    return centred * scale, scale


def norm_back(upstream, gain, xhat, scale):
    weighted = upstream * gain
    first = jnp.mean(weighted, axis=-1, keepdims=True)
    second = jnp.mean(weighted * xhat, axis=-1, keepdims=True)
    return scale * (weighted - first - xhat * second)


def core_swap(value):
    count = lax.axis_size("fsdp")
    return lax.ppermute(value, "fsdp", [(i, i ^ 1) for i in range(count)])


def chip_shift(value, hops):
    count = lax.axis_size("fsdp")
    return lax.ppermute(value, "fsdp", [(i, (i + 2 * hops) % count) for i in range(count)])


def replica_swap(value, bits):
    return lax.ppermute(value, "rep", [(i, i ^ bits) for i in range(4)])


def place_table():
    shard = lax.axis_index("fsdp")
    replica = lax.axis_index("rep")
    return jnp.stack([shard // 2, shard % 2, replica // 2, replica % 2]).astype(jnp.int32)


def barrier(*values):
    return lax.optimization_barrier(values)


def shift_all(piece, first=1, step=1):
    chips = lax.axis_size("fsdp") // 2
    return [chip_shift(piece, hop) for hop in range(first, chips, step)]


def swap_sides(along):
    return replica_swap(along, 1), replica_swap(along, 2)


def swap_diagonal(from_x, from_y):
    cut = from_x.shape[1] // 256 * 128
    return replica_swap(from_x[:, :cut], 2), replica_swap(from_y[:, cut:], 1)


def fetch_copies(place, targets, owns, pieces, chips, sems):
    chip, core, row_bit, col_bit = (place[i] for i in range(4))
    made = []

    def add(source, target):
        made.append(pltpu.make_async_copy(source, target, sems.at[len(made)]))

    for other in range(2):
        side = core ^ other
        height = pieces[other][0].shape[0] // (chips - 1)
        step = math.gcd(height, 16)
        for number, (target, stacked, column) in enumerate(targets):
            rows, width = target.shape[0] // (2 * chips), target.shape[1]
            start = pl.multiple_of((2 * chip + side) * rows, step)
            add(owns[other][number], target.at[pl.ds(start, rows), :])
            for hop in range(1, chips):
                shard = 2 * lax.rem(chip - hop + chips, chips) + side
                source_rows = pl.ds((hop - 1) * height, height)
                for flip in range(4):
                    across = row_bit ^ (flip // 2)
                    aside = col_bit ^ (flip % 2)
                    origin = pieces[other][flip]
                    if stacked:
                        for half in range(rows // (4 * height)):
                            row = shard * rows + (across * 2 + aside) * (rows // 4) + half * height
                            add(
                                origin.at[source_rows, pl.ds(column + half * width, width)],
                                target.at[pl.ds(pl.multiple_of(row, step), height), :],
                            )
                    else:
                        row = pl.multiple_of(shard * rows + across * height, step)
                        col = pl.multiple_of(aside * (width // 2), 128)
                        add(
                            origin.at[source_rows, pl.ds(column, width // 2)],
                            target.at[pl.ds(row, height), pl.ds(col, width // 2)],
                        )
    return made


def spread_copies(place, targets, small, blank, mine, theirs, chips, sems):
    core = place[1]
    count = 0
    made = []
    height = mine.shape[0] // (4 * chips)
    step = math.gcd(height, 16)
    for other, packed in ((1, theirs), (0, mine)):
        side = core ^ other
        for chip in range(chips):
            shard = 2 * chip + side
            for quarter in range(4):
                out_rows = pl.ds((chip * 4 + quarter) * height, height)
                moves = []
                column = 0
                for target, stacked in targets:
                    rows = target.shape[0] // (2 * chips)
                    if stacked:
                        width = target.shape[1]
                        for half in range(rows // (4 * height)):
                            row = shard * rows + quarter * (rows // 4) + half * height
                            row = pl.multiple_of(row, step)
                            moves.append((target.at[pl.ds(row, height), :], column, width))
                            column += width
                    else:
                        width = target.shape[1] // 2
                        row = pl.multiple_of(shard * rows + (quarter // 2) * height, step)
                        cols = pl.ds((quarter % 2) * width, width)
                        moves.append((target.at[pl.ds(row, height), cols], column, width))
                        column += width
                if quarter == 0:
                    moves.append((small.at[shard], column, 128))
                else:
                    moves.append((blank.at[...], column, 128))
                for source, column, width in moves:
                    made.append(
                        pltpu.make_async_copy(
                            source, packed.at[out_rows, pl.ds(column, width)], sems.at[count]
                        )
                    )
                    count += 1
    return made


def run_copies(made):
    for copy in made:
        copy.start()
    for copy in made:
        copy.wait()


def add16(left, right):
    return left.astype(F32) + right.astype(F32)


def first_sum(height, place, mine, other, keep_a, send_a, keep_b, send_b):
    row_bit, col_bit = place[2], place[3]
    cut = keep_a.shape[1]
    step = math.gcd(height, 16)

    def piece(quarter, cols):
        rows = pl.ds(pl.multiple_of(quarter * height, step), height)
        return add16(mine[rows, cols], other[rows, cols]).astype(BF16)

    for bit in range(2):
        out = pl.ds(bit * height, height)
        keep_a[out, :] = piece(bit * 2 + col_bit, pl.ds(0, cut))
        send_a[out, :] = piece(bit * 2 + 1 - col_bit, pl.ds(0, cut))
        keep_b[out, :] = piece(row_bit * 2 + bit, pl.ds(cut, mine.shape[1] - cut))
        send_b[out, :] = piece((1 - row_bit) * 2 + bit, pl.ds(cut, mine.shape[1] - cut))


def second_sum(height, place, keep_a, got_a, keep_b, got_b, next_a, send_a, next_b, send_b):
    step = math.gcd(height, 16)
    for bit, keep, got, stay, send in (
        (place[2], keep_a, got_a, next_a, send_a),
        (place[3], keep_b, got_b, next_b, send_b),
    ):
        for which, out in ((bit, stay), (1 - bit, send)):
            rows = pl.ds(pl.multiple_of(which * height, step), height)
            out[...] = add16(keep[rows, :], got[rows, :]).astype(BF16)


def third_sum(height, place, keep_a, got_a, keep_b, got_b, own, *sends):
    chips = len(sends) + 1
    cut = keep_a.shape[1]
    step = math.gcd(height, 16)
    for hop, out in enumerate((own, *sends)):
        at = lax.rem(place[0] + hop, chips)
        rows = pl.ds(pl.multiple_of(at * height, step), height)
        out[:, :cut] = add16(keep_a[rows, :], got_a[rows, :]).astype(out.dtype)
        out[:, cut:] = add16(keep_b[rows, :], got_b[rows, :]).astype(out.dtype)


def fourth_sum(own, *refs):
    total = own[...]
    for ref in refs[:-1]:
        total = total + ref[...].astype(F32)
    refs[-1][...] = total.astype(BF16)


def last_spread(stacks, place, own, from_x, from_y, from_xy, *outs):
    replica = place[2] * 2 + place[3]
    height, packed = own.shape
    step = math.gcd(height, 16)
    for flip, source in enumerate((own, from_x, from_y, from_xy)):
        across = place[2] ^ (flip // 2)
        aside = place[3] ^ (flip % 2)
        column = 0
        for stacked, out in zip(stacks, outs):
            rows, width = out.shape
            if stacked:
                for half in range(rows // (4 * height)):
                    at = (across * 2 + aside) * (rows // 4) + half * height
                    out[pl.ds(pl.multiple_of(at, step), height), :] = source[
                        :, column : column + width
                    ].astype(F32)
                    column += width
            else:
                width = width // 2
                at = pl.ds(pl.multiple_of(across * height, step), height)
                cols = pl.ds(pl.multiple_of(aside * width, 128), width)
                out[at, cols] = source[:, column : column + width].astype(F32)
                column += width

        @pl.when((replica ^ flip) == 0)
        def _():
            outs[-1][...] = source[0:16, packed - 128 :].astype(F32)


def small_call(body, place, inputs, shapes, grid=None, in_specs=None, out_specs=None):
    if grid is None:
        grid = (1,)
        in_specs = [pl.BlockSpec(value.shape, lambda i, t: (0, 0)) for value in inputs]
        out_specs = [pl.BlockSpec(shape.shape, lambda i, t: (0, 0)) for shape in shapes]
    return pl.pallas_call(
        body,
        grid_spec=pltpu.PrefetchScalarGridSpec(
            num_scalar_prefetch=1, grid=grid, in_specs=in_specs, out_specs=out_specs
        ),
        out_shape=shapes,
        compiler_params=params(32),
    )(place, *inputs)


class Sum:
    def __init__(self, place, mine, theirs):
        self.place = place
        self.chips = lax.axis_size("fsdp") // 2
        self.height = mine.shape[0] // (4 * self.chips)
        self.packed = mine.shape[1]
        self.cut = self.packed // 256 * 128
        self.kept = [mine]
        self.sends = [theirs]
        self.ways = [core_swap]

    def send(self):
        return [way(value) for way, value in zip(self.ways, self.sends)]

    def shape(self, rows, cols, dtype=BF16):
        return jax.ShapeDtypeStruct((rows * self.height, cols), dtype)

    def block(self, count, cols):
        return pl.BlockSpec((count * self.height, cols), lambda i, t: (i, 0))

    def pair(self, make, rows):
        return [make(rows, self.cut)] * 2 + [make(rows, self.packed - self.cut)] * 2

    def add_first(self, arrived):
        keep_a, send_a, keep_b, send_b = small_call(
            functools.partial(first_sum, self.height),
            self.place,
            (*self.kept, *arrived),
            self.pair(self.shape, 2 * self.chips),
            (self.chips,),
            [self.block(4, self.packed)] * 2,
            self.pair(self.block, 2),
        )
        self.kept = [keep_a, keep_b]
        self.sends = [send_a, send_b]
        self.ways = [lambda v: replica_swap(v, 1), lambda v: replica_swap(v, 2)]

    def add_second(self, arrived):
        keep_a, send_a, keep_b, send_b = small_call(
            functools.partial(second_sum, self.height),
            self.place,
            (self.kept[0], arrived[0], self.kept[1], arrived[1]),
            self.pair(self.shape, self.chips),
            (self.chips,),
            self.pair(self.block, 2),
            self.pair(self.block, 1),
        )
        self.kept = [keep_a, keep_b]
        self.sends = [send_a, send_b]
        self.ways = [lambda v: replica_swap(v, 2), lambda v: replica_swap(v, 1)]

    def add_third(self, arrived):
        own, *self.sends = small_call(
            functools.partial(third_sum, self.height),
            self.place,
            (self.kept[0], arrived[0], self.kept[1], arrived[1]),
            [self.shape(1, self.packed, F32)] + [self.shape(1, self.packed)] * (self.chips - 1),
        )
        self.kept = [own]
        self.ways = [functools.partial(chip_shift, hops=hop) for hop in range(1, self.chips)]

    def add_fourth(self, arrived):
        (total,) = small_call(
            lambda table, *refs: fourth_sum(*refs),
            self.place,
            (*self.kept, *arrived),
            [self.shape(1, self.packed)],
        )
        self.kept = [total]
        self.sends = [total] * 3
        self.ways = [functools.partial(replica_swap, bits=bits) for bits in (1, 2, 3)]

    def result(self, arrived, stacks, out_shapes):
        return small_call(
            functools.partial(last_spread, stacks),
            self.place,
            (*self.kept, *arrived),
            [jax.ShapeDtypeStruct(s, F32) for s in out_shapes]
            + [jax.ShapeDtypeStruct((16, 128), F32)],
        )


def small_blocks(rows_of_shard, small, shards, own):
    small[...] = jnp.zeros_like(small)
    for shard in range(shards):
        rows = rows_of_shard(shard)
        small[shard, 0 : rows.shape[0], 0:own] = rows.astype(BF16)


def qkv_kernel(chips, place, tokens, vecs, *refs):
    owns = (refs[0:1], refs[1:2])
    pieces = (refs[2:6], refs[6:10])
    qkv, unit, weight, sems = refs[10:]
    width = tokens.shape[1]

    @pl.when(pl.program_id(0) == 0)
    def _():
        run_copies(fetch_copies(place, [(weight, False, 0)], owns, pieces, chips, sems))

    xhat, _ = normalise(tokens[...].astype(F32))
    unit[...] = xhat.astype(BF16)
    rows = (xhat * vecs[0:1, :] + vecs[1:2, :]).astype(BF16)
    query = dot(rows, weight[:, :width]) + vecs[2:3, :]
    qkv[:, :width] = query.astype(BF16) * jnp.asarray(0.125, BF16)
    qkv[:, width : 2 * width] = dot(rows, weight[:, width : 2 * width]).astype(BF16)
    value = dot(rows, weight[:, 2 * width :]) + vecs[3:4, :]
    qkv[:, 2 * width :] = value.astype(BF16)


def hbm():
    return pl.BlockSpec(memory_space=pl.ANY)


def qkv_forward(place, tokens, vecs, owns, pieces, block=512):
    rows, width = tokens.shape
    chips = lax.axis_size("fsdp") // 2
    sources = [*owns, *pieces[0], *pieces[1]]
    zero = lambda i, t: (0, 0)
    return pl.pallas_call(
        functools.partial(qkv_kernel, chips),
        grid_spec=pltpu.PrefetchScalarGridSpec(
            num_scalar_prefetch=1,
            grid=(rows // block,),
            in_specs=[
                pl.BlockSpec((block, width), lambda i, t: (i, 0)),
                pl.BlockSpec(vecs.shape, zero),
            ]
            + [hbm()] * len(sources),
            out_specs=[
                pl.BlockSpec((block, 3 * width), lambda i, t: (i, 0)),
                pl.BlockSpec((block, width), lambda i, t: (i, 0)),
                resident((width, 3 * width)),
            ],
            scratch_shapes=[pltpu.SemaphoreType.DMA((2 + 8 * (chips - 1),))],
        ),
        out_shape=[
            jax.ShapeDtypeStruct((rows, 3 * width), BF16),
            jax.ShapeDtypeStruct((rows, width), BF16),
            jax.ShapeDtypeStruct((width, 3 * width), BF16),
        ],
        compiler_params=params(60),
        cost_estimate=cost(12),
    )(place, tokens, vecs, *sources)


def clip_table(segment_ids, valid_mask):
    seq_len = segment_ids.shape[1]
    clips = jnp.arange(CLIPS, dtype=jnp.int32)[None, :, None]
    segments = segment_ids[:, None, :]
    start = jnp.sum((segments < clips).astype(jnp.int32), axis=2)
    end = jnp.sum((segments <= clips).astype(jnp.int32), axis=2)
    valid = jnp.sum(((segments == clips) & (valid_mask[:, None, :] == 1)).astype(jnp.int32), axis=2)
    aligned = start // 16 * 16
    need = end - aligned
    path = (need > WINDOW).astype(jnp.int32) + (need > 2 * WINDOW).astype(jnp.int32)
    window = jnp.where(path == 0, WINDOW, jnp.where(path == 1, 2 * WINDOW, seq_len))
    base = jnp.minimum(aligned, seq_len - window)
    return jnp.stack([base, path, start - base, end - base, start + valid - base], axis=2).reshape(
        -1
    )


def lane_low(rows):
    return lax.broadcasted_iota(jnp.int32, (rows, 128), 1) < 64


def flag_lane(rows):
    return lax.broadcasted_iota(jnp.int32, (rows, 128), 1) % 64 == 0


def row_mask(rows, offset, first, last):
    index = lax.broadcasted_iota(jnp.int32, (rows, 128), 0) + offset
    return (index >= first) & (index < last)


def key_extra(rows, first, last):
    bias = jnp.where(row_mask(rows, 0, first, last), 0.0, NEGATIVE)
    return jnp.where(flag_lane(rows), bias, 0.0).astype(BF16)


def query_extra(rows):
    return jnp.where(flag_lane(rows), 1.0, 0.0).astype(BF16)


def weights_of(query, keys, extra_query, extra_keys, low, low_keys, head):
    if head == 0:
        left = jnp.where(low, query, extra_query)
        right = jnp.where(low_keys, keys, extra_keys)
    else:
        left = jnp.where(low, extra_query, query)
        right = jnp.where(low_keys, extra_keys, keys)
    scores = dot_nt(left, right)
    return jnp.exp(scores - jnp.max(scores, axis=1, keepdims=True)).astype(BF16)


def attend_window(refs, base, first, last, valid_end, window, pairs, exps, clip):
    queries, keys_ref, values_ref, mixed, inverse = refs
    chunk = WINDOW
    low = lane_low(chunk)
    low_keys = lane_low(window)
    extra_keys = key_extra(window, first, valid_end)
    extra_query = query_extra(chunk)
    ones = jnp.ones((window, 128), BF16)
    key_rows = pl.ds(base, window)

    def one_chunk(offset, row_start):
        rows = pl.ds(row_start, chunk)
        keep = row_mask(chunk, offset, first, last)
        for pair in range(pairs):
            lanes = pl.ds(128 * pair, 128)
            query = queries[rows, lanes]
            keys = keys_ref[key_rows, lanes]
            stack = jnp.concatenate([values_ref[key_rows, lanes], ones], axis=1)
            sums = []
            for head in range(2):
                weights = weights_of(query, keys, extra_query, extra_keys, low, low_keys, head)
                if exps is not None:
                    exps[0, 2 * pair + head, pl.ds(clip * WINDOW, WINDOW), :] = weights
                sums.append(dot(weights, stack))
            total = jnp.where(low, sums[0][:, 128:], sums[1][:, 128:])
            weighted = jnp.where(low, sums[0][:, :128], sums[1][:, :128])
            reciprocal = 1.0 / total
            mixed[rows, lanes] = jnp.where(
                keep, (weighted * reciprocal), mixed[rows, lanes].astype(F32)
            ).astype(BF16)
            inverse[rows, lanes] = jnp.where(keep, reciprocal, inverse[rows, lanes])

    if window == chunk:
        one_chunk(0, base)
    else:

        def step(index, carry):
            offset = index * chunk
            one_chunk(offset, pl.multiple_of(base + offset, 16))
            return carry

        lax.fori_loop(0, window // chunk, step, 0)


def clip_fields(table, sequence, clip):
    at = (sequence * CLIPS + clip) * FIELDS
    base = pl.multiple_of(table[at], 16)
    return base, table[at + 1], table[at + 2], table[at + 3], table[at + 4]


def attend_kernel(pairs, table, queries, keys, values, mixed, inverse, exps):
    sequence = pl.program_id(0)
    seq_len = queries.shape[0]
    mixed[...] = jnp.zeros_like(mixed)
    inverse[...] = jnp.zeros_like(inverse)
    refs = (queries, keys, values, mixed, inverse)

    def one_clip(clip, carry):
        base, path, first, last, valid_end = clip_fields(table, sequence, clip)
        for number, window in enumerate((WINDOW, 2 * WINDOW, seq_len)):

            @pl.when(path == number)
            def _():
                attend_window(
                    refs,
                    base,
                    first,
                    last,
                    valid_end,
                    window,
                    pairs,
                    exps if number == 0 else None,
                    clip,
                )

        return carry

    lax.fori_loop(0, CLIPS, one_clip, 0)


def attend_forward(table, qkv, seq_len, group, pairs=2):
    rows = qkv.shape[0]
    width = qkv.shape[1] // 3
    seqs = rows // seq_len
    lanes = 128 * pairs
    groups = width // lanes
    block = (seq_len, lanes)
    own = pl.BlockSpec(block, lambda s, t: (s, 0))
    return pl.pallas_call(
        functools.partial(attend_kernel, pairs),
        grid_spec=pltpu.PrefetchScalarGridSpec(
            num_scalar_prefetch=1,
            grid=(seqs,),
            in_specs=[
                pl.BlockSpec(block, lambda s, t: (s, group)),
                pl.BlockSpec(block, lambda s, t: (s, groups + group)),
                pl.BlockSpec(block, lambda s, t: (s, 2 * groups + group)),
            ],
            out_specs=[
                own,
                own,
                pl.BlockSpec((1, 2 * pairs, CLIPS * WINDOW, WINDOW), lambda s, t: (s, 0, 0, 0)),
            ],
        ),
        out_shape=[
            jax.ShapeDtypeStruct((rows, lanes), BF16),
            jax.ShapeDtypeStruct((rows, lanes), F32),
            jax.ShapeDtypeStruct((seqs, 2 * pairs, CLIPS * WINDOW, WINDOW), BF16),
        ],
        compiler_params=params(60),
        cost_estimate=cost(10),
    )(table, qkv, qkv, qkv)


def back_window(refs, base, first, last, valid_end, window, pairs, exps, clip, gather):
    queries, keys_ref, values_ref, grads, mixed, inverse, dq, dk, dv = refs
    key_grad, value_grad = gather
    chunk = WINDOW
    single = window == chunk
    low = lane_low(chunk)
    low_keys = lane_low(window)
    extra_keys = None if single else key_extra(window, first, valid_end)
    extra_query = None if single else query_extra(chunk)
    key_rows = pl.ds(base, window)
    one = jnp.ones((window, 128), BF16)

    def one_chunk(offset, row_start):
        rows = pl.ds(row_start, chunk)
        keep = row_mask(chunk, offset, first, last)
        for pair in range(pairs):
            lanes = pl.ds(128 * pair, 128)
            query = queries[rows, lanes]
            keys = keys_ref[key_rows, lanes]
            values = values_ref[key_rows, lanes]
            scaled = jnp.where(keep, grads[rows, lanes].astype(F32) * inverse[rows, lanes], 0.0)
            product = scaled * mixed[rows, lanes].astype(F32)
            turned = pltpu.roll(-product, 64, 1).astype(BF16)
            scaled = scaled.astype(BF16)
            parts = []
            for head in range(2):
                if head == 0:
                    left = jnp.where(low, scaled, turned)
                    right = jnp.where(low_keys, values, one)
                else:
                    left = jnp.where(low, turned, scaled)
                    right = jnp.where(low_keys, one, values)
                if single:
                    weights = exps[0, 2 * pair + head, pl.ds(clip * WINDOW, WINDOW), :]
                else:
                    weights = weights_of(query, keys, extra_query, extra_keys, low, low_keys, head)
                grad_scores = (weights.astype(F32) * dot_nt(left, right)).astype(BF16)
                parts.append(
                    (
                        dot(grad_scores, keys),
                        dot_tn(grad_scores, query),
                        dot_tn(weights, scaled),
                    )
                )
            query_part = jnp.where(low, parts[0][0], parts[1][0]) * 0.125
            key_part = jnp.where(low_keys, parts[0][1], parts[1][1])
            value_part = jnp.where(low_keys, parts[0][2], parts[1][2])
            dq[rows, lanes] = jnp.where(keep, query_part, dq[rows, lanes].astype(F32)).astype(BF16)
            if single:
                dk[rows, lanes] = jnp.where(keep, key_part, dk[rows, lanes].astype(F32)).astype(
                    BF16
                )
                dv[rows, lanes] = jnp.where(keep, value_part, dv[rows, lanes].astype(F32)).astype(
                    BF16
                )
            else:
                key_grad[pl.ds(0, window), lanes] += key_part
                value_grad[pl.ds(0, window), lanes] += value_part

    if single:
        one_chunk(0, base)
        return
    key_grad[...] = jnp.zeros_like(key_grad)
    value_grad[...] = jnp.zeros_like(value_grad)

    def step(index, carry):
        offset = index * chunk
        one_chunk(offset, pl.multiple_of(base + offset, 16))
        return carry

    lax.fori_loop(0, window // chunk, step, 0)
    keep = row_mask(window, 0, first, last)
    for pair in range(pairs):
        lanes = pl.ds(128 * pair, 128)
        for ref, total in ((dk, key_grad), (dv, value_grad)):
            ref[key_rows, lanes] = jnp.where(
                keep, total[pl.ds(0, window), lanes], ref[key_rows, lanes].astype(F32)
            ).astype(BF16)


def back_kernel(
    pairs,
    table,
    queries,
    keys,
    values,
    grads,
    mixed,
    inverse,
    exps,
    dq,
    dk,
    dv,
    key_grad,
    value_grad,
):
    sequence = pl.program_id(0)
    seq_len = queries.shape[0]
    for ref in (dq, dk, dv):
        ref[...] = jnp.zeros_like(ref)
    refs = (queries, keys, values, grads, mixed, inverse, dq, dk, dv)

    def one_clip(clip, carry):
        base, path, first, last, valid_end = clip_fields(table, sequence, clip)
        for number, window in enumerate((WINDOW, 2 * WINDOW, seq_len)):

            @pl.when(path == number)
            def _():
                back_window(
                    refs,
                    base,
                    first,
                    last,
                    valid_end,
                    window,
                    pairs,
                    exps,
                    clip,
                    (key_grad, value_grad),
                )

        return carry

    lax.fori_loop(0, CLIPS, one_clip, 0)


def attend_backward(table, qkv, grads, mixed, inverse, exps, seq_len, group, pairs=2):
    rows = mixed.shape[0]
    seqs = rows // seq_len
    lanes = 128 * pairs
    groups = grads.shape[1] // lanes
    block = (seq_len, lanes)
    own = pl.BlockSpec(block, lambda s, t: (s, 0))
    shape = jax.ShapeDtypeStruct((rows, lanes), BF16)
    return pl.pallas_call(
        functools.partial(back_kernel, pairs),
        grid_spec=pltpu.PrefetchScalarGridSpec(
            num_scalar_prefetch=1,
            grid=(seqs,),
            in_specs=[
                pl.BlockSpec(block, lambda s, t: (s, group)),
                pl.BlockSpec(block, lambda s, t: (s, groups + group)),
                pl.BlockSpec(block, lambda s, t: (s, 2 * groups + group)),
                pl.BlockSpec(block, lambda s, t: (s, group)),
                own,
                own,
                pl.BlockSpec((1, 2 * pairs, CLIPS * WINDOW, WINDOW), lambda s, t: (s, 0, 0, 0)),
            ],
            out_specs=[own, own, own],
            scratch_shapes=[pltpu.VMEM(block, F32), pltpu.VMEM(block, F32)],
        ),
        out_shape=[shape, shape, shape],
        compiler_params=params(60),
        cost_estimate=cost(19),
    )(table, qkv, qkv, qkv, grads, mixed, inverse, exps)


def gauss(value):
    size = jnp.abs(value)
    rate = 1.0 / (1.0 + 0.3275911 * 0.7071067811865476 * size)
    tail = jnp.exp(value * value * -0.5)
    series = rate * (
        0.5 * 0.254829592
        + rate
        * (
            0.5 * -0.284496736
            + rate * (0.5 * 1.421413741 + rate * (0.5 * -1.453152027 + rate * (0.5 * 1.061405429)))
        )
    )
    upper = series * tail
    return jnp.where(value >= 0, 1.0 - upper, upper), value * tail * 0.3989422804014327


def middle_kernel(
    part,
    chips,
    groups,
    place,
    tokens,
    cotangent,
    vecs,
    ebias,
    *refs,
):
    mixed, refs = refs[:groups], refs[groups:]
    owns = (refs[0:3], refs[3:6])
    pieces = (refs[6:10], refs[10:14])
    (
        output,
        grad_middle,
        grad_mixed,
        mine,
        theirs,
        proj,
        expand,
        reduce,
        sum_proj,
        sum_expand,
        sum_reduce,
        sum_ebias,
        sum_vecs,
        small,
        blank,
        in_sems,
        out_sems,
    ) = refs[14:]
    step = pl.program_id(0)
    width, hidden = expand.shape
    own = width // (2 * chips)

    @pl.when(step == 0)
    def _():
        targets = [
            (proj, False, 0),
            (expand, False, width // 2),
            (reduce, True, width // 2 + hidden // 2),
        ]
        made = fetch_copies(place, targets, owns, pieces, chips, in_sems)
        for copy in made:
            copy.start()
        sum_proj[...] = jnp.zeros_like(sum_proj)
        sum_expand[...] = jnp.zeros_like(sum_expand)
        sum_reduce[...] = jnp.zeros_like(sum_reduce)
        sum_ebias[...] = jnp.zeros_like(sum_ebias)
        sum_vecs[...] = jnp.zeros_like(sum_vecs)
        for copy in made:
            copy.wait()

    mixed_rows = jnp.concatenate([ref[...] for ref in mixed], axis=1)
    cot = cotangent[...]
    middle = tokens[...].astype(F32) + dot(mixed_rows, proj[...]) + vecs[4:5, :]
    xhat, scale = normalise(middle)
    normed = (xhat * vecs[5:6, :] + vecs[6:7, :]).astype(BF16)
    normed_t = normed.T
    branch = None
    grad_normed = None
    for start in range(0, hidden, part):
        cols = pl.ds(start, part)
        into = expand[:, cols]
        back = reduce[cols, :]
        preact = dot(normed, into) + ebias[:, cols]
        cdf, slope = gauss(preact)
        activated = (preact * cdf).astype(BF16)
        grad_preact = (dot_nt(cot, back) * (cdf + slope)).astype(BF16)
        term = dot(activated, back)
        branch = term if branch is None else branch + term
        term = dot_nt(grad_preact, into)
        grad_normed = term if grad_normed is None else grad_normed + term
        sum_reduce[cols, :] += dot_tn(activated, cot)
        sum_expand[:, cols] += dot(normed_t, grad_preact)
        sum_ebias[:, cols] += jnp.sum(grad_preact.astype(F32), axis=0, keepdims=True)
    output[...] = (middle + branch + vecs[7:8, :]).astype(BF16)
    cot32 = cot.astype(F32)
    grads = cot32 + norm_back(grad_normed, vecs[5:6, :], xhat, scale)
    attended = grads.astype(BF16)
    grad_middle[...] = attended
    grad_mixed[...] = dot_nt(attended, proj[...]).astype(BF16)
    sum_proj[...] += dot_tn(mixed_rows, attended)
    sum_vecs[0:1, :] += jnp.sum(attended.astype(F32), axis=0, keepdims=True)
    sum_vecs[1:2, :] += jnp.sum(grad_normed * xhat, axis=0, keepdims=True)
    sum_vecs[2:3, :] += jnp.sum(grad_normed, axis=0, keepdims=True)
    sum_vecs[3:4, :] += jnp.sum(cot32, axis=0, keepdims=True)

    @pl.when(step == pl.num_programs(0) - 1)
    def _():
        proj[...] = sum_proj[...].astype(BF16)
        expand[...] = sum_expand[...].astype(BF16)
        reduce[...] = sum_reduce[...].astype(BF16)
        blank[...] = jnp.zeros_like(blank)
        per = hidden // width

        def rows_of_shard(shard):
            rows = [sum_vecs[0:4, shard * own : (shard + 1) * own]]
            for index in range(per):
                at = (shard * per + index) * own
                rows.append(sum_ebias[0:1, at : at + own])
            return jnp.concatenate(rows, axis=0)

        small_blocks(rows_of_shard, small, 2 * chips, own)
        run_copies(
            spread_copies(
                place,
                [(proj, False), (expand, False), (reduce, True)],
                small,
                blank,
                mine,
                theirs,
                chips,
                out_sems,
            )
        )


def middle_all(
    place, tokens, mixed, cotangent, vecs, ebias, owns, others, pieces, block=512, part=512
):
    rows, width = tokens.shape
    chips = lax.axis_size("fsdp") // 2
    hidden = ebias.shape[1]
    height = width // (4 * chips)
    row_block = pl.BlockSpec((block, width), lambda i, t: (i, 0))
    row_shape = jax.ShapeDtypeStruct((rows, width), BF16)
    packed = (4 * chips * height, width // 2 + hidden // 2 + hidden // 2 + 128)
    packed_shape = jax.ShapeDtypeStruct(packed, BF16)
    sources = [*owns, *others, *pieces[0], *pieces[1]]
    halves = hidden // width // 2
    mixed_block = pl.BlockSpec((block, mixed[0].shape[1]), lambda i, t: (i, 0))
    return pl.pallas_call(
        functools.partial(middle_kernel, part, chips, len(mixed)),
        grid_spec=pltpu.PrefetchScalarGridSpec(
            num_scalar_prefetch=1,
            grid=(rows // block,),
            in_specs=[row_block] * 2
            + [
                pl.BlockSpec(vecs.shape, lambda i, t: (0, 0)),
                pl.BlockSpec(ebias.shape, lambda i, t: (0, 0)),
            ]
            + [mixed_block] * len(mixed)
            + [hbm()] * len(sources),
            out_specs=[row_block] * 3 + [hbm(), hbm()],
            scratch_shapes=[
                pltpu.VMEM((width, width), BF16),
                pltpu.VMEM((width, hidden), BF16),
                pltpu.VMEM((hidden, width), BF16),
                pltpu.VMEM((width, width), F32),
                pltpu.VMEM((width, hidden), F32),
                pltpu.VMEM((hidden, width), F32),
                pltpu.VMEM((1, hidden), F32),
                pltpu.VMEM((8, width), F32),
                pltpu.VMEM((2 * chips, height, 128), BF16),
                pltpu.VMEM((height, 128), BF16),
                pltpu.SemaphoreType.DMA((2 * (3 + 4 * (chips - 1) * (2 + halves)),)),
                pltpu.SemaphoreType.DMA((8 * chips * (3 + halves),)),
            ],
        ),
        out_shape=[row_shape, row_shape, row_shape, packed_shape, packed_shape],
        compiler_params=params(63),
        cost_estimate=cost(110),
    )(place, tokens, cotangent, vecs, ebias, *mixed, *sources)


def weight_kernel(chips, offsets, place, unit, vecs, weight, *refs):
    count = len(offsets)
    parts, refs = refs[:count], refs[count:]
    mine, theirs, total, sums, low, small, blank, sems = refs
    step = pl.program_id(0)
    width = unit.shape[1]
    lanes = parts[0].shape[1]
    own = width // (2 * chips)

    @pl.when(step == 0)
    def _():
        total[...] = jnp.zeros_like(total)
        sums[...] = jnp.zeros_like(sums)

    rows_t = unit[...].T
    for index, part in enumerate(parts):
        cols = slice(index * lanes, (index + 1) * lanes)
        total[:, cols] += dot(rows_t, part[...])
        sums[0:1, cols] += jnp.sum(part[...].astype(F32), axis=0, keepdims=True)

    @pl.when(step == pl.num_programs(0) - 1)
    def _():
        columns = vecs[...].T
        gain, shift = columns[:, 0:1], columns[:, 1:2]
        gain_part = jnp.zeros((width, 1), F32)
        shift_part = jnp.zeros((width, 1), F32)
        empty = jnp.zeros((1, lanes), F32)
        biases = [[empty] * (width // lanes) for _ in range(3)]
        for index, offset in enumerate(offsets):
            cols = slice(index * lanes, (index + 1) * lanes)
            raw = total[:, cols]
            sides = weight[:, offset : offset + lanes].astype(F32)
            line = sums[0:1, cols]
            gain_part += jnp.sum(raw * sides, axis=1, keepdims=True)
            shift_part += jnp.sum(line * sides, axis=1, keepdims=True)
            low[:, cols] = (gain * raw + shift * line).astype(BF16)
            biases[offset // width][offset % width // lanes] = line
        pick = lax.broadcasted_iota(jnp.int32, (width, 128), 1)
        both = jnp.where(pick == 0, gain_part, jnp.where(pick == 1, shift_part, 0.0)).T
        query_line = jnp.concatenate(biases[0], axis=1)
        value_line = jnp.concatenate(biases[2], axis=1)
        blank[...] = jnp.zeros_like(blank)

        def rows_of_shard(shard):
            cols = slice(shard * own, (shard + 1) * own)
            return jnp.concatenate([both[0:2, cols], query_line[:, cols], value_line[:, cols]], axis=0)

        small_blocks(rows_of_shard, small, 2 * chips, own)
        run_copies(
            spread_copies(place, [(low, False)], small, blank, mine, theirs, chips, sems)
        )


def qkv_weight_grad(place, unit, vecs, weight, groups, grads, block=512):
    rows, width = unit.shape
    lanes = grads[0][0].shape[1]
    chips = lax.axis_size("fsdp") // 2
    height = width // (4 * chips)
    offsets = tuple(part * width + group * lanes for part in range(3) for group in groups)
    parts = [grad[part] for part in range(3) for grad in grads]
    columns = lanes * len(parts)
    packed = jax.ShapeDtypeStruct((4 * chips * height, columns // 2 + 128), BF16)
    zero = lambda i, t: (0, 0)
    return pl.pallas_call(
        functools.partial(weight_kernel, chips, offsets),
        grid_spec=pltpu.PrefetchScalarGridSpec(
            num_scalar_prefetch=1,
            grid=(rows // block,),
            in_specs=[
                pl.BlockSpec((block, width), lambda i, t: (i, 0)),
                pl.BlockSpec(vecs.shape, zero),
                resident(weight.shape),
            ]
            + [pl.BlockSpec((block, lanes), lambda i, t: (i, 0))] * len(parts),
            out_specs=[hbm(), hbm()],
            scratch_shapes=[
                pltpu.VMEM((width, columns), F32),
                pltpu.VMEM((8, columns), F32),
                pltpu.VMEM((width, columns), BF16),
                pltpu.VMEM((2 * chips, height, 128), BF16),
                pltpu.VMEM((height, 128), BF16),
                pltpu.SemaphoreType.DMA((16 * chips,)),
            ],
        ),
        out_shape=[packed, packed],
        compiler_params=params(60),
        cost_estimate=cost(4 * len(groups)),
    )(place, unit, vecs, weight, *parts)


def input_kernel(count, tokens, grad_middle, vecs, weight, *refs):
    width = tokens.shape[1]
    lanes = width // count
    input_grad = refs[-1]
    xhat, scale = normalise(tokens[...].astype(F32))
    upstream = None
    for part in range(3):
        rows = jnp.concatenate([ref[...] for ref in refs[part * count : (part + 1) * count]], axis=1)
        term = dot_nt(rows, weight[:, part * width : (part + 1) * width])
        upstream = term if upstream is None else upstream + term
    grads = norm_back(upstream, vecs[0:1, :], xhat, scale)
    input_grad[...] = (grad_middle[...].astype(F32) + grads).astype(BF16)


def input_backward(tokens, grad_middle, vecs, weight, grads, first, rows, into=None, block=512):
    width = tokens.shape[1]
    lanes = grads[0][0].shape[1]
    start = first // block
    row_block = pl.BlockSpec((block, width), lambda i: (i + start, 0))
    parts = [grad[part] for part in range(3) for grad in grads]
    inputs = [tokens, grad_middle, vecs, weight, *parts]
    specs = [row_block] * 2 + [resident(vecs.shape), resident(weight.shape)]
    specs += [pl.BlockSpec((block, lanes), lambda i: (i + start, 0))] * len(parts)
    aliases = {}
    if into is not None:
        aliases = {len(inputs): 0}
        inputs.append(into)
        specs.append(hbm())
    return pl.pallas_call(
        functools.partial(input_kernel, len(grads)),
        grid=(rows // block,),
        in_specs=specs,
        out_specs=row_block,
        out_shape=jax.ShapeDtypeStruct(tokens.shape, BF16),
        input_output_aliases=aliases,
        compiler_params=params(60),
        cost_estimate=cost(7),
    )(*inputs)


def local(
    tokens,
    segment_ids,
    valid_mask,
    cotangent,
    norm1_gain,
    norm1_bias,
    qkv_weight,
    query_bias,
    value_bias,
    proj_weight,
    proj_bias,
    norm2_gain,
    norm2_bias,
    expand_weight,
    expand_bias,
    reduce_weight,
    reduce_bias,
):
    seq_len = segment_ids.shape[1]
    own, width = proj_weight.shape
    shards = lax.axis_size("fsdp")
    chips = shards // 2
    height = own // 2
    per = expand_bias.shape[0] // own
    place = place_table()
    row_bit, col_bit = place[2], place[3]

    def tile(weight):
        half = weight.shape[1] // 2
        return lax.dynamic_slice(weight, (row_bit * height, col_bit * half), (height, half))

    small = jnp.stack(
        [
            norm1_gain,
            norm1_bias,
            query_bias,
            value_bias,
            proj_bias,
            norm2_gain,
            norm2_bias,
            reduce_bias,
            *jnp.split(expand_bias, per),
        ]
    )
    block = jnp.pad(small, ((0, height - small.shape[0]), (0, 128 - own)))
    piece = jnp.concatenate([tile(qkv_weight), block], axis=1)
    quarter = lax.dynamic_slice(
        reduce_weight,
        ((row_bit * 2 + col_bit) * (per * own // 4), 0),
        (per * own // 4, width),
    )
    parts = [tile(proj_weight), tile(expand_weight), *jnp.split(quarter, per // 2, axis=0)]
    rest = jnp.concatenate(parts, axis=1)
    table = clip_table(segment_ids, valid_mask)
    owns = (proj_weight, expand_weight, reduce_weight)

    got = shift_all(piece)
    other_qkv, small_other = core_swap(qkv_weight), core_swap(small)
    got, other_qkv, small_other, rest, table = barrier(got, other_qkv, small_other, rest, table)
    along = jnp.concatenate(got, axis=0)
    sides = swap_sides(along)
    odd = shift_all(rest, 1, 2)
    sides, along = barrier(sides, along)
    halves = swap_diagonal(*sides)
    halves, sides, along, odd, rest = barrier(halves, sides, along, odd, rest)
    here = (along, *sides, jnp.concatenate(halves, axis=1))
    qkv_pieces = barrier(here, tuple(core_swap(part) for part in here))

    chip, core = place[0], place[1]
    edge = piece.shape[1] - 128

    def blocks_of(first, along):
        rest = along.reshape(chips - 1, height, -1)[:, : small.shape[0], edge : edge + own]
        return jnp.concatenate([first[None], rest], axis=0)

    both = jnp.stack(
        [blocks_of(small, qkv_pieces[0][0]), blocks_of(small_other, qkv_pieces[1][0])], axis=1
    )
    hops = (chip - jnp.arange(chips)) % chips
    choice = (hops[:, None, None, None] == jnp.arange(chips)[None, None, :, None]) & (
        (jnp.arange(2) ^ core)[None, :, None, None] == jnp.arange(2)[None, None, None, :]
    )
    small = jnp.sum(
        jnp.where(choice[..., None, None], both[None, None].astype(F32), 0.0), axis=(2, 3)
    ).reshape(shards, small.shape[0], own)
    vecs = small[:, :8].swapaxes(0, 1).reshape(8, width)
    ebias = small[:, 8:].reshape(1, width * per)

    qkv, unit, qkv_full = qkv_forward(
        place, tokens, vecs, (qkv_weight, other_qkv), qkv_pieces
    )
    even = shift_all(rest, 2, 2)
    even, qkv, unit, qkv_full = barrier(even, qkv, unit, qkv_full)

    along = jnp.concatenate(
        [(even, odd)[hop % 2][(hop - 1) // 2] for hop in range(1, chips)], axis=0
    )
    along, qkv = barrier(along, qkv)
    sides = swap_sides(along)
    others = [core_swap(weight) for weight in owns]
    forward = [attend_forward(table, qkv, seq_len, 0)]
    forward, now, others = barrier(forward, qkv, others)
    forward.append(attend_forward(table, now, seq_len, 1))
    sides, forward, now, along = barrier(sides, forward, now, along)
    halves = swap_diagonal(*sides)
    swapped = [core_swap(part) for part in (along, *sides)]
    forward.append(attend_forward(table, now, seq_len, 2))
    halves, swapped, forward = barrier(halves, swapped, forward)
    diagonal = jnp.concatenate(halves, axis=1)
    rest_pieces = ((along, *sides, diagonal), (*swapped, core_swap(diagonal)))
    mixed = [result[0] for result in forward]

    output, grad_middle, grad_mixed, mine, theirs = middle_all(
        place, tokens, mixed, cotangent, vecs, ebias, owns, others, rest_pieces
    )

    def back(group, grads):
        return attend_backward(table, qkv, grads, *forward[group], seq_len, group)

    middle_sum = Sum(place, mine, theirs)
    moving = middle_sum.send()
    backward = [back(0, grad_mixed)]
    moving, backward, grad_mixed = barrier(moving, backward, grad_mixed)
    middle_sum.add_first(moving)
    middle_sum.sends, grad_mixed = barrier(middle_sum.sends, grad_mixed)
    moving = middle_sum.send()
    backward.append(back(1, grad_mixed))
    backward, grad_mixed = barrier(backward, grad_mixed)
    backward.append(back(2, grad_mixed))
    moving, backward, unit = barrier(moving, backward, unit)
    middle_sum.add_second(moving)
    middle_sum.sends, unit = barrier(middle_sum.sends, unit)
    moving = middle_sum.send()
    mine, theirs = qkv_weight_grad(place, unit, vecs, qkv_full, (0, 1, 2), backward)
    moving, mine, theirs = barrier(moving, mine, theirs)
    middle_sum.add_third(moving)
    middle_sum.sends, theirs, tokens = barrier(middle_sum.sends, theirs, tokens)
    qkv_sum = Sum(place, mine, theirs)
    moving = middle_sum.send()
    qkv_moving = qkv_sum.send()
    half = seq_len
    input_grad = input_backward(tokens, grad_middle, vecs, qkv_full, backward, 0, half)
    qkv_moving, input_grad, tokens = barrier(qkv_moving, input_grad, tokens)
    qkv_sum.add_first(qkv_moving)
    qkv_sum.sends, tokens = barrier(qkv_sum.sends, tokens)
    qkv_moving = qkv_sum.send()
    input_grad = input_backward(
        tokens, grad_middle, vecs, qkv_full, backward, half, half, input_grad
    )
    qkv_moving, input_grad = barrier(qkv_moving, input_grad)
    qkv_sum.add_second(qkv_moving)
    qkv_moving = qkv_sum.send()
    moving, qkv_moving = barrier(moving, qkv_moving)
    qkv_sum.add_third(qkv_moving)
    qkv_moving = qkv_sum.send()
    middle_sum.add_fourth(moving)
    moving = middle_sum.send()
    qkv_sum.add_fourth(qkv_moving)
    qkv_moving = qkv_sum.send()
    sum_proj, sum_expand, sum_reduce, middle_small = middle_sum.result(
        moving,
        (False, False, True),
        (proj_weight.shape, expand_weight.shape, reduce_weight.shape),
    )
    sum_qkv, qkv_small = qkv_sum.result(qkv_moving, (False,), (qkv_weight.shape,))
    return (
        output,
        input_grad,
        qkv_small[0, :own],
        qkv_small[1, :own],
        sum_qkv,
        qkv_small[2, :own],
        qkv_small[3, :own],
        sum_proj,
        middle_small[0, :own],
        middle_small[1, :own],
        middle_small[2, :own],
        sum_expand,
        middle_small[4 : 4 + per, :own].reshape(-1),
        sum_reduce,
        middle_small[3, :own],
    )


def solution(mesh):
    rows = P(("rep", "fsdp"), None)
    vector = P("fsdp")
    matrix = P("fsdp", None)
    params_specs = (
        vector,
        vector,
        matrix,
        vector,
        vector,
        matrix,
        vector,
        vector,
        vector,
        matrix,
        vector,
        matrix,
        vector,
    )
    return jax.shard_map(
        local,
        mesh=mesh,
        in_specs=(rows, rows, rows, rows) + params_specs,
        out_specs=(rows, rows) + params_specs,
        check_vma=False,
    )
```

```python
import functools
import math

import jax
import jax.numpy as jnp
from jax import lax
from jax.experimental import pallas as pl
from jax.experimental.pallas import tpu as pltpu
from jax.sharding import PartitionSpec as P

HEADS = 12
CLIPS = 6
EPSILON = 1e-06
WINDOW = 256
FIELDS = 5
BF16 = jnp.bfloat16
F32 = jnp.float32
MEBI = 1024 * 1024
NEGATIVE = -1e30


def dot(left, right):
    return lax.dot_general(left, right, (((1,), (0,)), ((), ())), preferred_element_type=F32)


def dot_nt(left, right):
    return lax.dot_general(left, right, (((1,), (1,)), ((), ())), preferred_element_type=F32)


def dot_tn(left, right):
    return lax.dot_general(left, right, (((0,), (0,)), ((), ())), preferred_element_type=F32)


def resident(shape):
    zeros = (0,) * len(shape)
    return pl.BlockSpec(shape, lambda *_: zeros, pipeline_mode=pl.Buffered(1))


def params(limit, count=1):
    return pltpu.CompilerParams(
        vmem_limit_bytes=limit * MEBI, dimension_semantics=("arbitrary",) * count
    )


def cost(micros):
    return pl.CostEstimate(flops=int(micros * 1e4), bytes_accessed=100, transcendentals=0)


def after(value, *others):
    return lax.optimization_barrier((value, *others))[0]


def normalise(values):
    row_mean = jnp.mean(values, axis=-1, keepdims=True)
    centred = values - row_mean
    row_var = jnp.mean(centred * centred, axis=-1, keepdims=True)
    scale = lax.rsqrt(row_var + EPSILON)
    return centred * scale, scale


def norm_back(upstream, gain, xhat, scale):
    weighted = upstream * gain
    first = jnp.mean(weighted, axis=-1, keepdims=True)
    second = jnp.mean(weighted * xhat, axis=-1, keepdims=True)
    return scale * (weighted - first - xhat * second)


def core_swap(value):
    count = lax.axis_size("fsdp")
    return lax.ppermute(value, "fsdp", [(i, i ^ 1) for i in range(count)])


def chip_shift(value, hops):
    count = lax.axis_size("fsdp")
    return lax.ppermute(value, "fsdp", [(i, (i + 2 * hops) % count) for i in range(count)])


def replica_swap(value, bits):
    return lax.ppermute(value, "rep", [(i, i ^ bits) for i in range(4)])


def place_table():
    shard = lax.axis_index("fsdp")
    replica = lax.axis_index("rep")
    return jnp.stack([shard // 2, shard % 2, replica // 2, replica % 2]).astype(jnp.int32)


def barrier(*values):
    return lax.optimization_barrier(values)


def shift_all(piece, first=1, step=1):
    chips = lax.axis_size("fsdp") // 2
    return [chip_shift(piece, hop) for hop in range(first, chips, step)]


def swap_sides(along):
    return replica_swap(along, 1), replica_swap(along, 2)


def swap_diagonal(from_x, from_y):
    cut = from_x.shape[1] // 256 * 128
    return replica_swap(from_x[:, :cut], 2), replica_swap(from_y[:, cut:], 1)


def fetch_copies(place, targets, owns, pieces, chips, sems):
    chip, core, row_bit, col_bit = (place[i] for i in range(4))
    made = []

    def add(number, source, target):
        made.append((number, pltpu.make_async_copy(source, target, sems.at[len(made)])))

    for other in range(2):
        side = core ^ other
        height = pieces[other][0].shape[0] // (chips - 1)
        step = math.gcd(height, 16)
        for number, (target, stacked, column) in enumerate(targets):
            rows, width = target.shape[0] // (2 * chips), target.shape[1]
            start = pl.multiple_of((2 * chip + side) * rows, step)
            add(number, owns[other][number], target.at[pl.ds(start, rows), :])
            for hop in range(1, chips):
                shard = 2 * lax.rem(chip - hop + chips, chips) + side
                source_rows = pl.ds((hop - 1) * height, height)
                for flip in range(4):
                    across = row_bit ^ (flip // 2)
                    aside = col_bit ^ (flip % 2)
                    origin = pieces[other][flip]
                    if stacked:
                        for half in range(rows // (4 * height)):
                            row = shard * rows + (across * 2 + aside) * (rows // 4) + half * height
                            add(
                                number,
                                origin.at[source_rows, pl.ds(column + half * width, width)],
                                target.at[pl.ds(pl.multiple_of(row, step), height), :],
                            )
                    else:
                        row = pl.multiple_of(shard * rows + across * height, step)
                        col = pl.multiple_of(aside * (width // 2), 128)
                        add(
                            number,
                            origin.at[source_rows, pl.ds(column, width // 2)],
                            target.at[pl.ds(row, height), pl.ds(col, width // 2)],
                        )
    return made


def spread_copies(place, targets, small, blank, mine, theirs, chips, sems):
    core = place[1]
    made = []
    height = mine.shape[0] // (4 * chips)
    step = math.gcd(height, 16)
    for other, packed in ((1, theirs), (0, mine)):
        side = core ^ other
        for chip in range(chips):
            shard = 2 * chip + side
            for quarter in range(4):
                out_rows = pl.ds((chip * 4 + quarter) * height, height)
                moves = []
                column = 0
                for number, (target, stacked) in enumerate(targets):
                    rows = target.shape[0] // (2 * chips)
                    if stacked:
                        width = target.shape[1]
                        for half in range(rows // (4 * height)):
                            row = shard * rows + quarter * (rows // 4) + half * height
                            row = pl.multiple_of(row, step)
                            moves.append((number, target.at[pl.ds(row, height), :], column, width))
                            column += width
                    else:
                        width = target.shape[1] // 2
                        row = pl.multiple_of(shard * rows + (quarter // 2) * height, step)
                        cols = pl.ds((quarter % 2) * width, width)
                        moves.append((number, target.at[pl.ds(row, height), cols], column, width))
                        column += width
                if quarter == 0:
                    moves.append((len(targets), small.at[shard], column, 128))
                else:
                    moves.append((len(targets), blank.at[...], column, 128))
                for number, source, column, width in moves:
                    target = packed.at[out_rows, pl.ds(column, width)]
                    made.append(
                        (number, pltpu.make_async_copy(source, target, sems.at[len(made)]))
                    )
    return made


def run_copies(made):
    for _, copy in made:
        copy.start()
    for _, copy in made:
        copy.wait()


def add16(left, right):
    return left.astype(F32) + right.astype(F32)


def first_sum(height, place, mine, other, keep_a, send_a, keep_b, send_b):
    row_bit, col_bit = place[2], place[3]
    cut = keep_a.shape[1]
    step = math.gcd(height, 16)

    def piece(quarter, cols):
        rows = pl.ds(pl.multiple_of(quarter * height, step), height)
        return add16(mine[rows, cols], other[rows, cols]).astype(BF16)

    for bit in range(2):
        out = pl.ds(bit * height, height)
        keep_a[out, :] = piece(bit * 2 + col_bit, pl.ds(0, cut))
        send_a[out, :] = piece(bit * 2 + 1 - col_bit, pl.ds(0, cut))
        keep_b[out, :] = piece(row_bit * 2 + bit, pl.ds(cut, mine.shape[1] - cut))
        send_b[out, :] = piece((1 - row_bit) * 2 + bit, pl.ds(cut, mine.shape[1] - cut))


def second_sum(height, place, keep_a, got_a, keep_b, got_b, next_a, send_a, next_b, send_b):
    step = math.gcd(height, 16)
    for bit, keep, got, stay, send in (
        (place[2], keep_a, got_a, next_a, send_a),
        (place[3], keep_b, got_b, next_b, send_b),
    ):
        for which, out in ((bit, stay), (1 - bit, send)):
            rows = pl.ds(pl.multiple_of(which * height, step), height)
            out[...] = add16(keep[rows, :], got[rows, :]).astype(BF16)


def third_sum(height, place, keep_a, got_a, keep_b, got_b, own, *sends):
    chips = len(sends) + 1
    cut = keep_a.shape[1]
    step = math.gcd(height, 16)
    for hop, out in enumerate((own, *sends)):
        at = lax.rem(place[0] + hop, chips)
        rows = pl.ds(pl.multiple_of(at * height, step), height)
        out[:, :cut] = add16(keep_a[rows, :], got_a[rows, :]).astype(out.dtype)
        out[:, cut:] = add16(keep_b[rows, :], got_b[rows, :]).astype(out.dtype)


def fourth_sum(own, *refs):
    total = own[...]
    for ref in refs[:-1]:
        total = total + ref[...].astype(F32)
    refs[-1][...] = total.astype(BF16)


def last_spread(stacks, place, own, from_x, from_y, from_xy, *outs):
    replica = place[2] * 2 + place[3]
    height, packed = own.shape
    step = math.gcd(height, 16)
    for flip, source in enumerate((own, from_x, from_y, from_xy)):
        across = place[2] ^ (flip // 2)
        aside = place[3] ^ (flip % 2)
        column = 0
        for stacked, out in zip(stacks, outs):
            rows, width = out.shape
            if stacked:
                for half in range(rows // (4 * height)):
                    at = (across * 2 + aside) * (rows // 4) + half * height
                    out[pl.ds(pl.multiple_of(at, step), height), :] = source[
                        :, column : column + width
                    ].astype(F32)
                    column += width
            else:
                width = width // 2
                at = pl.ds(pl.multiple_of(across * height, step), height)
                cols = pl.ds(pl.multiple_of(aside * width, 128), width)
                out[at, cols] = source[:, column : column + width].astype(F32)
                column += width

        @pl.when((replica ^ flip) == 0)
        def _():
            outs[-1][...] = source[0:16, packed - 128 :].astype(F32)


def small_call(body, place, inputs, shapes, grid=None, in_specs=None, out_specs=None):
    if grid is None:
        grid = (1,)
        in_specs = [pl.BlockSpec(value.shape, lambda i, t: (0, 0)) for value in inputs]
        out_specs = [pl.BlockSpec(shape.shape, lambda i, t: (0, 0)) for shape in shapes]
    return pl.pallas_call(
        body,
        grid_spec=pltpu.PrefetchScalarGridSpec(
            num_scalar_prefetch=1, grid=grid, in_specs=in_specs, out_specs=out_specs
        ),
        out_shape=shapes,
        compiler_params=params(32),
    )(place, *inputs)


class Sum:
    def __init__(self, place, mine, theirs):
        self.place = place
        self.chips = lax.axis_size("fsdp") // 2
        self.height = mine.shape[0] // (4 * self.chips)
        self.packed = mine.shape[1]
        self.cut = self.packed // 256 * 128
        self.kept = [mine]
        self.sends = [theirs]
        self.ways = [core_swap]

    def send(self):
        return [way(value) for way, value in zip(self.ways, self.sends)]

    def shape(self, rows, cols, dtype=BF16):
        return jax.ShapeDtypeStruct((rows * self.height, cols), dtype)

    def block(self, count, cols):
        return pl.BlockSpec((count * self.height, cols), lambda i, t: (i, 0))

    def pair(self, make, rows):
        return [make(rows, self.cut)] * 2 + [make(rows, self.packed - self.cut)] * 2

    def add_first(self, arrived):
        keep_a, send_a, keep_b, send_b = small_call(
            functools.partial(first_sum, self.height),
            self.place,
            (*self.kept, *arrived),
            self.pair(self.shape, 2 * self.chips),
            (self.chips,),
            [self.block(4, self.packed)] * 2,
            self.pair(self.block, 2),
        )
        self.kept = [keep_a, keep_b]
        self.sends = [send_a, send_b]
        self.ways = [lambda v: replica_swap(v, 1), lambda v: replica_swap(v, 2)]

    def add_second(self, arrived):
        keep_a, send_a, keep_b, send_b = small_call(
            functools.partial(second_sum, self.height),
            self.place,
            (self.kept[0], arrived[0], self.kept[1], arrived[1]),
            self.pair(self.shape, self.chips),
            (self.chips,),
            self.pair(self.block, 2),
            self.pair(self.block, 1),
        )
        self.kept = [keep_a, keep_b]
        self.sends = [send_a, send_b]
        self.ways = [lambda v: replica_swap(v, 2), lambda v: replica_swap(v, 1)]

    def add_third(self, arrived):
        own, *self.sends = small_call(
            functools.partial(third_sum, self.height),
            self.place,
            (self.kept[0], arrived[0], self.kept[1], arrived[1]),
            [self.shape(1, self.packed, F32)] + [self.shape(1, self.packed)] * (self.chips - 1),
        )
        self.kept = [own]
        self.ways = [functools.partial(chip_shift, hops=hop) for hop in range(1, self.chips)]

    def add_fourth(self, arrived):
        (total,) = small_call(
            lambda table, *refs: fourth_sum(*refs),
            self.place,
            (*self.kept, *arrived),
            [self.shape(1, self.packed)],
        )
        self.kept = [total]
        self.sends = [total] * 3
        self.ways = [functools.partial(replica_swap, bits=bits) for bits in (1, 2, 3)]

    def result(self, arrived, stacks, out_shapes):
        return small_call(
            functools.partial(last_spread, stacks),
            self.place,
            (*self.kept, *arrived),
            [jax.ShapeDtypeStruct(s, F32) for s in out_shapes]
            + [jax.ShapeDtypeStruct((16, 128), F32)],
        )


def small_blocks(rows_of_shard, small, shards, own):
    small[...] = jnp.zeros_like(small)
    for shard in range(shards):
        rows = rows_of_shard(shard)
        small[shard, 0 : rows.shape[0], 0:own] = rows.astype(BF16)


def qkv_kernel(chips, place, tokens, vecs, *refs):
    owns = (refs[0:1], refs[1:2])
    pieces = (refs[2:6], refs[6:10])
    qkv, unit, weight, sems = refs[10:]
    width = tokens.shape[1]

    @pl.when(pl.program_id(0) == 0)
    def _():
        run_copies(fetch_copies(place, [(weight, False, 0)], owns, pieces, chips, sems))

    xhat, _ = normalise(tokens[...].astype(F32))
    unit[...] = xhat.astype(BF16)
    rows = (xhat * vecs[0:1, :] + vecs[1:2, :]).astype(BF16)
    query = dot(rows, weight[:, :width]) + vecs[2:3, :]
    qkv[:, :width] = query.astype(BF16) * jnp.asarray(0.125, BF16)
    qkv[:, width : 2 * width] = dot(rows, weight[:, width : 2 * width]).astype(BF16)
    value = dot(rows, weight[:, 2 * width :]) + vecs[3:4, :]
    qkv[:, 2 * width :] = value.astype(BF16)


def hbm():
    return pl.BlockSpec(memory_space=pl.ANY)


def qkv_forward(place, tokens, vecs, owns, pieces, block=512):
    rows, width = tokens.shape
    chips = lax.axis_size("fsdp") // 2
    sources = [*owns, *pieces[0], *pieces[1]]
    zero = lambda i, t: (0, 0)
    return pl.pallas_call(
        functools.partial(qkv_kernel, chips),
        grid_spec=pltpu.PrefetchScalarGridSpec(
            num_scalar_prefetch=1,
            grid=(rows // block,),
            in_specs=[
                pl.BlockSpec((block, width), lambda i, t: (i, 0)),
                pl.BlockSpec(vecs.shape, zero),
            ]
            + [hbm()] * len(sources),
            out_specs=[
                pl.BlockSpec((block, 3 * width), lambda i, t: (i, 0)),
                pl.BlockSpec((block, width), lambda i, t: (i, 0)),
                resident((width, 3 * width)),
            ],
            scratch_shapes=[pltpu.SemaphoreType.DMA((2 + 8 * (chips - 1),))],
        ),
        out_shape=[
            jax.ShapeDtypeStruct((rows, 3 * width), BF16),
            jax.ShapeDtypeStruct((rows, width), BF16),
            jax.ShapeDtypeStruct((width, 3 * width), BF16),
        ],
        compiler_params=params(60),
        cost_estimate=cost(12),
    )(place, tokens, vecs, *sources)


def clip_table(segment_ids, valid_mask):
    seq_len = segment_ids.shape[1]
    clips = jnp.arange(CLIPS, dtype=jnp.int32)[None, :, None]
    segments = segment_ids[:, None, :]
    start = jnp.sum((segments < clips).astype(jnp.int32), axis=2)
    end = jnp.sum((segments <= clips).astype(jnp.int32), axis=2)
    valid = jnp.sum(((segments == clips) & (valid_mask[:, None, :] == 1)).astype(jnp.int32), axis=2)
    aligned = start // 16 * 16
    need = end - aligned
    path = (need > WINDOW).astype(jnp.int32) + (need > 2 * WINDOW).astype(jnp.int32)
    window = jnp.where(path == 0, WINDOW, jnp.where(path == 1, 2 * WINDOW, seq_len))
    base = jnp.minimum(aligned, seq_len - window)
    return jnp.stack([base, path, start - base, end - base, start + valid - base], axis=2).reshape(
        -1
    )


def lane_low(rows):
    return lax.broadcasted_iota(jnp.int32, (rows, 128), 1) < 64


def flag_lane(rows):
    return lax.broadcasted_iota(jnp.int32, (rows, 128), 1) % 64 == 0


def row_mask(rows, offset, first, last):
    index = lax.broadcasted_iota(jnp.int32, (rows, 128), 0) + offset
    return (index >= first) & (index < last)


def key_extra(rows, first, last):
    bias = jnp.where(row_mask(rows, 0, first, last), 0.0, NEGATIVE)
    return jnp.where(flag_lane(rows), bias, 0.0).astype(BF16)


def query_extra(rows):
    return jnp.where(flag_lane(rows), 1.0, 0.0).astype(BF16)


def weights_of(query, keys, extra_query, extra_keys, low, low_keys, head):
    if head == 0:
        left = jnp.where(low, query, extra_query)
        right = jnp.where(low_keys, keys, extra_keys)
    else:
        left = jnp.where(low, extra_query, query)
        right = jnp.where(low_keys, extra_keys, keys)
    scores = dot_nt(left, right)
    return jnp.exp(scores - jnp.max(scores, axis=1, keepdims=True)).astype(BF16)


def attend_window(refs, base, first, last, valid_end, window, pairs, exps, clip):
    queries, keys_ref, values_ref, mixed, inverse = refs
    chunk = WINDOW
    low = lane_low(chunk)
    low_keys = lane_low(window)
    extra_keys = key_extra(window, first, valid_end)
    extra_query = query_extra(chunk)
    ones = jnp.ones((window, 128), BF16)
    key_rows = pl.ds(base, window)

    def one_chunk(offset, row_start):
        rows = pl.ds(row_start, chunk)
        keep = row_mask(chunk, offset, first, last)
        for pair in range(pairs):
            lanes = pl.ds(128 * pair, 128)
            query = queries[rows, lanes]
            keys = keys_ref[key_rows, lanes]
            stack = jnp.concatenate([values_ref[key_rows, lanes], ones], axis=1)
            sums = []
            for head in range(2):
                weights = weights_of(query, keys, extra_query, extra_keys, low, low_keys, head)
                if exps is not None:
                    exps[0, 2 * pair + head, pl.ds(clip * WINDOW, WINDOW), :] = weights
                sums.append(dot(weights, stack))
            total = jnp.where(low, sums[0][:, 128:], sums[1][:, 128:])
            weighted = jnp.where(low, sums[0][:, :128], sums[1][:, :128])
            reciprocal = 1.0 / total
            mixed[rows, lanes] = jnp.where(
                keep, (weighted * reciprocal), mixed[rows, lanes].astype(F32)
            ).astype(BF16)
            inverse[rows, lanes] = jnp.where(keep, reciprocal, inverse[rows, lanes])

    if window == chunk:
        one_chunk(0, base)
    else:

        def step(index, carry):
            offset = index * chunk
            one_chunk(offset, pl.multiple_of(base + offset, 16))
            return carry

        lax.fori_loop(0, window // chunk, step, 0)


def clip_fields(table, sequence, clip):
    at = (sequence * CLIPS + clip) * FIELDS
    base = pl.multiple_of(table[at], 16)
    return base, table[at + 1], table[at + 2], table[at + 3], table[at + 4]


def attend_kernel(pairs, table, queries, keys, values, mixed, inverse, exps):
    sequence = pl.program_id(0)
    seq_len = queries.shape[0]
    mixed[...] = jnp.zeros_like(mixed)
    inverse[...] = jnp.zeros_like(inverse)
    refs = (queries, keys, values, mixed, inverse)

    def one_clip(clip, carry):
        base, path, first, last, valid_end = clip_fields(table, sequence, clip)
        for number, window in enumerate((WINDOW, 2 * WINDOW, seq_len)):

            @pl.when(path == number)
            def _():
                attend_window(
                    refs,
                    base,
                    first,
                    last,
                    valid_end,
                    window,
                    pairs,
                    exps if number == 0 else None,
                    clip,
                )

        return carry

    lax.fori_loop(0, CLIPS, one_clip, 0)


def attend_forward(table, qkv, seq_len, group, pairs=2):
    rows = qkv.shape[0]
    width = qkv.shape[1] // 3
    seqs = rows // seq_len
    lanes = 128 * pairs
    groups = width // lanes
    block = (seq_len, lanes)
    own = pl.BlockSpec(block, lambda s, t: (s, 0))
    return pl.pallas_call(
        functools.partial(attend_kernel, pairs),
        grid_spec=pltpu.PrefetchScalarGridSpec(
            num_scalar_prefetch=1,
            grid=(seqs,),
            in_specs=[
                pl.BlockSpec(block, lambda s, t: (s, group)),
                pl.BlockSpec(block, lambda s, t: (s, groups + group)),
                pl.BlockSpec(block, lambda s, t: (s, 2 * groups + group)),
            ],
            out_specs=[
                own,
                own,
                pl.BlockSpec((1, 2 * pairs, CLIPS * WINDOW, WINDOW), lambda s, t: (s, 0, 0, 0)),
            ],
        ),
        out_shape=[
            jax.ShapeDtypeStruct((rows, lanes), BF16),
            jax.ShapeDtypeStruct((rows, lanes), F32),
            jax.ShapeDtypeStruct((seqs, 2 * pairs, CLIPS * WINDOW, WINDOW), BF16),
        ],
        compiler_params=params(60),
        cost_estimate=cost(10),
    )(table, qkv, qkv, qkv)


def back_window(refs, base, first, last, valid_end, window, pairs, exps, clip, gather):
    queries, keys_ref, values_ref, grads, mixed, inverse, dq, dk, dv = refs
    key_grad, value_grad = gather
    chunk = WINDOW
    single = window == chunk
    low = lane_low(chunk)
    low_keys = lane_low(window)
    extra_keys = None if single else key_extra(window, first, valid_end)
    extra_query = None if single else query_extra(chunk)
    key_rows = pl.ds(base, window)
    one = jnp.ones((window, 128), BF16)

    def one_chunk(offset, row_start):
        rows = pl.ds(row_start, chunk)
        keep = row_mask(chunk, offset, first, last)
        for pair in range(pairs):
            lanes = pl.ds(128 * pair, 128)
            query = queries[rows, lanes]
            keys = keys_ref[key_rows, lanes]
            values = values_ref[key_rows, lanes]
            scaled = jnp.where(keep, grads[rows, lanes].astype(F32) * inverse[rows, lanes], 0.0)
            product = scaled * mixed[rows, lanes].astype(F32)
            turned = pltpu.roll(-product, 64, 1).astype(BF16)
            scaled = scaled.astype(BF16)
            parts = []
            for head in range(2):
                if head == 0:
                    left = jnp.where(low, scaled, turned)
                    right = jnp.where(low_keys, values, one)
                else:
                    left = jnp.where(low, turned, scaled)
                    right = jnp.where(low_keys, one, values)
                if single:
                    weights = exps[0, 2 * pair + head, pl.ds(clip * WINDOW, WINDOW), :]
                else:
                    weights = weights_of(query, keys, extra_query, extra_keys, low, low_keys, head)
                grad_scores = (weights.astype(F32) * dot_nt(left, right)).astype(BF16)
                parts.append(
                    (
                        dot(grad_scores, keys),
                        dot_tn(grad_scores, query),
                        dot_tn(weights, scaled),
                    )
                )
            query_part = jnp.where(low, parts[0][0], parts[1][0]) * 0.125
            key_part = jnp.where(low_keys, parts[0][1], parts[1][1])
            value_part = jnp.where(low_keys, parts[0][2], parts[1][2])
            dq[rows, lanes] = jnp.where(keep, query_part, dq[rows, lanes].astype(F32)).astype(BF16)
            if single:
                dk[rows, lanes] = jnp.where(keep, key_part, dk[rows, lanes].astype(F32)).astype(
                    BF16
                )
                dv[rows, lanes] = jnp.where(keep, value_part, dv[rows, lanes].astype(F32)).astype(
                    BF16
                )
            else:
                key_grad[pl.ds(0, window), lanes] += key_part
                value_grad[pl.ds(0, window), lanes] += value_part

    if single:
        one_chunk(0, base)
        return
    key_grad[...] = jnp.zeros_like(key_grad)
    value_grad[...] = jnp.zeros_like(value_grad)

    def step(index, carry):
        offset = index * chunk
        one_chunk(offset, pl.multiple_of(base + offset, 16))
        return carry

    lax.fori_loop(0, window // chunk, step, 0)
    keep = row_mask(window, 0, first, last)
    for pair in range(pairs):
        lanes = pl.ds(128 * pair, 128)
        for ref, total in ((dk, key_grad), (dv, value_grad)):
            ref[key_rows, lanes] = jnp.where(
                keep, total[pl.ds(0, window), lanes], ref[key_rows, lanes].astype(F32)
            ).astype(BF16)


def back_kernel(
    pairs,
    table,
    queries,
    keys,
    values,
    grads,
    mixed,
    inverse,
    exps,
    dq,
    dk,
    dv,
    key_grad,
    value_grad,
):
    sequence = pl.program_id(0)
    seq_len = queries.shape[0]
    for ref in (dq, dk, dv):
        ref[...] = jnp.zeros_like(ref)
    refs = (queries, keys, values, grads, mixed, inverse, dq, dk, dv)

    def one_clip(clip, carry):
        base, path, first, last, valid_end = clip_fields(table, sequence, clip)
        for number, window in enumerate((WINDOW, 2 * WINDOW, seq_len)):

            @pl.when(path == number)
            def _():
                back_window(
                    refs,
                    base,
                    first,
                    last,
                    valid_end,
                    window,
                    pairs,
                    exps,
                    clip,
                    (key_grad, value_grad),
                )

        return carry

    lax.fori_loop(0, CLIPS, one_clip, 0)


def attend_backward(table, qkv, grads, mixed, inverse, exps, seq_len, group, pairs=2):
    rows = mixed.shape[0]
    seqs = rows // seq_len
    lanes = 128 * pairs
    groups = grads.shape[1] // lanes
    block = (seq_len, lanes)
    own = pl.BlockSpec(block, lambda s, t: (s, 0))
    shape = jax.ShapeDtypeStruct((rows, lanes), BF16)
    return pl.pallas_call(
        functools.partial(back_kernel, pairs),
        grid_spec=pltpu.PrefetchScalarGridSpec(
            num_scalar_prefetch=1,
            grid=(seqs,),
            in_specs=[
                pl.BlockSpec(block, lambda s, t: (s, group)),
                pl.BlockSpec(block, lambda s, t: (s, groups + group)),
                pl.BlockSpec(block, lambda s, t: (s, 2 * groups + group)),
                pl.BlockSpec(block, lambda s, t: (s, group)),
                own,
                own,
                pl.BlockSpec((1, 2 * pairs, CLIPS * WINDOW, WINDOW), lambda s, t: (s, 0, 0, 0)),
            ],
            out_specs=[own, own, own],
            scratch_shapes=[pltpu.VMEM(block, F32), pltpu.VMEM(block, F32)],
        ),
        out_shape=[shape, shape, shape],
        compiler_params=params(60),
        cost_estimate=cost(19),
    )(table, qkv, qkv, qkv, grads, mixed, inverse, exps)


def gauss(value):
    cdf = 0.5 + 0.5 * lax.erf(value * 0.7071067811865476)
    tail = jnp.exp2(value * value * (-0.5 * 1.4426950408889634))
    return cdf, value * tail * 0.3989422804014327


def middle_kernel(
    part,
    chips,
    groups,
    place,
    tokens,
    cotangent,
    vecs,
    ebias,
    *refs,
):
    mixed, refs = refs[:groups], refs[groups:]
    owns = (refs[0:3], refs[3:6])
    pieces = (refs[6:10], refs[10:14])
    (
        output,
        grad_middle,
        grad_mixed,
        mine,
        theirs,
        proj,
        expand,
        reduce,
        sum_proj,
        sum_expand,
        sum_reduce,
        sum_ebias,
        sum_vecs,
        middle,
        units,
        scales,
        normed,
        grad_normed,
        activated,
        grad_hidden,
        small,
        blank,
        in_sems,
        out_sems,
    ) = refs[14:]
    step = pl.program_id(0)
    width, hidden = expand.shape
    block = tokens.shape[0]
    half = block // 2
    own = width // (2 * chips)
    targets = [
        (proj, False, 0),
        (expand, False, width // 2),
        (reduce, True, width // 2 + hidden // 2),
    ]

    @pl.when(step == 0)
    def _():
        made = fetch_copies(place, targets, owns, pieces, chips, in_sems)
        for _, copy in made:
            copy.start()
        sum_proj[...] = jnp.zeros_like(sum_proj)
        sum_expand[...] = jnp.zeros_like(sum_expand)
        sum_reduce[...] = jnp.zeros_like(sum_reduce)
        sum_ebias[...] = jnp.zeros_like(sum_ebias)
        sum_vecs[...] = jnp.zeros_like(sum_vecs)
        for _, copy in made:
            copy.wait()

    def norm_rows(first, count):
        rows = slice(first, first + count)
        xhat, scale = normalise(middle[rows, :])
        units[rows, :] = xhat
        scales[rows, :] = scale
        normed[rows, :] = (xhat * vecs[5:6, :] + vecs[6:7, :]).astype(BF16)

    def hidden_part(which, start):
        rows = slice(which * half, (which + 1) * half)
        cols = pl.ds(start, part)
        into = expand[:, cols]
        back = reduce[cols, :]
        preact = dot(normed[rows, :], into) + ebias[:, cols]
        cdf, slope = gauss(preact)
        active = (preact * cdf).astype(BF16)
        activated[rows, cols] = active
        grad_preact = (dot_nt(cotangent[rows, :], back) * (cdf + slope)).astype(BF16)
        grad_hidden[rows, cols] = grad_preact
        sum_ebias[:, cols] += jnp.sum(grad_preact.astype(F32), axis=0, keepdims=True)
        middle[rows, :] += dot(active, back)
        term = dot_nt(grad_preact, into)
        if start == 0:
            grad_normed[rows, :] = term
        else:
            grad_normed[rows, :] += term

    def end_rows(first, count):
        rows = slice(first, first + count)
        upstream = grad_normed[rows, :]
        xhat = units[rows, :]
        output[rows, :] = (middle[rows, :] + vecs[7:8, :]).astype(BF16)
        cot = cotangent[rows, :].astype(F32)
        grads = cot + norm_back(upstream, vecs[5:6, :], xhat, scales[rows, :])
        attended = grads.astype(BF16)
        grad_middle[rows, :] = attended
        sum_vecs[0:1, :] += jnp.sum(attended.astype(F32), axis=0, keepdims=True)
        sum_vecs[1:2, :] += jnp.sum(upstream * xhat, axis=0, keepdims=True)
        sum_vecs[2:3, :] += jnp.sum(upstream, axis=0, keepdims=True)
        sum_vecs[3:4, :] += jnp.sum(cot, axis=0, keepdims=True)

    mixed_rows = jnp.concatenate([ref[...] for ref in mixed], axis=1)
    middle[...] = tokens[...].astype(F32) + dot(mixed_rows, proj[...]) + vecs[4:5, :]
    parts = hidden // part
    piece = half // parts
    norm_rows(0, half)
    for index in range(parts):
        hidden_part(0, index * part)
        norm_rows(half + index * piece, piece)
    normed_t = normed[...].T
    for index in range(parts):
        hidden_part(1, index * part)
        cols = pl.ds(index * part, part)
        sum_reduce[cols, :] += dot_tn(activated[:, cols], cotangent[...])
        sum_expand[:, cols] += dot(normed_t, grad_hidden[:, cols])
        end_rows(index * piece, piece)
    end_rows(half, half)
    attended = grad_middle[...]
    grad_mixed[...] = dot_nt(attended, proj[...]).astype(BF16)
    sum_proj[...] += dot_tn(mixed_rows, attended)

    @pl.when(step == pl.num_programs(0) - 1)
    def _():
        blank[...] = jnp.zeros_like(blank)
        per = hidden // width

        def rows_of_shard(shard):
            rows = [sum_vecs[0:4, shard * own : (shard + 1) * own]]
            for index in range(per):
                at = (shard * per + index) * own
                rows.append(sum_ebias[0:1, at : at + own])
            return jnp.concatenate(rows, axis=0)

        small_blocks(rows_of_shard, small, 2 * chips, own)
        made = spread_copies(
            place,
            [(proj, False), (expand, False), (reduce, True)],
            small,
            blank,
            mine,
            theirs,
            chips,
            out_sems,
        )
        for number, (low, total) in enumerate(
            ((proj, sum_proj), (expand, sum_expand), (reduce, sum_reduce))
        ):
            low[...] = total[...].astype(BF16)
            for which, copy in made:
                if which == number or (which == 3 and number == 0):
                    copy.start()
        for _, copy in made:
            copy.wait()


def middle_all(
    place, tokens, mixed, cotangent, vecs, ebias, owns, others, pieces, block=512, part=768
):
    rows, width = tokens.shape
    chips = lax.axis_size("fsdp") // 2
    hidden = ebias.shape[1]
    height = width // (4 * chips)
    row_block = pl.BlockSpec((block, width), lambda i, t: (i, 0))
    row_shape = jax.ShapeDtypeStruct((rows, width), BF16)
    packed = (4 * chips * height, width // 2 + hidden // 2 + hidden // 2 + 128)
    packed_shape = jax.ShapeDtypeStruct(packed, BF16)
    sources = [*owns, *others, *pieces[0], *pieces[1]]
    halves = hidden // width // 2
    mixed_block = pl.BlockSpec((block, mixed[0].shape[1]), lambda i, t: (i, 0))
    return pl.pallas_call(
        functools.partial(middle_kernel, part, chips, len(mixed)),
        grid_spec=pltpu.PrefetchScalarGridSpec(
            num_scalar_prefetch=1,
            grid=(rows // block,),
            in_specs=[row_block] * 2
            + [
                pl.BlockSpec(vecs.shape, lambda i, t: (0, 0)),
                pl.BlockSpec(ebias.shape, lambda i, t: (0, 0)),
            ]
            + [mixed_block] * len(mixed)
            + [hbm()] * len(sources),
            out_specs=[row_block] * 3 + [hbm(), hbm()],
            scratch_shapes=[
                pltpu.VMEM((width, width), BF16),
                pltpu.VMEM((width, hidden), BF16),
                pltpu.VMEM((hidden, width), BF16),
                pltpu.VMEM((width, width), F32),
                pltpu.VMEM((width, hidden), F32),
                pltpu.VMEM((hidden, width), F32),
                pltpu.VMEM((1, hidden), F32),
                pltpu.VMEM((8, width), F32),
                pltpu.VMEM((block, width), F32),
                pltpu.VMEM((block, width), F32),
                pltpu.VMEM((block, 1), F32),
                pltpu.VMEM((block, width), BF16),
                pltpu.VMEM((block, width), F32),
                pltpu.VMEM((block, hidden), BF16),
                pltpu.VMEM((block, hidden), BF16),
                pltpu.VMEM((2 * chips, height, 128), BF16),
                pltpu.VMEM((height, 128), BF16),
                pltpu.SemaphoreType.DMA((2 * (3 + 4 * (chips - 1) * (2 + halves)),)),
                pltpu.SemaphoreType.DMA((8 * chips * (3 + halves),)),
            ],
        ),
        out_shape=[row_shape, row_shape, row_shape, packed_shape, packed_shape],
        compiler_params=params(63),
        cost_estimate=cost(110),
    )(place, tokens, cotangent, vecs, ebias, *mixed, *sources)


def weight_kernel(chips, offsets, place, unit, vecs, weight, *refs):
    count = len(offsets)
    parts, refs = refs[:count], refs[count:]
    mine, theirs, total, sums, low, small, blank, sems = refs
    step = pl.program_id(0)
    width = unit.shape[1]
    lanes = parts[0].shape[1]
    own = width // (2 * chips)

    @pl.when(step == 0)
    def _():
        total[...] = jnp.zeros_like(total)
        sums[...] = jnp.zeros_like(sums)

    rows_t = unit[...].T
    for index, part in enumerate(parts):
        cols = slice(index * lanes, (index + 1) * lanes)
        total[:, cols] += dot(rows_t, part[...])
        sums[0:1, cols] += jnp.sum(part[...].astype(F32), axis=0, keepdims=True)

    @pl.when(step == pl.num_programs(0) - 1)
    def _():
        columns = vecs[...].T
        gain, shift = columns[:, 0:1], columns[:, 1:2]
        gain_part = jnp.zeros((width, 1), F32)
        shift_part = jnp.zeros((width, 1), F32)
        empty = jnp.zeros((1, lanes), F32)
        biases = [[empty] * (width // lanes) for _ in range(3)]
        for index, offset in enumerate(offsets):
            cols = slice(index * lanes, (index + 1) * lanes)
            raw = total[:, cols]
            sides = weight[:, offset : offset + lanes].astype(F32)
            line = sums[0:1, cols]
            gain_part += jnp.sum(raw * sides, axis=1, keepdims=True)
            shift_part += jnp.sum(line * sides, axis=1, keepdims=True)
            low[:, cols] = (gain * raw + shift * line).astype(BF16)
            biases[offset // width][offset % width // lanes] = line
        pick = lax.broadcasted_iota(jnp.int32, (width, 128), 1)
        both = jnp.where(pick == 0, gain_part, jnp.where(pick == 1, shift_part, 0.0)).T
        query_line = jnp.concatenate(biases[0], axis=1)
        value_line = jnp.concatenate(biases[2], axis=1)
        blank[...] = jnp.zeros_like(blank)

        def rows_of_shard(shard):
            cols = slice(shard * own, (shard + 1) * own)
            return jnp.concatenate([both[0:2, cols], query_line[:, cols], value_line[:, cols]], axis=0)

        small_blocks(rows_of_shard, small, 2 * chips, own)
        run_copies(
            spread_copies(place, [(low, False)], small, blank, mine, theirs, chips, sems)
        )


def qkv_weight_grad(place, unit, vecs, weight, groups, grads, block=512):
    rows, width = unit.shape
    lanes = grads[0][0].shape[1]
    chips = lax.axis_size("fsdp") // 2
    height = width // (4 * chips)
    offsets = tuple(part * width + group * lanes for part in range(3) for group in groups)
    parts = [grad[part] for part in range(3) for grad in grads]
    columns = lanes * len(parts)
    packed = jax.ShapeDtypeStruct((4 * chips * height, columns // 2 + 128), BF16)
    zero = lambda i, t: (0, 0)
    return pl.pallas_call(
        functools.partial(weight_kernel, chips, offsets),
        grid_spec=pltpu.PrefetchScalarGridSpec(
            num_scalar_prefetch=1,
            grid=(rows // block,),
            in_specs=[
                pl.BlockSpec((block, width), lambda i, t: (i, 0)),
                pl.BlockSpec(vecs.shape, zero),
                resident(weight.shape),
            ]
            + [pl.BlockSpec((block, lanes), lambda i, t: (i, 0))] * len(parts),
            out_specs=[hbm(), hbm()],
            scratch_shapes=[
                pltpu.VMEM((width, columns), F32),
                pltpu.VMEM((8, columns), F32),
                pltpu.VMEM((width, columns), BF16),
                pltpu.VMEM((2 * chips, height, 128), BF16),
                pltpu.VMEM((height, 128), BF16),
                pltpu.SemaphoreType.DMA((16 * chips,)),
            ],
        ),
        out_shape=[packed, packed],
        compiler_params=params(60),
        cost_estimate=cost(4 * len(groups)),
    )(place, unit, vecs, weight, *parts)


def input_kernel(count, tokens, grad_middle, vecs, weight, *refs):
    width = tokens.shape[1]
    lanes = width // count
    input_grad = refs[-1]
    xhat, scale = normalise(tokens[...].astype(F32))
    upstream = None
    for part in range(3):
        rows = jnp.concatenate([ref[...] for ref in refs[part * count : (part + 1) * count]], axis=1)
        term = dot_nt(rows, weight[:, part * width : (part + 1) * width])
        upstream = term if upstream is None else upstream + term
    grads = norm_back(upstream, vecs[0:1, :], xhat, scale)
    input_grad[...] = (grad_middle[...].astype(F32) + grads).astype(BF16)


def input_backward(tokens, grad_middle, vecs, weight, grads, first, rows, into=None, block=512):
    width = tokens.shape[1]
    lanes = grads[0][0].shape[1]
    start = first // block
    row_block = pl.BlockSpec((block, width), lambda i: (i + start, 0))
    parts = [grad[part] for part in range(3) for grad in grads]
    inputs = [tokens, grad_middle, vecs, weight, *parts]
    specs = [row_block] * 2 + [resident(vecs.shape), resident(weight.shape)]
    specs += [pl.BlockSpec((block, lanes), lambda i: (i + start, 0))] * len(parts)
    aliases = {}
    if into is not None:
        aliases = {len(inputs): 0}
        inputs.append(into)
        specs.append(hbm())
    return pl.pallas_call(
        functools.partial(input_kernel, len(grads)),
        grid=(rows // block,),
        in_specs=specs,
        out_specs=row_block,
        out_shape=jax.ShapeDtypeStruct(tokens.shape, BF16),
        input_output_aliases=aliases,
        compiler_params=params(60),
        cost_estimate=cost(7),
    )(*inputs)


def local(
    tokens,
    segment_ids,
    valid_mask,
    cotangent,
    norm1_gain,
    norm1_bias,
    qkv_weight,
    query_bias,
    value_bias,
    proj_weight,
    proj_bias,
    norm2_gain,
    norm2_bias,
    expand_weight,
    expand_bias,
    reduce_weight,
    reduce_bias,
):
    seq_len = segment_ids.shape[1]
    own, width = proj_weight.shape
    shards = lax.axis_size("fsdp")
    chips = shards // 2
    height = own // 2
    per = expand_bias.shape[0] // own
    place = place_table()
    row_bit, col_bit = place[2], place[3]

    def tile(weight):
        half = weight.shape[1] // 2
        return lax.dynamic_slice(weight, (row_bit * height, col_bit * half), (height, half))

    small = jnp.stack(
        [
            norm1_gain,
            norm1_bias,
            query_bias,
            value_bias,
            proj_bias,
            norm2_gain,
            norm2_bias,
            reduce_bias,
            *jnp.split(expand_bias, per),
        ]
    )
    block = jnp.pad(small, ((0, height - small.shape[0]), (0, 128 - own)))
    piece = jnp.concatenate([tile(qkv_weight), block], axis=1)
    quarter = lax.dynamic_slice(
        reduce_weight,
        ((row_bit * 2 + col_bit) * (per * own // 4), 0),
        (per * own // 4, width),
    )
    parts = [tile(proj_weight), tile(expand_weight), *jnp.split(quarter, per // 2, axis=0)]
    rest = jnp.concatenate(parts, axis=1)
    table = clip_table(segment_ids, valid_mask)
    owns = (proj_weight, expand_weight, reduce_weight)

    got = shift_all(piece)
    other_qkv, small_other = core_swap(qkv_weight), core_swap(small)
    got, other_qkv, small_other, rest, table = barrier(got, other_qkv, small_other, rest, table)
    along = jnp.concatenate(got, axis=0)
    sides = swap_sides(along)
    odd = shift_all(rest, 1, 2)
    sides, along = barrier(sides, along)
    halves = swap_diagonal(*sides)
    halves, sides, along, odd, rest = barrier(halves, sides, along, odd, rest)
    here = (along, *sides, jnp.concatenate(halves, axis=1))
    qkv_pieces = barrier(here, tuple(core_swap(part) for part in here))

    chip, core = place[0], place[1]
    edge = piece.shape[1] - 128

    def blocks_of(first, along):
        rest = along.reshape(chips - 1, height, -1)[:, : small.shape[0], edge : edge + own]
        return jnp.concatenate([first[None], rest], axis=0)

    both = jnp.stack(
        [blocks_of(small, qkv_pieces[0][0]), blocks_of(small_other, qkv_pieces[1][0])], axis=1
    )
    hops = (chip - jnp.arange(chips)) % chips
    choice = (hops[:, None, None, None] == jnp.arange(chips)[None, None, :, None]) & (
        (jnp.arange(2) ^ core)[None, :, None, None] == jnp.arange(2)[None, None, None, :]
    )
    small = jnp.sum(
        jnp.where(choice[..., None, None], both[None, None].astype(F32), 0.0), axis=(2, 3)
    ).reshape(shards, small.shape[0], own)
    vecs = small[:, :8].swapaxes(0, 1).reshape(8, width)
    ebias = small[:, 8:].reshape(1, width * per)

    qkv, unit, qkv_full = qkv_forward(
        place, tokens, vecs, (qkv_weight, other_qkv), qkv_pieces
    )
    even = shift_all(rest, 2, 2)
    even, qkv, unit, qkv_full = barrier(even, qkv, unit, qkv_full)

    along = jnp.concatenate(
        [(even, odd)[hop % 2][(hop - 1) // 2] for hop in range(1, chips)], axis=0
    )
    along, qkv = barrier(along, qkv)
    sides = swap_sides(along)
    others = [core_swap(weight) for weight in owns]
    forward = [attend_forward(table, qkv, seq_len, 0)]
    forward, now, others = barrier(forward, qkv, others)
    forward.append(attend_forward(table, now, seq_len, 1))
    sides, forward, now, along = barrier(sides, forward, now, along)
    halves = swap_diagonal(*sides)
    swapped = [core_swap(part) for part in (along, *sides)]
    forward.append(attend_forward(table, now, seq_len, 2))
    halves, swapped, forward = barrier(halves, swapped, forward)
    diagonal = jnp.concatenate(halves, axis=1)
    rest_pieces = ((along, *sides, diagonal), (*swapped, core_swap(diagonal)))
    mixed = [result[0] for result in forward]

    output, grad_middle, grad_mixed, mine, theirs = middle_all(
        place, tokens, mixed, cotangent, vecs, ebias, owns, others, rest_pieces
    )

    def back(group, grads):
        return attend_backward(table, qkv, grads, *forward[group], seq_len, group)

    middle_sum = Sum(place, mine, theirs)
    moving = middle_sum.send()
    backward = [back(0, grad_mixed)]
    moving, backward, grad_mixed = barrier(moving, backward, grad_mixed)
    middle_sum.add_first(moving)
    middle_sum.sends, grad_mixed = barrier(middle_sum.sends, grad_mixed)
    moving = middle_sum.send()
    backward.append(back(1, grad_mixed))
    backward, grad_mixed = barrier(backward, grad_mixed)
    backward.append(back(2, grad_mixed))
    moving, backward, unit = barrier(moving, backward, unit)
    middle_sum.add_second(moving)
    middle_sum.sends, unit = barrier(middle_sum.sends, unit)
    moving = middle_sum.send()
    mine, theirs = qkv_weight_grad(place, unit, vecs, qkv_full, (0, 1, 2), backward)
    moving, mine, theirs = barrier(moving, mine, theirs)
    middle_sum.add_third(moving)
    middle_sum.sends, theirs, tokens = barrier(middle_sum.sends, theirs, tokens)
    qkv_sum = Sum(place, mine, theirs)
    moving = middle_sum.send()
    qkv_moving = qkv_sum.send()
    half = seq_len
    input_grad = input_backward(tokens, grad_middle, vecs, qkv_full, backward, 0, half)
    qkv_moving, input_grad, tokens = barrier(qkv_moving, input_grad, tokens)
    qkv_sum.add_first(qkv_moving)
    qkv_sum.sends, tokens = barrier(qkv_sum.sends, tokens)
    qkv_moving = qkv_sum.send()
    input_grad = input_backward(
        tokens, grad_middle, vecs, qkv_full, backward, half, half, input_grad
    )
    qkv_moving, input_grad = barrier(qkv_moving, input_grad)
    qkv_sum.add_second(qkv_moving)
    qkv_moving = qkv_sum.send()
    moving, qkv_moving = barrier(moving, qkv_moving)
    qkv_sum.add_third(qkv_moving)
    qkv_moving = qkv_sum.send()
    middle_sum.add_fourth(moving)
    moving = middle_sum.send()
    qkv_sum.add_fourth(qkv_moving)
    qkv_moving = qkv_sum.send()
    sum_proj, sum_expand, sum_reduce, middle_small = middle_sum.result(
        moving,
        (False, False, True),
        (proj_weight.shape, expand_weight.shape, reduce_weight.shape),
    )
    sum_qkv, qkv_small = qkv_sum.result(qkv_moving, (False,), (qkv_weight.shape,))
    return (
        output,
        input_grad,
        qkv_small[0, :own],
        qkv_small[1, :own],
        sum_qkv,
        qkv_small[2, :own],
        qkv_small[3, :own],
        sum_proj,
        middle_small[0, :own],
        middle_small[1, :own],
        middle_small[2, :own],
        sum_expand,
        middle_small[4 : 4 + per, :own].reshape(-1),
        sum_reduce,
        middle_small[3, :own],
    )


def solution(mesh):
    rows = P(("rep", "fsdp"), None)
    vector = P("fsdp")
    matrix = P("fsdp", None)
    params_specs = (
        vector,
        vector,
        matrix,
        vector,
        vector,
        matrix,
        vector,
        vector,
        vector,
        matrix,
        vector,
        matrix,
        vector,
    )
    return jax.shard_map(
        local,
        mesh=mesh,
        in_specs=(rows, rows, rows, rows) + params_specs,
        out_specs=(rows, rows) + params_specs,
        check_vma=False,
    )
```

```python
import functools
import math

import jax
import jax.numpy as jnp
from jax import lax
from jax.experimental import pallas as pl
from jax.experimental.pallas import tpu as pltpu
from jax.sharding import PartitionSpec as P

HEADS = 12
CLIPS = 6
EPSILON = 1e-06
WINDOW = 256
FIELDS = 5
TOGETHER = 3
BF16 = jnp.bfloat16
F32 = jnp.float32
MEBI = 1024 * 1024
NEGATIVE = -1e30


def dot(left, right):
    return lax.dot_general(left, right, (((1,), (0,)), ((), ())), preferred_element_type=F32)


def dot_nt(left, right):
    return lax.dot_general(left, right, (((1,), (1,)), ((), ())), preferred_element_type=F32)


def dot_tn(left, right):
    return lax.dot_general(left, right, (((0,), (0,)), ((), ())), preferred_element_type=F32)


def resident(shape):
    zeros = (0,) * len(shape)
    return pl.BlockSpec(shape, lambda *_: zeros, pipeline_mode=pl.Buffered(1))


def params(limit, count=1):
    return pltpu.CompilerParams(
        vmem_limit_bytes=limit * MEBI, dimension_semantics=("arbitrary",) * count
    )


def cost(micros):
    return pl.CostEstimate(flops=int(micros * 1e4), bytes_accessed=100, transcendentals=0)


def after(value, *others):
    return lax.optimization_barrier((value, *others))[0]


def normalise(values):
    row_mean = jnp.mean(values, axis=-1, keepdims=True)
    centred = values - row_mean
    row_var = jnp.mean(centred * centred, axis=-1, keepdims=True)
    scale = lax.rsqrt(row_var + EPSILON)
    return centred * scale, scale


def norm_back(upstream, gain, xhat, scale):
    weighted = upstream * gain
    first = jnp.mean(weighted, axis=-1, keepdims=True)
    second = jnp.mean(weighted * xhat, axis=-1, keepdims=True)
    return scale * (weighted - first - xhat * second)


def core_swap(value):
    count = lax.axis_size("fsdp")
    return lax.ppermute(value, "fsdp", [(i, i ^ 1) for i in range(count)])


def chip_shift(value, hops):
    count = lax.axis_size("fsdp")
    return lax.ppermute(value, "fsdp", [(i, (i + 2 * hops) % count) for i in range(count)])


def replica_swap(value, bits):
    return lax.ppermute(value, "rep", [(i, i ^ bits) for i in range(4)])


def place_table():
    shard = lax.axis_index("fsdp")
    replica = lax.axis_index("rep")
    return jnp.stack([shard // 2, shard % 2, replica // 2, replica % 2]).astype(jnp.int32)


def barrier(*values):
    return lax.optimization_barrier(values)


def shift_all(piece, first=1, step=1):
    chips = lax.axis_size("fsdp") // 2
    return [chip_shift(piece, hop) for hop in range(first, chips, step)]


def swap_sides(along):
    return replica_swap(along, 1), replica_swap(along, 2)


def swap_diagonal(from_x, from_y):
    cut = from_x.shape[1] // 256 * 128
    return replica_swap(from_x[:, :cut], 2), replica_swap(from_y[:, cut:], 1)


def fetch_copies(place, targets, owns, pieces, chips, sems):
    chip, core, row_bit, col_bit = (place[i] for i in range(4))
    made = []

    def add(number, source, target):
        made.append((number, pltpu.make_async_copy(source, target, sems.at[len(made)])))

    for other in range(2):
        side = core ^ other
        height = pieces[other][0].shape[0] // (chips - 1)
        step = math.gcd(height, 16)
        for number, (target, stacked, column) in enumerate(targets):
            rows, width = target.shape[0] // (2 * chips), target.shape[1]
            start = pl.multiple_of((2 * chip + side) * rows, step)
            add(number, owns[other][number], target.at[pl.ds(start, rows), :])
            for hop in range(1, chips):
                shard = 2 * lax.rem(chip - hop + chips, chips) + side
                source_rows = pl.ds((hop - 1) * height, height)
                for flip in range(4):
                    across = row_bit ^ (flip // 2)
                    aside = col_bit ^ (flip % 2)
                    origin = pieces[other][flip]
                    if stacked:
                        for half in range(rows // (4 * height)):
                            row = shard * rows + (across * 2 + aside) * (rows // 4) + half * height
                            add(
                                number,
                                origin.at[source_rows, pl.ds(column + half * width, width)],
                                target.at[pl.ds(pl.multiple_of(row, step), height), :],
                            )
                    else:
                        row = pl.multiple_of(shard * rows + across * height, step)
                        col = pl.multiple_of(aside * (width // 2), 128)
                        add(
                            number,
                            origin.at[source_rows, pl.ds(column, width // 2)],
                            target.at[pl.ds(row, height), pl.ds(col, width // 2)],
                        )
    return made


def spread_copies(place, targets, small, blank, mine, theirs, chips, sems):
    core = place[1]
    made = []
    height = mine.shape[0] // (4 * chips)
    step = math.gcd(height, 16)
    for other, packed in ((1, theirs), (0, mine)):
        side = core ^ other
        for chip in range(chips):
            shard = 2 * chip + side
            for quarter in range(4):
                out_rows = pl.ds((chip * 4 + quarter) * height, height)
                moves = []
                column = 0
                for number, (target, stacked) in enumerate(targets):
                    rows = target.shape[0] // (2 * chips)
                    if stacked:
                        width = target.shape[1]
                        for half in range(rows // (4 * height)):
                            row = shard * rows + quarter * (rows // 4) + half * height
                            row = pl.multiple_of(row, step)
                            moves.append((number, target.at[pl.ds(row, height), :], column, width))
                            column += width
                    else:
                        width = target.shape[1] // 2
                        row = pl.multiple_of(shard * rows + (quarter // 2) * height, step)
                        cols = pl.ds((quarter % 2) * width, width)
                        moves.append((number, target.at[pl.ds(row, height), cols], column, width))
                        column += width
                if quarter == 0:
                    moves.append((len(targets), small.at[shard], column, 128))
                else:
                    moves.append((len(targets), blank.at[...], column, 128))
                for number, source, column, width in moves:
                    target = packed.at[out_rows, pl.ds(column, width)]
                    made.append(
                        (number, pltpu.make_async_copy(source, target, sems.at[len(made)]))
                    )
    return made


def run_copies(made):
    for _, copy in made:
        copy.start()
    for _, copy in made:
        copy.wait()


def add16(left, right):
    return left.astype(F32) + right.astype(F32)


def first_sum(height, place, mine, other, keep_a, send_a, keep_b, send_b):
    row_bit, col_bit = place[2], place[3]
    cut = keep_a.shape[1]
    step = math.gcd(height, 16)

    def piece(quarter, cols):
        rows = pl.ds(pl.multiple_of(quarter * height, step), height)
        return add16(mine[rows, cols], other[rows, cols]).astype(BF16)

    for bit in range(2):
        out = pl.ds(bit * height, height)
        keep_a[out, :] = piece(bit * 2 + col_bit, pl.ds(0, cut))
        send_a[out, :] = piece(bit * 2 + 1 - col_bit, pl.ds(0, cut))
        keep_b[out, :] = piece(row_bit * 2 + bit, pl.ds(cut, mine.shape[1] - cut))
        send_b[out, :] = piece((1 - row_bit) * 2 + bit, pl.ds(cut, mine.shape[1] - cut))


def second_sum(height, place, keep_a, got_a, keep_b, got_b, next_a, send_a, next_b, send_b):
    step = math.gcd(height, 16)
    for bit, keep, got, stay, send in (
        (place[2], keep_a, got_a, next_a, send_a),
        (place[3], keep_b, got_b, next_b, send_b),
    ):
        for which, out in ((bit, stay), (1 - bit, send)):
            rows = pl.ds(pl.multiple_of(which * height, step), height)
            out[...] = add16(keep[rows, :], got[rows, :]).astype(BF16)


def third_sum(height, place, keep_a, got_a, keep_b, got_b, own, *sends):
    chips = len(sends) + 1
    cut = keep_a.shape[1]
    step = math.gcd(height, 16)
    for hop, out in enumerate((own, *sends)):
        at = lax.rem(place[0] + hop, chips)
        rows = pl.ds(pl.multiple_of(at * height, step), height)
        out[:, :cut] = add16(keep_a[rows, :], got_a[rows, :]).astype(out.dtype)
        out[:, cut:] = add16(keep_b[rows, :], got_b[rows, :]).astype(out.dtype)


def fourth_sum(own, *refs):
    total = own[...]
    for ref in refs[:-1]:
        total = total + ref[...].astype(F32)
    refs[-1][...] = total.astype(BF16)


def last_spread(stacks, place, own, from_x, from_y, from_xy, *outs):
    replica = place[2] * 2 + place[3]
    height, packed = own.shape
    step = math.gcd(height, 16)
    for flip, source in enumerate((own, from_x, from_y, from_xy)):
        across = place[2] ^ (flip // 2)
        aside = place[3] ^ (flip % 2)
        column = 0
        for stacked, out in zip(stacks, outs):
            rows, width = out.shape
            if stacked:
                for half in range(rows // (4 * height)):
                    at = (across * 2 + aside) * (rows // 4) + half * height
                    out[pl.ds(pl.multiple_of(at, step), height), :] = source[
                        :, column : column + width
                    ].astype(F32)
                    column += width
            else:
                width = width // 2
                at = pl.ds(pl.multiple_of(across * height, step), height)
                cols = pl.ds(pl.multiple_of(aside * width, 128), width)
                out[at, cols] = source[:, column : column + width].astype(F32)
                column += width

        @pl.when((replica ^ flip) == 0)
        def _():
            outs[-1][...] = source[0:16, packed - 128 :].astype(F32)


def small_call(body, place, inputs, shapes, grid=None, in_specs=None, out_specs=None):
    if grid is None:
        grid = (1,)
        in_specs = [pl.BlockSpec(value.shape, lambda i, t: (0, 0)) for value in inputs]
        out_specs = [pl.BlockSpec(shape.shape, lambda i, t: (0, 0)) for shape in shapes]
    return pl.pallas_call(
        body,
        grid_spec=pltpu.PrefetchScalarGridSpec(
            num_scalar_prefetch=1, grid=grid, in_specs=in_specs, out_specs=out_specs
        ),
        out_shape=shapes,
        compiler_params=params(32),
    )(place, *inputs)


class Sum:
    def __init__(self, place, mine, theirs):
        self.place = place
        self.chips = lax.axis_size("fsdp") // 2
        self.height = mine.shape[0] // (4 * self.chips)
        self.packed = mine.shape[1]
        self.cut = self.packed // 256 * 128
        self.kept = [mine]
        self.sends = [theirs]
        self.ways = [core_swap]

    def send(self):
        return [way(value) for way, value in zip(self.ways, self.sends)]

    def shape(self, rows, cols, dtype=BF16):
        return jax.ShapeDtypeStruct((rows * self.height, cols), dtype)

    def block(self, count, cols):
        return pl.BlockSpec((count * self.height, cols), lambda i, t: (i, 0))

    def pair(self, make, rows):
        return [make(rows, self.cut)] * 2 + [make(rows, self.packed - self.cut)] * 2

    def add_first(self, arrived):
        keep_a, send_a, keep_b, send_b = small_call(
            functools.partial(first_sum, self.height),
            self.place,
            (*self.kept, *arrived),
            self.pair(self.shape, 2 * self.chips),
            (self.chips,),
            [self.block(4, self.packed)] * 2,
            self.pair(self.block, 2),
        )
        self.kept = [keep_a, keep_b]
        self.sends = [send_a, send_b]
        self.ways = [lambda v: replica_swap(v, 1), lambda v: replica_swap(v, 2)]

    def add_second(self, arrived):
        keep_a, send_a, keep_b, send_b = small_call(
            functools.partial(second_sum, self.height),
            self.place,
            (self.kept[0], arrived[0], self.kept[1], arrived[1]),
            self.pair(self.shape, self.chips),
            (self.chips,),
            self.pair(self.block, 2),
            self.pair(self.block, 1),
        )
        self.kept = [keep_a, keep_b]
        self.sends = [send_a, send_b]
        self.ways = [lambda v: replica_swap(v, 2), lambda v: replica_swap(v, 1)]

    def add_third(self, arrived):
        own, *self.sends = small_call(
            functools.partial(third_sum, self.height),
            self.place,
            (self.kept[0], arrived[0], self.kept[1], arrived[1]),
            [self.shape(1, self.packed, F32)] + [self.shape(1, self.packed)] * (self.chips - 1),
        )
        self.kept = [own]
        self.ways = [functools.partial(chip_shift, hops=hop) for hop in range(1, self.chips)]

    def add_fourth(self, arrived):
        (total,) = small_call(
            lambda table, *refs: fourth_sum(*refs),
            self.place,
            (*self.kept, *arrived),
            [self.shape(1, self.packed)],
        )
        self.kept = [total]
        self.sends = [total] * 3
        self.ways = [functools.partial(replica_swap, bits=bits) for bits in (1, 2, 3)]

    def result(self, arrived, stacks, out_shapes):
        return small_call(
            functools.partial(last_spread, stacks),
            self.place,
            (*self.kept, *arrived),
            [jax.ShapeDtypeStruct(s, F32) for s in out_shapes]
            + [jax.ShapeDtypeStruct((16, 128), F32)],
        )


def small_blocks(rows_of_shard, small, shards, own):
    small[...] = jnp.zeros_like(small)
    for shard in range(shards):
        rows = rows_of_shard(shard)
        small[shard, 0 : rows.shape[0], 0:own] = rows.astype(BF16)


def qkv_kernel(chips, place, tokens, vecs, *refs):
    owns = (refs[0:1], refs[1:2])
    pieces = (refs[2:6], refs[6:10])
    qkv, unit, weight, sems = refs[10:]
    width = tokens.shape[1]

    @pl.when(pl.program_id(0) == 0)
    def _():
        run_copies(fetch_copies(place, [(weight, False, 0)], owns, pieces, chips, sems))

    xhat, _ = normalise(tokens[...].astype(F32))
    unit[...] = xhat.astype(BF16)
    rows = (xhat * vecs[0:1, :] + vecs[1:2, :]).astype(BF16)
    query = dot(rows, weight[:, :width]) + vecs[2:3, :]
    qkv[:, :width] = query.astype(BF16) * jnp.asarray(0.125, BF16)
    qkv[:, width : 2 * width] = dot(rows, weight[:, width : 2 * width]).astype(BF16)
    value = dot(rows, weight[:, 2 * width :]) + vecs[3:4, :]
    qkv[:, 2 * width :] = value.astype(BF16)


def hbm():
    return pl.BlockSpec(memory_space=pl.ANY)


def qkv_forward(place, tokens, vecs, owns, pieces, block=512):
    rows, width = tokens.shape
    chips = lax.axis_size("fsdp") // 2
    sources = [*owns, *pieces[0], *pieces[1]]
    zero = lambda i, t: (0, 0)
    return pl.pallas_call(
        functools.partial(qkv_kernel, chips),
        grid_spec=pltpu.PrefetchScalarGridSpec(
            num_scalar_prefetch=1,
            grid=(rows // block,),
            in_specs=[
                pl.BlockSpec((block, width), lambda i, t: (i, 0)),
                pl.BlockSpec(vecs.shape, zero),
            ]
            + [hbm()] * len(sources),
            out_specs=[
                pl.BlockSpec((block, 3 * width), lambda i, t: (i, 0)),
                pl.BlockSpec((block, width), lambda i, t: (i, 0)),
                resident((width, 3 * width)),
            ],
            scratch_shapes=[pltpu.SemaphoreType.DMA((2 + 8 * (chips - 1),))],
        ),
        out_shape=[
            jax.ShapeDtypeStruct((rows, 3 * width), BF16),
            jax.ShapeDtypeStruct((rows, width), BF16),
            jax.ShapeDtypeStruct((width, 3 * width), BF16),
        ],
        compiler_params=params(60),
        cost_estimate=cost(12),
    )(place, tokens, vecs, *sources)


def clip_table(segment_ids, valid_mask):
    seq_len = segment_ids.shape[1]
    clips = jnp.arange(CLIPS, dtype=jnp.int32)[None, :, None]
    segments = segment_ids[:, None, :]
    start = jnp.sum((segments < clips).astype(jnp.int32), axis=2)
    end = jnp.sum((segments <= clips).astype(jnp.int32), axis=2)
    valid = jnp.sum(((segments == clips) & (valid_mask[:, None, :] == 1)).astype(jnp.int32), axis=2)
    aligned = start // 16 * 16
    need = end - aligned
    path = (need > WINDOW).astype(jnp.int32) + (need > 2 * WINDOW).astype(jnp.int32)
    window = jnp.where(path == 0, WINDOW, jnp.where(path == 1, 2 * WINDOW, seq_len))
    base = jnp.minimum(aligned, seq_len - window)
    return jnp.stack([base, path, start - base, end - base, start + valid - base], axis=2).reshape(
        -1
    )


def lane_low(rows):
    return lax.broadcasted_iota(jnp.int32, (rows, 128), 1) < 64


def flag_lane(rows):
    return lax.broadcasted_iota(jnp.int32, (rows, 128), 1) % 64 == 0


def row_mask(rows, offset, first, last):
    index = lax.broadcasted_iota(jnp.int32, (rows, 128), 0) + offset
    return (index >= first) & (index < last)


def key_extra(rows, first, last):
    bias = jnp.where(row_mask(rows, 0, first, last), 0.0, NEGATIVE)
    return jnp.where(flag_lane(rows), bias, 0.0).astype(BF16)


def query_extra(rows):
    return jnp.where(flag_lane(rows), 1.0, 0.0).astype(BF16)


def weights_of(query, keys, extra_query, extra_keys, low, low_keys, head):
    if head == 0:
        left = jnp.where(low, query, extra_query)
        right = jnp.where(low_keys, keys, extra_keys)
    else:
        left = jnp.where(low, extra_query, query)
        right = jnp.where(low_keys, extra_keys, keys)
    scores = dot_nt(left, right)
    return jnp.exp(scores - jnp.max(scores, axis=1, keepdims=True)).astype(BF16)


def attend_window(refs, base, first, last, valid_end, window, pairs, exps, clip):
    queries, keys_ref, values_ref, mixed, inverse = refs
    chunk = WINDOW
    low = lane_low(chunk)
    low_keys = lane_low(window)
    extra_keys = key_extra(window, first, valid_end)
    extra_query = query_extra(chunk)
    ones = jnp.ones((window, 128), BF16)
    key_rows = pl.ds(base, window)

    def one_chunk(offset, row_start):
        rows = pl.ds(row_start, chunk)
        keep = row_mask(chunk, offset, first, last)
        for pair in range(pairs):
            lanes = pl.ds(128 * pair, 128)
            query = queries[rows, lanes]
            keys = keys_ref[key_rows, lanes]
            stack = jnp.concatenate([values_ref[key_rows, lanes], ones], axis=1)
            sums = []
            for head in range(2):
                weights = weights_of(query, keys, extra_query, extra_keys, low, low_keys, head)
                if exps is not None:
                    exps[0, 2 * pair + head, pl.ds(clip * WINDOW, WINDOW), :] = weights
                sums.append(dot(weights, stack))
            total = jnp.where(low, sums[0][:, 128:], sums[1][:, 128:])
            weighted = jnp.where(low, sums[0][:, :128], sums[1][:, :128])
            reciprocal = 1.0 / total
            mixed[rows, lanes] = jnp.where(
                keep, (weighted * reciprocal), mixed[rows, lanes].astype(F32)
            ).astype(BF16)
            inverse[rows, lanes] = jnp.where(keep, reciprocal, inverse[rows, lanes])

    if window == chunk:
        one_chunk(0, base)
    else:

        def step(index, carry):
            offset = index * chunk
            one_chunk(offset, pl.multiple_of(base + offset, 16))
            return carry

        lax.fori_loop(0, window // chunk, step, 0)


def clip_fields(table, sequence, clip):
    at = (sequence * CLIPS + clip) * FIELDS
    base = pl.multiple_of(table[at], 16)
    return base, table[at + 1], table[at + 2], table[at + 3], table[at + 4]


def loop_clips(table, sequence, one_clip, some_clips):
    longest = 0
    for clip in range(CLIPS):
        longest = jnp.maximum(longest, clip_fields(table, sequence, clip)[1])

    @pl.when(longest == 0)
    def _():
        lax.fori_loop(0, CLIPS // TOGETHER, some_clips, 0)

    @pl.when(longest > 0)
    def _():
        lax.fori_loop(0, CLIPS, one_clip, 0)


def attend_kernel(pairs, table, queries, keys, values, mixed, inverse, exps):
    sequence = pl.program_id(0)
    seq_len = queries.shape[0]
    mixed[...] = jnp.zeros_like(mixed)
    inverse[...] = jnp.zeros_like(inverse)
    refs = (queries, keys, values, mixed, inverse)

    def one_clip(clip, carry):
        base, path, first, last, valid_end = clip_fields(table, sequence, clip)
        for number, window in enumerate((WINDOW, 2 * WINDOW, seq_len)):

            @pl.when(path == number)
            def _():
                attend_window(
                    refs,
                    base,
                    first,
                    last,
                    valid_end,
                    window,
                    pairs,
                    exps if number == 0 else None,
                    clip,
                )

        return carry

    def some_clips(index, carry):
        for clip in range(TOGETHER):
            clip = index * TOGETHER + clip
            base, _, first, last, valid_end = clip_fields(table, sequence, clip)
            attend_window(refs, base, first, last, valid_end, WINDOW, pairs, exps, clip)
        return carry

    loop_clips(table, sequence, one_clip, some_clips)


def attend_forward(table, qkv, seq_len, group, pairs=2):
    rows = qkv.shape[0]
    width = qkv.shape[1] // 3
    seqs = rows // seq_len
    lanes = 128 * pairs
    groups = width // lanes
    block = (seq_len, lanes)
    own = pl.BlockSpec(block, lambda s, t: (s, 0))
    return pl.pallas_call(
        functools.partial(attend_kernel, pairs),
        grid_spec=pltpu.PrefetchScalarGridSpec(
            num_scalar_prefetch=1,
            grid=(seqs,),
            in_specs=[
                pl.BlockSpec(block, lambda s, t: (s, group)),
                pl.BlockSpec(block, lambda s, t: (s, groups + group)),
                pl.BlockSpec(block, lambda s, t: (s, 2 * groups + group)),
            ],
            out_specs=[
                own,
                own,
                pl.BlockSpec((1, 2 * pairs, CLIPS * WINDOW, WINDOW), lambda s, t: (s, 0, 0, 0)),
            ],
        ),
        out_shape=[
            jax.ShapeDtypeStruct((rows, lanes), BF16),
            jax.ShapeDtypeStruct((rows, lanes), F32),
            jax.ShapeDtypeStruct((seqs, 2 * pairs, CLIPS * WINDOW, WINDOW), BF16),
        ],
        compiler_params=params(60),
        cost_estimate=cost(10),
    )(table, qkv, qkv, qkv)


def back_window(refs, base, first, last, valid_end, window, pairs, exps, clip, gather):
    queries, keys_ref, values_ref, grads, mixed, inverse, dq, dk, dv = refs
    key_grad, value_grad = gather
    chunk = WINDOW
    single = window == chunk
    low = lane_low(chunk)
    low_keys = lane_low(window)
    extra_keys = None if single else key_extra(window, first, valid_end)
    extra_query = None if single else query_extra(chunk)
    key_rows = pl.ds(base, window)
    one = jnp.ones((window, 128), BF16)

    def one_chunk(offset, row_start):
        rows = pl.ds(row_start, chunk)
        keep = row_mask(chunk, offset, first, last)
        for pair in range(pairs):
            lanes = pl.ds(128 * pair, 128)
            query = queries[rows, lanes]
            keys = keys_ref[key_rows, lanes]
            values = values_ref[key_rows, lanes]
            scaled = jnp.where(keep, grads[rows, lanes].astype(F32) * inverse[rows, lanes], 0.0)
            product = scaled * mixed[rows, lanes].astype(F32)
            turned = pltpu.roll(-product, 64, 1).astype(BF16)
            scaled = scaled.astype(BF16)
            parts = []
            for head in range(2):
                if head == 0:
                    left = jnp.where(low, scaled, turned)
                    right = jnp.where(low_keys, values, one)
                else:
                    left = jnp.where(low, turned, scaled)
                    right = jnp.where(low_keys, one, values)
                if single:
                    weights = exps[0, 2 * pair + head, pl.ds(clip * WINDOW, WINDOW), :]
                else:
                    weights = weights_of(query, keys, extra_query, extra_keys, low, low_keys, head)
                grad_scores = (weights.astype(F32) * dot_nt(left, right)).astype(BF16)
                parts.append(
                    (
                        dot(grad_scores, keys),
                        dot_tn(grad_scores, query),
                        dot_tn(weights, scaled),
                    )
                )
            query_part = jnp.where(low, parts[0][0], parts[1][0]) * 0.125
            key_part = jnp.where(low_keys, parts[0][1], parts[1][1])
            value_part = jnp.where(low_keys, parts[0][2], parts[1][2])
            dq[rows, lanes] = jnp.where(keep, query_part, dq[rows, lanes].astype(F32)).astype(BF16)
            if single:
                dk[rows, lanes] = jnp.where(keep, key_part, dk[rows, lanes].astype(F32)).astype(
                    BF16
                )
                dv[rows, lanes] = jnp.where(keep, value_part, dv[rows, lanes].astype(F32)).astype(
                    BF16
                )
            else:
                key_grad[pl.ds(0, window), lanes] += key_part
                value_grad[pl.ds(0, window), lanes] += value_part

    if single:
        one_chunk(0, base)
        return
    key_grad[...] = jnp.zeros_like(key_grad)
    value_grad[...] = jnp.zeros_like(value_grad)

    def step(index, carry):
        offset = index * chunk
        one_chunk(offset, pl.multiple_of(base + offset, 16))
        return carry

    lax.fori_loop(0, window // chunk, step, 0)
    keep = row_mask(window, 0, first, last)
    for pair in range(pairs):
        lanes = pl.ds(128 * pair, 128)
        for ref, total in ((dk, key_grad), (dv, value_grad)):
            ref[key_rows, lanes] = jnp.where(
                keep, total[pl.ds(0, window), lanes], ref[key_rows, lanes].astype(F32)
            ).astype(BF16)


def back_kernel(
    pairs,
    table,
    queries,
    keys,
    values,
    grads,
    mixed,
    inverse,
    exps,
    dq,
    dk,
    dv,
    key_grad,
    value_grad,
):
    sequence = pl.program_id(0)
    seq_len = queries.shape[0]
    for ref in (dq, dk, dv):
        ref[...] = jnp.zeros_like(ref)
    refs = (queries, keys, values, grads, mixed, inverse, dq, dk, dv)

    gather = (key_grad, value_grad)

    def one_clip(clip, carry):
        base, path, first, last, valid_end = clip_fields(table, sequence, clip)
        for number, window in enumerate((WINDOW, 2 * WINDOW, seq_len)):

            @pl.when(path == number)
            def _():
                back_window(
                    refs, base, first, last, valid_end, window, pairs, exps, clip, gather
                )

        return carry

    def some_clips(index, carry):
        for clip in range(TOGETHER):
            clip = index * TOGETHER + clip
            base, _, first, last, valid_end = clip_fields(table, sequence, clip)
            back_window(refs, base, first, last, valid_end, WINDOW, pairs, exps, clip, gather)
        return carry

    loop_clips(table, sequence, one_clip, some_clips)


def attend_backward(table, qkv, grads, mixed, inverse, exps, seq_len, group, pairs=2):
    rows = mixed.shape[0]
    seqs = rows // seq_len
    lanes = 128 * pairs
    groups = grads.shape[1] // lanes
    block = (seq_len, lanes)
    own = pl.BlockSpec(block, lambda s, t: (s, 0))
    shape = jax.ShapeDtypeStruct((rows, lanes), BF16)
    return pl.pallas_call(
        functools.partial(back_kernel, pairs),
        grid_spec=pltpu.PrefetchScalarGridSpec(
            num_scalar_prefetch=1,
            grid=(seqs,),
            in_specs=[
                pl.BlockSpec(block, lambda s, t: (s, group)),
                pl.BlockSpec(block, lambda s, t: (s, groups + group)),
                pl.BlockSpec(block, lambda s, t: (s, 2 * groups + group)),
                pl.BlockSpec(block, lambda s, t: (s, group)),
                own,
                own,
                pl.BlockSpec((1, 2 * pairs, CLIPS * WINDOW, WINDOW), lambda s, t: (s, 0, 0, 0)),
            ],
            out_specs=[own, own, own],
            scratch_shapes=[pltpu.VMEM(block, F32), pltpu.VMEM(block, F32)],
        ),
        out_shape=[shape, shape, shape],
        compiler_params=params(60),
        cost_estimate=cost(19),
    )(table, qkv, qkv, qkv, grads, mixed, inverse, exps)


def gauss(value):
    cdf = 0.5 + 0.5 * lax.erf(value * 0.7071067811865476)
    tail = jnp.exp2(value * value * (-0.5 * 1.4426950408889634))
    return cdf, value * tail * 0.3989422804014327


def middle_kernel(
    part,
    chips,
    groups,
    place,
    tokens,
    cotangent,
    vecs,
    ebias,
    *refs,
):
    mixed, refs = refs[:groups], refs[groups:]
    owns = (refs[0:3], refs[3:6])
    pieces = (refs[6:10], refs[10:14])
    (
        output,
        grad_middle,
        grad_mixed,
        mine,
        theirs,
        proj,
        expand,
        reduce,
        sum_proj,
        sum_expand,
        sum_reduce,
        sum_ebias,
        sum_vecs,
        middle,
        units,
        scales,
        normed,
        normed_t,
        grad_normed,
        activated,
        grad_hidden,
        small,
        blank,
        in_sems,
        out_sems,
    ) = refs[14:]
    step = pl.program_id(0)
    width, hidden = expand.shape
    block = tokens.shape[0]
    half = block // 2
    own = width // (2 * chips)
    targets = [
        (proj, False, 0),
        (expand, False, width // 2),
        (reduce, True, width // 2 + hidden // 2),
    ]

    @pl.when(step == 0)
    def _():
        made = fetch_copies(place, targets, owns, pieces, chips, in_sems)
        for _, copy in made:
            copy.start()
        sum_proj[...] = jnp.zeros_like(sum_proj)
        sum_expand[...] = jnp.zeros_like(sum_expand)
        sum_reduce[...] = jnp.zeros_like(sum_reduce)
        sum_ebias[...] = jnp.zeros_like(sum_ebias)
        sum_vecs[...] = jnp.zeros_like(sum_vecs)
        for _, copy in made:
            copy.wait()

    def norm_rows(first, count):
        rows = pl.ds(first, count)
        xhat, scale = normalise(middle[rows, :])
        units[rows, :] = xhat
        scales[rows, :] = scale
        normed[rows, :] = (xhat * vecs[5:6, :] + vecs[6:7, :]).astype(BF16)

    def hidden_part(which, start):
        rows = pl.ds(which * half, half)
        cols = pl.ds(start, part)
        into = expand[:, cols]
        back = reduce[cols, :]
        preact = dot(normed[rows, :], into) + ebias[:, cols]
        cdf, slope = gauss(preact)
        active = (preact * cdf).astype(BF16)
        activated[rows, cols] = active
        grad_preact = (dot_nt(cotangent[rows, :], back) * (cdf + slope)).astype(BF16)
        grad_hidden[rows, cols] = grad_preact
        sum_ebias[:, cols] += jnp.sum(grad_preact.astype(F32), axis=0, keepdims=True)
        middle[rows, :] += dot(active, back)
        grad_normed[rows, :] += dot_nt(grad_preact, into)

    def end_rows(first, count):
        rows = pl.ds(first, count)
        upstream = grad_normed[rows, :]
        xhat = units[rows, :]
        output[rows, :] = (middle[rows, :] + vecs[7:8, :]).astype(BF16)
        cot = cotangent[rows, :].astype(F32)
        grads = cot + norm_back(upstream, vecs[5:6, :], xhat, scales[rows, :])
        attended = grads.astype(BF16)
        grad_middle[rows, :] = attended
        sum_vecs[0:1, :] += jnp.sum(attended.astype(F32), axis=0, keepdims=True)
        sum_vecs[1:2, :] += jnp.sum(upstream * xhat, axis=0, keepdims=True)
        sum_vecs[2:3, :] += jnp.sum(upstream, axis=0, keepdims=True)
        sum_vecs[3:4, :] += jnp.sum(cot, axis=0, keepdims=True)

    mixed_rows = jnp.concatenate([ref[...] for ref in mixed], axis=1)
    middle[...] = tokens[...].astype(F32) + dot(mixed_rows, proj[...]) + vecs[4:5, :]
    parts = hidden // part
    piece = half // parts
    grad_normed[...] = jnp.zeros_like(grad_normed)
    norm_rows(0, half)

    def first_half(index, carry):
        hidden_part(0, pl.multiple_of(index * part, part))
        norm_rows(pl.multiple_of(half + index * piece, piece), piece)
        return carry

    lax.fori_loop(0, parts, first_half, 0)
    normed_t[...] = normed[...].T

    def second_half(index, carry):
        start = pl.multiple_of(index * part, part)
        hidden_part(1, start)
        cols = pl.ds(start, part)
        sum_reduce[cols, :] += dot_tn(activated[:, cols], cotangent[...])
        sum_expand[:, cols] += dot(normed_t[...], grad_hidden[:, cols])
        end_rows(pl.multiple_of(index * piece, piece), piece)
        return carry

    lax.fori_loop(0, parts, second_half, 0, unroll=4)
    end_rows(half, half)
    attended = grad_middle[...]
    grad_mixed[...] = dot_nt(attended, proj[...]).astype(BF16)
    sum_proj[...] += dot_tn(mixed_rows, attended)

    @pl.when(step == pl.num_programs(0) - 1)
    def _():
        blank[...] = jnp.zeros_like(blank)
        per = hidden // width

        def rows_of_shard(shard):
            rows = [sum_vecs[0:4, shard * own : (shard + 1) * own]]
            for index in range(per):
                at = (shard * per + index) * own
                rows.append(sum_ebias[0:1, at : at + own])
            return jnp.concatenate(rows, axis=0)

        small_blocks(rows_of_shard, small, 2 * chips, own)
        made = spread_copies(
            place,
            [(proj, False), (expand, False), (reduce, True)],
            small,
            blank,
            mine,
            theirs,
            chips,
            out_sems,
        )
        for number, (low, total) in enumerate(
            ((proj, sum_proj), (expand, sum_expand), (reduce, sum_reduce))
        ):
            low[...] = total[...].astype(BF16)
            for which, copy in made:
                if which == number or (which == 3 and number == 0):
                    copy.start()
        for _, copy in made:
            copy.wait()


def middle_all(
    place, tokens, mixed, cotangent, vecs, ebias, owns, others, pieces, block=512, part=768
):
    rows, width = tokens.shape
    chips = lax.axis_size("fsdp") // 2
    hidden = ebias.shape[1]
    height = width // (4 * chips)
    row_block = pl.BlockSpec((block, width), lambda i, t: (i, 0))
    row_shape = jax.ShapeDtypeStruct((rows, width), BF16)
    packed = (4 * chips * height, width // 2 + hidden // 2 + hidden // 2 + 128)
    packed_shape = jax.ShapeDtypeStruct(packed, BF16)
    sources = [*owns, *others, *pieces[0], *pieces[1]]
    halves = hidden // width // 2
    mixed_block = pl.BlockSpec((block, mixed[0].shape[1]), lambda i, t: (i, 0))
    return pl.pallas_call(
        functools.partial(middle_kernel, part, chips, len(mixed)),
        grid_spec=pltpu.PrefetchScalarGridSpec(
            num_scalar_prefetch=1,
            grid=(rows // block,),
            in_specs=[row_block] * 2
            + [
                pl.BlockSpec(vecs.shape, lambda i, t: (0, 0)),
                pl.BlockSpec(ebias.shape, lambda i, t: (0, 0)),
            ]
            + [mixed_block] * len(mixed)
            + [hbm()] * len(sources),
            out_specs=[row_block] * 3 + [hbm(), hbm()],
            scratch_shapes=[
                pltpu.VMEM((width, width), BF16),
                pltpu.VMEM((width, hidden), BF16),
                pltpu.VMEM((hidden, width), BF16),
                pltpu.VMEM((width, width), F32),
                pltpu.VMEM((width, hidden), F32),
                pltpu.VMEM((hidden, width), F32),
                pltpu.VMEM((1, hidden), F32),
                pltpu.VMEM((8, width), F32),
                pltpu.VMEM((block, width), F32),
                pltpu.VMEM((block, width), F32),
                pltpu.VMEM((block, 1), F32),
                pltpu.VMEM((block, width), BF16),
                pltpu.VMEM((width, block), BF16),
                pltpu.VMEM((block, width), F32),
                pltpu.VMEM((block, hidden), BF16),
                pltpu.VMEM((block, hidden), BF16),
                pltpu.VMEM((2 * chips, height, 128), BF16),
                pltpu.VMEM((height, 128), BF16),
                pltpu.SemaphoreType.DMA((2 * (3 + 4 * (chips - 1) * (2 + halves)),)),
                pltpu.SemaphoreType.DMA((8 * chips * (3 + halves),)),
            ],
        ),
        out_shape=[row_shape, row_shape, row_shape, packed_shape, packed_shape],
        compiler_params=params(63),
        cost_estimate=cost(110),
    )(place, tokens, cotangent, vecs, ebias, *mixed, *sources)


def weight_kernel(chips, offsets, place, unit, vecs, weight, *refs):
    count = len(offsets)
    parts, refs = refs[:count], refs[count:]
    mine, theirs, total, sums, low, small, blank, sems = refs
    step = pl.program_id(0)
    width = unit.shape[1]
    lanes = parts[0].shape[1]
    own = width // (2 * chips)

    @pl.when(step == 0)
    def _():
        total[...] = jnp.zeros_like(total)
        sums[...] = jnp.zeros_like(sums)

    rows_t = unit[...].T
    for index, part in enumerate(parts):
        cols = slice(index * lanes, (index + 1) * lanes)
        total[:, cols] += dot(rows_t, part[...])
        sums[0:1, cols] += jnp.sum(part[...].astype(F32), axis=0, keepdims=True)

    @pl.when(step == pl.num_programs(0) - 1)
    def _():
        columns = vecs[...].T
        gain, shift = columns[:, 0:1], columns[:, 1:2]
        gain_part = jnp.zeros((width, 1), F32)
        shift_part = jnp.zeros((width, 1), F32)
        empty = jnp.zeros((1, lanes), F32)
        biases = [[empty] * (width // lanes) for _ in range(3)]
        for index, offset in enumerate(offsets):
            cols = slice(index * lanes, (index + 1) * lanes)
            raw = total[:, cols]
            sides = weight[:, offset : offset + lanes].astype(F32)
            line = sums[0:1, cols]
            gain_part += jnp.sum(raw * sides, axis=1, keepdims=True)
            shift_part += jnp.sum(line * sides, axis=1, keepdims=True)
            low[:, cols] = (gain * raw + shift * line).astype(BF16)
            biases[offset // width][offset % width // lanes] = line
        pick = lax.broadcasted_iota(jnp.int32, (width, 128), 1)
        both = jnp.where(pick == 0, gain_part, jnp.where(pick == 1, shift_part, 0.0)).T
        query_line = jnp.concatenate(biases[0], axis=1)
        value_line = jnp.concatenate(biases[2], axis=1)
        blank[...] = jnp.zeros_like(blank)

        def rows_of_shard(shard):
            cols = slice(shard * own, (shard + 1) * own)
            return jnp.concatenate([both[0:2, cols], query_line[:, cols], value_line[:, cols]], axis=0)

        small_blocks(rows_of_shard, small, 2 * chips, own)
        run_copies(
            spread_copies(place, [(low, False)], small, blank, mine, theirs, chips, sems)
        )


def qkv_weight_grad(place, unit, vecs, weight, groups, grads, block=512):
    rows, width = unit.shape
    lanes = grads[0][0].shape[1]
    chips = lax.axis_size("fsdp") // 2
    height = width // (4 * chips)
    offsets = tuple(part * width + group * lanes for part in range(3) for group in groups)
    parts = [grad[part] for part in range(3) for grad in grads]
    columns = lanes * len(parts)
    packed = jax.ShapeDtypeStruct((4 * chips * height, columns // 2 + 128), BF16)
    zero = lambda i, t: (0, 0)
    return pl.pallas_call(
        functools.partial(weight_kernel, chips, offsets),
        grid_spec=pltpu.PrefetchScalarGridSpec(
            num_scalar_prefetch=1,
            grid=(rows // block,),
            in_specs=[
                pl.BlockSpec((block, width), lambda i, t: (i, 0)),
                pl.BlockSpec(vecs.shape, zero),
                resident(weight.shape),
            ]
            + [pl.BlockSpec((block, lanes), lambda i, t: (i, 0))] * len(parts),
            out_specs=[hbm(), hbm()],
            scratch_shapes=[
                pltpu.VMEM((width, columns), F32),
                pltpu.VMEM((8, columns), F32),
                pltpu.VMEM((width, columns), BF16),
                pltpu.VMEM((2 * chips, height, 128), BF16),
                pltpu.VMEM((height, 128), BF16),
                pltpu.SemaphoreType.DMA((16 * chips,)),
            ],
        ),
        out_shape=[packed, packed],
        compiler_params=params(60),
        cost_estimate=cost(4 * len(groups)),
    )(place, unit, vecs, weight, *parts)


def input_kernel(count, tokens, grad_middle, vecs, weight, *refs):
    width = tokens.shape[1]
    lanes = width // count
    input_grad = refs[-1]
    xhat, scale = normalise(tokens[...].astype(F32))
    upstream = None
    for part in range(3):
        rows = jnp.concatenate([ref[...] for ref in refs[part * count : (part + 1) * count]], axis=1)
        term = dot_nt(rows, weight[:, part * width : (part + 1) * width])
        upstream = term if upstream is None else upstream + term
    grads = norm_back(upstream, vecs[0:1, :], xhat, scale)
    input_grad[...] = (grad_middle[...].astype(F32) + grads).astype(BF16)


def input_backward(tokens, grad_middle, vecs, weight, grads, first, rows, into=None, block=512):
    width = tokens.shape[1]
    lanes = grads[0][0].shape[1]
    start = first // block
    row_block = pl.BlockSpec((block, width), lambda i: (i + start, 0))
    parts = [grad[part] for part in range(3) for grad in grads]
    inputs = [tokens, grad_middle, vecs, weight, *parts]
    specs = [row_block] * 2 + [resident(vecs.shape), resident(weight.shape)]
    specs += [pl.BlockSpec((block, lanes), lambda i: (i + start, 0))] * len(parts)
    aliases = {}
    if into is not None:
        aliases = {len(inputs): 0}
        inputs.append(into)
        specs.append(hbm())
    return pl.pallas_call(
        functools.partial(input_kernel, len(grads)),
        grid=(rows // block,),
        in_specs=specs,
        out_specs=row_block,
        out_shape=jax.ShapeDtypeStruct(tokens.shape, BF16),
        input_output_aliases=aliases,
        compiler_params=params(60),
        cost_estimate=cost(7),
    )(*inputs)


def local(
    tokens,
    segment_ids,
    valid_mask,
    cotangent,
    norm1_gain,
    norm1_bias,
    qkv_weight,
    query_bias,
    value_bias,
    proj_weight,
    proj_bias,
    norm2_gain,
    norm2_bias,
    expand_weight,
    expand_bias,
    reduce_weight,
    reduce_bias,
):
    seq_len = segment_ids.shape[1]
    own, width = proj_weight.shape
    shards = lax.axis_size("fsdp")
    chips = shards // 2
    height = own // 2
    per = expand_bias.shape[0] // own
    place = place_table()
    row_bit, col_bit = place[2], place[3]

    def tile(weight):
        half = weight.shape[1] // 2
        return lax.dynamic_slice(weight, (row_bit * height, col_bit * half), (height, half))

    small = jnp.stack(
        [
            norm1_gain,
            norm1_bias,
            query_bias,
            value_bias,
            proj_bias,
            norm2_gain,
            norm2_bias,
            reduce_bias,
            *jnp.split(expand_bias, per),
        ]
    )
    block = jnp.pad(small, ((0, height - small.shape[0]), (0, 128 - own)))
    piece = jnp.concatenate([tile(qkv_weight), block], axis=1)
    quarter = lax.dynamic_slice(
        reduce_weight,
        ((row_bit * 2 + col_bit) * (per * own // 4), 0),
        (per * own // 4, width),
    )
    parts = [tile(proj_weight), tile(expand_weight), *jnp.split(quarter, per // 2, axis=0)]
    rest = jnp.concatenate(parts, axis=1)
    table = clip_table(segment_ids, valid_mask)
    owns = (proj_weight, expand_weight, reduce_weight)

    got = shift_all(piece)
    other_qkv, small_other = core_swap(qkv_weight), core_swap(small)
    got, other_qkv, small_other, rest, table = barrier(got, other_qkv, small_other, rest, table)
    along = jnp.concatenate(got, axis=0)
    sides = swap_sides(along)
    odd = shift_all(rest, 1, 2)
    sides, along = barrier(sides, along)
    halves = swap_diagonal(*sides)
    halves, sides, along, odd, rest = barrier(halves, sides, along, odd, rest)
    here = (along, *sides, jnp.concatenate(halves, axis=1))
    qkv_pieces = barrier(here, tuple(core_swap(part) for part in here))

    chip, core = place[0], place[1]
    edge = piece.shape[1] - 128

    def blocks_of(first, along):
        rest = along.reshape(chips - 1, height, -1)[:, : small.shape[0], edge : edge + own]
        return jnp.concatenate([first[None], rest], axis=0)

    both = jnp.stack(
        [blocks_of(small, qkv_pieces[0][0]), blocks_of(small_other, qkv_pieces[1][0])], axis=1
    )
    hops = (chip - jnp.arange(chips)) % chips
    choice = (hops[:, None, None, None] == jnp.arange(chips)[None, None, :, None]) & (
        (jnp.arange(2) ^ core)[None, :, None, None] == jnp.arange(2)[None, None, None, :]
    )
    small = jnp.sum(
        jnp.where(choice[..., None, None], both[None, None].astype(F32), 0.0), axis=(2, 3)
    ).reshape(shards, small.shape[0], own)
    vecs = small[:, :8].swapaxes(0, 1).reshape(8, width)
    ebias = small[:, 8:].reshape(1, width * per)

    qkv, unit, qkv_full = qkv_forward(
        place, tokens, vecs, (qkv_weight, other_qkv), qkv_pieces
    )
    even = shift_all(rest, 2, 2)
    even, qkv, unit, qkv_full = barrier(even, qkv, unit, qkv_full)

    along = jnp.concatenate(
        [(even, odd)[hop % 2][(hop - 1) // 2] for hop in range(1, chips)], axis=0
    )
    along, qkv = barrier(along, qkv)
    sides = swap_sides(along)
    others = [core_swap(weight) for weight in owns]
    forward = [attend_forward(table, qkv, seq_len, 0)]
    forward, now, others = barrier(forward, qkv, others)
    forward.append(attend_forward(table, now, seq_len, 1))
    sides, forward, now, along = barrier(sides, forward, now, along)
    halves = swap_diagonal(*sides)
    swapped = [core_swap(part) for part in (along, *sides)]
    forward.append(attend_forward(table, now, seq_len, 2))
    halves, swapped, forward = barrier(halves, swapped, forward)
    diagonal = jnp.concatenate(halves, axis=1)
    rest_pieces = ((along, *sides, diagonal), (*swapped, core_swap(diagonal)))
    mixed = [result[0] for result in forward]

    output, grad_middle, grad_mixed, mine, theirs = middle_all(
        place, tokens, mixed, cotangent, vecs, ebias, owns, others, rest_pieces
    )

    def back(group, grads):
        return attend_backward(table, qkv, grads, *forward[group], seq_len, group)

    middle_sum = Sum(place, mine, theirs)
    moving = middle_sum.send()
    backward = [back(0, grad_mixed)]
    moving, backward, grad_mixed = barrier(moving, backward, grad_mixed)
    middle_sum.add_first(moving)
    middle_sum.sends, grad_mixed = barrier(middle_sum.sends, grad_mixed)
    moving = middle_sum.send()
    backward.append(back(1, grad_mixed))
    backward, grad_mixed = barrier(backward, grad_mixed)
    backward.append(back(2, grad_mixed))
    moving, backward, unit = barrier(moving, backward, unit)
    middle_sum.add_second(moving)
    middle_sum.sends, unit = barrier(middle_sum.sends, unit)
    moving = middle_sum.send()
    mine, theirs = qkv_weight_grad(place, unit, vecs, qkv_full, (0, 1, 2), backward)
    moving, mine, theirs = barrier(moving, mine, theirs)
    middle_sum.add_third(moving)
    middle_sum.sends, theirs, tokens = barrier(middle_sum.sends, theirs, tokens)
    qkv_sum = Sum(place, mine, theirs)
    moving = middle_sum.send()
    qkv_moving = qkv_sum.send()
    half = seq_len
    input_grad = input_backward(tokens, grad_middle, vecs, qkv_full, backward, 0, half)
    qkv_moving, input_grad, tokens = barrier(qkv_moving, input_grad, tokens)
    qkv_sum.add_first(qkv_moving)
    qkv_sum.sends, tokens = barrier(qkv_sum.sends, tokens)
    qkv_moving = qkv_sum.send()
    input_grad = input_backward(
        tokens, grad_middle, vecs, qkv_full, backward, half, half, input_grad
    )
    qkv_moving, input_grad = barrier(qkv_moving, input_grad)
    qkv_sum.add_second(qkv_moving)
    qkv_moving = qkv_sum.send()
    moving, qkv_moving = barrier(moving, qkv_moving)
    qkv_sum.add_third(qkv_moving)
    qkv_moving = qkv_sum.send()
    middle_sum.add_fourth(moving)
    moving = middle_sum.send()
    qkv_sum.add_fourth(qkv_moving)
    qkv_moving = qkv_sum.send()
    sum_proj, sum_expand, sum_reduce, middle_small = middle_sum.result(
        moving,
        (False, False, True),
        (proj_weight.shape, expand_weight.shape, reduce_weight.shape),
    )
    sum_qkv, qkv_small = qkv_sum.result(qkv_moving, (False,), (qkv_weight.shape,))
    return (
        output,
        input_grad,
        qkv_small[0, :own],
        qkv_small[1, :own],
        sum_qkv,
        qkv_small[2, :own],
        qkv_small[3, :own],
        sum_proj,
        middle_small[0, :own],
        middle_small[1, :own],
        middle_small[2, :own],
        sum_expand,
        middle_small[4 : 4 + per, :own].reshape(-1),
        sum_reduce,
        middle_small[3, :own],
    )


def solution(mesh):
    rows = P(("rep", "fsdp"), None)
    vector = P("fsdp")
    matrix = P("fsdp", None)
    params_specs = (
        vector,
        vector,
        matrix,
        vector,
        vector,
        matrix,
        vector,
        vector,
        vector,
        matrix,
        vector,
        matrix,
        vector,
    )
    return jax.shard_map(
        local,
        mesh=mesh,
        in_specs=(rows, rows, rows, rows) + params_specs,
        out_specs=(rows, rows) + params_specs,
        check_vma=False,
    )
```

```python
import functools
import math

import jax
import jax.numpy as jnp
from jax import lax
from jax.experimental import pallas as pl
from jax.experimental.pallas import tpu as pltpu
from jax.sharding import PartitionSpec as P

HEADS = 12
CLIPS = 6
EPSILON = 1e-06
WINDOW = 256
FIELDS = 5
TOGETHER = 6
BF16 = jnp.bfloat16
F32 = jnp.float32
MEBI = 1024 * 1024
NEGATIVE = -1e30


def dot(left, right):
    return lax.dot_general(left, right, (((1,), (0,)), ((), ())), preferred_element_type=F32)


def dot_nt(left, right):
    return lax.dot_general(left, right, (((1,), (1,)), ((), ())), preferred_element_type=F32)


def dot_tn(left, right):
    return lax.dot_general(left, right, (((0,), (0,)), ((), ())), preferred_element_type=F32)


def resident(shape):
    zeros = (0,) * len(shape)
    return pl.BlockSpec(shape, lambda *_: zeros, pipeline_mode=pl.Buffered(1))


def params(limit, count=1):
    return pltpu.CompilerParams(
        vmem_limit_bytes=limit * MEBI, dimension_semantics=("arbitrary",) * count
    )


def cost(micros):
    return pl.CostEstimate(flops=int(micros * 1e4), bytes_accessed=100, transcendentals=0)


def after(value, *others):
    return lax.optimization_barrier((value, *others))[0]


def normalise(values):
    row_mean = jnp.mean(values, axis=-1, keepdims=True)
    centred = values - row_mean
    row_var = jnp.mean(centred * centred, axis=-1, keepdims=True)
    scale = lax.rsqrt(row_var + EPSILON)
    return centred * scale, scale


def norm_back(upstream, gain, xhat, scale):
    weighted = upstream * gain
    first = jnp.mean(weighted, axis=-1, keepdims=True)
    second = jnp.mean(weighted * xhat, axis=-1, keepdims=True)
    return scale * (weighted - first - xhat * second)


def core_swap(value):
    count = lax.axis_size("fsdp")
    return lax.ppermute(value, "fsdp", [(i, i ^ 1) for i in range(count)])


def chip_shift(value, hops):
    count = lax.axis_size("fsdp")
    return lax.ppermute(value, "fsdp", [(i, (i + 2 * hops) % count) for i in range(count)])


def replica_swap(value, bits):
    return lax.ppermute(value, "rep", [(i, i ^ bits) for i in range(4)])


def place_table():
    shard = lax.axis_index("fsdp")
    replica = lax.axis_index("rep")
    return jnp.stack([shard // 2, shard % 2, replica // 2, replica % 2]).astype(jnp.int32)


def barrier(*values):
    return lax.optimization_barrier(values)


def shift_all(piece, first=1, step=1):
    chips = lax.axis_size("fsdp") // 2
    return [chip_shift(piece, hop) for hop in range(first, chips, step)]


def swap_sides(along):
    return replica_swap(along, 1), replica_swap(along, 2)


def swap_diagonal(from_x, from_y):
    cut = from_x.shape[1] // 256 * 128
    return replica_swap(from_x[:, :cut], 2), replica_swap(from_y[:, cut:], 1)


def fetch_copies(place, targets, owns, pieces, chips, sems):
    chip, core, row_bit, col_bit = (place[i] for i in range(4))
    made = []

    def add(number, source, target):
        made.append((number, pltpu.make_async_copy(source, target, sems.at[len(made)])))

    for other in range(2):
        side = core ^ other
        height = pieces[other][0].shape[0] // (chips - 1)
        step = math.gcd(height, 16)
        for number, (target, stacked, column) in enumerate(targets):
            rows, width = target.shape[0] // (2 * chips), target.shape[1]
            start = pl.multiple_of((2 * chip + side) * rows, step)
            add(number, owns[other][number], target.at[pl.ds(start, rows), :])
            for hop in range(1, chips):
                shard = 2 * lax.rem(chip - hop + chips, chips) + side
                source_rows = pl.ds((hop - 1) * height, height)
                for flip in range(4):
                    across = row_bit ^ (flip // 2)
                    aside = col_bit ^ (flip % 2)
                    origin = pieces[other][flip]
                    if stacked:
                        for half in range(rows // (4 * height)):
                            row = shard * rows + (across * 2 + aside) * (rows // 4) + half * height
                            add(
                                number,
                                origin.at[source_rows, pl.ds(column + half * width, width)],
                                target.at[pl.ds(pl.multiple_of(row, step), height), :],
                            )
                    else:
                        row = pl.multiple_of(shard * rows + across * height, step)
                        col = pl.multiple_of(aside * (width // 2), 128)
                        add(
                            number,
                            origin.at[source_rows, pl.ds(column, width // 2)],
                            target.at[pl.ds(row, height), pl.ds(col, width // 2)],
                        )
    return made


def spread_copies(place, targets, small, blank, mine, theirs, chips, sems):
    core = place[1]
    made = []
    height = mine.shape[0] // (4 * chips)
    step = math.gcd(height, 16)
    for other, packed in ((1, theirs), (0, mine)):
        side = core ^ other
        for chip in range(chips):
            shard = 2 * chip + side
            for quarter in range(4):
                out_rows = pl.ds((chip * 4 + quarter) * height, height)
                moves = []
                column = 0
                for number, (target, stacked) in enumerate(targets):
                    rows = target.shape[0] // (2 * chips)
                    if stacked:
                        width = target.shape[1]
                        for half in range(rows // (4 * height)):
                            row = shard * rows + quarter * (rows // 4) + half * height
                            row = pl.multiple_of(row, step)
                            moves.append((number, target.at[pl.ds(row, height), :], column, width))
                            column += width
                    else:
                        width = target.shape[1] // 2
                        row = pl.multiple_of(shard * rows + (quarter // 2) * height, step)
                        cols = pl.ds((quarter % 2) * width, width)
                        moves.append((number, target.at[pl.ds(row, height), cols], column, width))
                        column += width
                if quarter == 0:
                    moves.append((len(targets), small.at[shard], column, 128))
                else:
                    moves.append((len(targets), blank.at[...], column, 128))
                for number, source, column, width in moves:
                    target = packed.at[out_rows, pl.ds(column, width)]
                    made.append(
                        (number, pltpu.make_async_copy(source, target, sems.at[len(made)]))
                    )
    return made


def run_copies(made):
    for _, copy in made:
        copy.start()
    for _, copy in made:
        copy.wait()


def add16(left, right):
    return left.astype(F32) + right.astype(F32)


def first_sum(height, place, mine, other, keep_a, send_a, keep_b, send_b):
    row_bit, col_bit = place[2], place[3]
    cut = keep_a.shape[1]
    step = math.gcd(height, 16)

    def piece(quarter, cols):
        rows = pl.ds(pl.multiple_of(quarter * height, step), height)
        return add16(mine[rows, cols], other[rows, cols]).astype(BF16)

    for bit in range(2):
        out = pl.ds(bit * height, height)
        keep_a[out, :] = piece(bit * 2 + col_bit, pl.ds(0, cut))
        send_a[out, :] = piece(bit * 2 + 1 - col_bit, pl.ds(0, cut))
        keep_b[out, :] = piece(row_bit * 2 + bit, pl.ds(cut, mine.shape[1] - cut))
        send_b[out, :] = piece((1 - row_bit) * 2 + bit, pl.ds(cut, mine.shape[1] - cut))


def second_sum(height, place, keep_a, got_a, keep_b, got_b, next_a, send_a, next_b, send_b):
    step = math.gcd(height, 16)
    for bit, keep, got, stay, send in (
        (place[2], keep_a, got_a, next_a, send_a),
        (place[3], keep_b, got_b, next_b, send_b),
    ):
        for which, out in ((bit, stay), (1 - bit, send)):
            rows = pl.ds(pl.multiple_of(which * height, step), height)
            out[...] = add16(keep[rows, :], got[rows, :]).astype(BF16)


def third_sum(height, place, keep_a, got_a, keep_b, got_b, own, *sends):
    chips = len(sends) + 1
    cut = keep_a.shape[1]
    step = math.gcd(height, 16)
    for hop, out in enumerate((own, *sends)):
        at = lax.rem(place[0] + hop, chips)
        rows = pl.ds(pl.multiple_of(at * height, step), height)
        out[:, :cut] = add16(keep_a[rows, :], got_a[rows, :]).astype(out.dtype)
        out[:, cut:] = add16(keep_b[rows, :], got_b[rows, :]).astype(out.dtype)


def fourth_sum(own, *refs):
    total = own[...]
    for ref in refs[:-1]:
        total = total + ref[...].astype(F32)
    refs[-1][...] = total.astype(BF16)


def last_spread(stacks, place, own, from_x, from_y, from_xy, *outs):
    replica = place[2] * 2 + place[3]
    height, packed = own.shape
    step = math.gcd(height, 16)
    for flip, source in enumerate((own, from_x, from_y, from_xy)):
        across = place[2] ^ (flip // 2)
        aside = place[3] ^ (flip % 2)
        column = 0
        for stacked, out in zip(stacks, outs):
            rows, width = out.shape
            if stacked:
                for half in range(rows // (4 * height)):
                    at = (across * 2 + aside) * (rows // 4) + half * height
                    out[pl.ds(pl.multiple_of(at, step), height), :] = source[
                        :, column : column + width
                    ].astype(F32)
                    column += width
            else:
                width = width // 2
                at = pl.ds(pl.multiple_of(across * height, step), height)
                cols = pl.ds(pl.multiple_of(aside * width, 128), width)
                out[at, cols] = source[:, column : column + width].astype(F32)
                column += width

        @pl.when((replica ^ flip) == 0)
        def _():
            outs[-1][...] = source[0:16, packed - 128 :].astype(F32)


def small_call(body, place, inputs, shapes, grid=None, in_specs=None, out_specs=None):
    if grid is None:
        grid = (1,)
        in_specs = [pl.BlockSpec(value.shape, lambda i, t: (0, 0)) for value in inputs]
        out_specs = [pl.BlockSpec(shape.shape, lambda i, t: (0, 0)) for shape in shapes]
    return pl.pallas_call(
        body,
        grid_spec=pltpu.PrefetchScalarGridSpec(
            num_scalar_prefetch=1, grid=grid, in_specs=in_specs, out_specs=out_specs
        ),
        out_shape=shapes,
        compiler_params=params(32),
    )(place, *inputs)


class Sum:
    def __init__(self, place, mine, theirs):
        self.place = place
        self.chips = lax.axis_size("fsdp") // 2
        self.height = mine.shape[0] // (4 * self.chips)
        self.packed = mine.shape[1]
        self.cut = self.packed // 256 * 128
        self.kept = [mine]
        self.sends = [theirs]
        self.ways = [core_swap]

    def send(self):
        return [way(value) for way, value in zip(self.ways, self.sends)]

    def shape(self, rows, cols, dtype=BF16):
        return jax.ShapeDtypeStruct((rows * self.height, cols), dtype)

    def block(self, count, cols):
        return pl.BlockSpec((count * self.height, cols), lambda i, t: (i, 0))

    def pair(self, make, rows):
        return [make(rows, self.cut)] * 2 + [make(rows, self.packed - self.cut)] * 2

    def add_first(self, arrived):
        keep_a, send_a, keep_b, send_b = small_call(
            functools.partial(first_sum, self.height),
            self.place,
            (*self.kept, *arrived),
            self.pair(self.shape, 2 * self.chips),
            (self.chips,),
            [self.block(4, self.packed)] * 2,
            self.pair(self.block, 2),
        )
        self.kept = [keep_a, keep_b]
        self.sends = [send_a, send_b]
        self.ways = [lambda v: replica_swap(v, 1), lambda v: replica_swap(v, 2)]

    def add_second(self, arrived):
        keep_a, send_a, keep_b, send_b = small_call(
            functools.partial(second_sum, self.height),
            self.place,
            (self.kept[0], arrived[0], self.kept[1], arrived[1]),
            self.pair(self.shape, self.chips),
            (self.chips,),
            self.pair(self.block, 2),
            self.pair(self.block, 1),
        )
        self.kept = [keep_a, keep_b]
        self.sends = [send_a, send_b]
        self.ways = [lambda v: replica_swap(v, 2), lambda v: replica_swap(v, 1)]

    def add_third(self, arrived):
        own, *self.sends = small_call(
            functools.partial(third_sum, self.height),
            self.place,
            (self.kept[0], arrived[0], self.kept[1], arrived[1]),
            [self.shape(1, self.packed, F32)] + [self.shape(1, self.packed)] * (self.chips - 1),
        )
        self.kept = [own]
        self.ways = [functools.partial(chip_shift, hops=hop) for hop in range(1, self.chips)]

    def add_fourth(self, arrived):
        (total,) = small_call(
            lambda table, *refs: fourth_sum(*refs),
            self.place,
            (*self.kept, *arrived),
            [self.shape(1, self.packed)],
        )
        self.kept = [total]
        self.sends = [total] * 3
        self.ways = [functools.partial(replica_swap, bits=bits) for bits in (1, 2, 3)]

    def result(self, arrived, stacks, out_shapes):
        return small_call(
            functools.partial(last_spread, stacks),
            self.place,
            (*self.kept, *arrived),
            [jax.ShapeDtypeStruct(s, F32) for s in out_shapes]
            + [jax.ShapeDtypeStruct((16, 128), F32)],
        )


def small_blocks(rows_of_shard, small, shards, own):
    small[...] = jnp.zeros_like(small)
    for shard in range(shards):
        rows = rows_of_shard(shard)
        small[shard, 0 : rows.shape[0], 0:own] = rows.astype(BF16)


def qkv_kernel(chips, place, tokens, vecs, *refs):
    owns = (refs[0:1], refs[1:2])
    pieces = (refs[2:6], refs[6:10])
    qkv, unit, weight, sems = refs[10:]
    width = tokens.shape[1]

    @pl.when(pl.program_id(0) == 0)
    def _():
        run_copies(fetch_copies(place, [(weight, False, 0)], owns, pieces, chips, sems))

    xhat, _ = normalise(tokens[...].astype(F32))
    unit[...] = xhat.astype(BF16)
    rows = (xhat * vecs[0:1, :] + vecs[1:2, :]).astype(BF16)
    query = dot(rows, weight[:, :width]) + vecs[2:3, :]
    qkv[:, :width] = query.astype(BF16) * jnp.asarray(0.125, BF16)
    qkv[:, width : 2 * width] = dot(rows, weight[:, width : 2 * width]).astype(BF16)
    value = dot(rows, weight[:, 2 * width :]) + vecs[3:4, :]
    qkv[:, 2 * width :] = value.astype(BF16)


def hbm():
    return pl.BlockSpec(memory_space=pl.ANY)


def qkv_forward(place, tokens, vecs, owns, pieces, block=512):
    rows, width = tokens.shape
    chips = lax.axis_size("fsdp") // 2
    sources = [*owns, *pieces[0], *pieces[1]]
    zero = lambda i, t: (0, 0)
    return pl.pallas_call(
        functools.partial(qkv_kernel, chips),
        grid_spec=pltpu.PrefetchScalarGridSpec(
            num_scalar_prefetch=1,
            grid=(rows // block,),
            in_specs=[
                pl.BlockSpec((block, width), lambda i, t: (i, 0)),
                pl.BlockSpec(vecs.shape, zero),
            ]
            + [hbm()] * len(sources),
            out_specs=[
                pl.BlockSpec((block, 3 * width), lambda i, t: (i, 0)),
                pl.BlockSpec((block, width), lambda i, t: (i, 0)),
                resident((width, 3 * width)),
            ],
            scratch_shapes=[pltpu.SemaphoreType.DMA((2 + 8 * (chips - 1),))],
        ),
        out_shape=[
            jax.ShapeDtypeStruct((rows, 3 * width), BF16),
            jax.ShapeDtypeStruct((rows, width), BF16),
            jax.ShapeDtypeStruct((width, 3 * width), BF16),
        ],
        compiler_params=params(60),
        cost_estimate=cost(12),
    )(place, tokens, vecs, *sources)


def clip_table(segment_ids, valid_mask):
    seq_len = segment_ids.shape[1]
    clips = jnp.arange(CLIPS, dtype=jnp.int32)[None, :, None]
    segments = segment_ids[:, None, :]
    start = jnp.sum((segments < clips).astype(jnp.int32), axis=2)
    end = jnp.sum((segments <= clips).astype(jnp.int32), axis=2)
    valid = jnp.sum(((segments == clips) & (valid_mask[:, None, :] == 1)).astype(jnp.int32), axis=2)
    aligned = start // 16 * 16
    need = end - aligned
    path = (need > WINDOW).astype(jnp.int32) + (need > 2 * WINDOW).astype(jnp.int32)
    window = jnp.where(path == 0, WINDOW, jnp.where(path == 1, 2 * WINDOW, seq_len))
    base = jnp.minimum(aligned, seq_len - window)
    return jnp.stack([base, path, start - base, end - base, start + valid - base], axis=2).reshape(
        -1
    )


def lane_low(rows):
    return lax.broadcasted_iota(jnp.int32, (rows, 128), 1) < 64


def flag_lane(rows):
    return lax.broadcasted_iota(jnp.int32, (rows, 128), 1) % 64 == 0


def row_mask(rows, offset, first, last):
    index = lax.broadcasted_iota(jnp.int32, (rows, 128), 0) + offset
    return (index >= first) & (index < last)


def key_extra(rows, first, last):
    bias = jnp.where(row_mask(rows, 0, first, last), 0.0, NEGATIVE)
    return jnp.where(flag_lane(rows), bias, 0.0).astype(BF16)


def query_extra(rows):
    return jnp.where(flag_lane(rows), 1.0, 0.0).astype(BF16)


def weights_of(query, keys, extra_query, extra_keys, low, low_keys, head):
    if head == 0:
        left = jnp.where(low, query, extra_query)
        right = jnp.where(low_keys, keys, extra_keys)
    else:
        left = jnp.where(low, extra_query, query)
        right = jnp.where(low_keys, extra_keys, keys)
    scores = dot_nt(left, right)
    return jnp.exp(scores - jnp.max(scores, axis=1, keepdims=True)).astype(BF16)


def attend_window(refs, base, first, last, valid_end, window, pairs, exps, clip):
    queries, keys_ref, values_ref, mixed, inverse = refs
    chunk = WINDOW
    low = lane_low(chunk)
    low_keys = lane_low(window)
    extra_keys = key_extra(window, first, valid_end)
    extra_query = query_extra(chunk)
    ones = jnp.ones((window, 128), BF16)
    key_rows = pl.ds(base, window)

    def one_chunk(offset, row_start):
        rows = pl.ds(row_start, chunk)
        keep = row_mask(chunk, offset, first, last)
        for pair in range(pairs):
            lanes = pl.ds(128 * pair, 128)
            query = queries[rows, lanes]
            keys = keys_ref[key_rows, lanes]
            stack = jnp.concatenate([values_ref[key_rows, lanes], ones], axis=1)
            sums = []
            for head in range(2):
                weights = weights_of(query, keys, extra_query, extra_keys, low, low_keys, head)
                if exps is not None:
                    exps[0, 2 * pair + head, pl.ds(clip * WINDOW, WINDOW), :] = weights
                sums.append(dot(weights, stack))
            total = jnp.where(low, sums[0][:, 128:], sums[1][:, 128:])
            weighted = jnp.where(low, sums[0][:, :128], sums[1][:, :128])
            reciprocal = 1.0 / total
            mixed[rows, lanes] = jnp.where(
                keep, (weighted * reciprocal), mixed[rows, lanes].astype(F32)
            ).astype(BF16)
            inverse[rows, lanes] = jnp.where(keep, reciprocal, inverse[rows, lanes])

    if window == chunk:
        one_chunk(0, base)
    else:

        def step(index, carry):
            offset = index * chunk
            one_chunk(offset, pl.multiple_of(base + offset, 16))
            return carry

        lax.fori_loop(0, window // chunk, step, 0)


def clip_fields(table, sequence, clip):
    at = (sequence * CLIPS + clip) * FIELDS
    base = pl.multiple_of(table[at], 16)
    return base, table[at + 1], table[at + 2], table[at + 3], table[at + 4]


def loop_clips(table, sequence, one_clip, some_clips):
    longest = 0
    for clip in range(CLIPS):
        longest = jnp.maximum(longest, clip_fields(table, sequence, clip)[1])

    @pl.when(longest == 0)
    def _():
        lax.fori_loop(0, CLIPS // TOGETHER, some_clips, 0)

    @pl.when(longest > 0)
    def _():
        lax.fori_loop(0, CLIPS, one_clip, 0)


def attend_kernel(pairs, table, queries, keys, values, mixed, inverse, exps):
    sequence = pl.program_id(0)
    seq_len = queries.shape[0]
    mixed[...] = jnp.zeros_like(mixed)
    inverse[...] = jnp.zeros_like(inverse)
    refs = (queries, keys, values, mixed, inverse)

    def one_clip(clip, carry):
        base, path, first, last, valid_end = clip_fields(table, sequence, clip)
        for number, window in enumerate((WINDOW, 2 * WINDOW, seq_len)):

            @pl.when(path == number)
            def _():
                attend_window(
                    refs,
                    base,
                    first,
                    last,
                    valid_end,
                    window,
                    pairs,
                    exps if number == 0 else None,
                    clip,
                )

        return carry

    def some_clips(index, carry):
        for clip in range(TOGETHER):
            clip = index * TOGETHER + clip
            base, _, first, last, valid_end = clip_fields(table, sequence, clip)
            attend_window(refs, base, first, last, valid_end, WINDOW, pairs, exps, clip)
        return carry

    loop_clips(table, sequence, one_clip, some_clips)


def attend_forward(table, qkv, seq_len, group, pairs=2):
    rows = qkv.shape[0]
    width = qkv.shape[1] // 3
    seqs = rows // seq_len
    lanes = 128 * pairs
    groups = width // lanes
    block = (seq_len, lanes)
    own = pl.BlockSpec(block, lambda s, t: (s, 0))
    return pl.pallas_call(
        functools.partial(attend_kernel, pairs),
        grid_spec=pltpu.PrefetchScalarGridSpec(
            num_scalar_prefetch=1,
            grid=(seqs,),
            in_specs=[
                pl.BlockSpec(block, lambda s, t: (s, group)),
                pl.BlockSpec(block, lambda s, t: (s, groups + group)),
                pl.BlockSpec(block, lambda s, t: (s, 2 * groups + group)),
            ],
            out_specs=[
                own,
                own,
                pl.BlockSpec((1, 2 * pairs, CLIPS * WINDOW, WINDOW), lambda s, t: (s, 0, 0, 0)),
            ],
        ),
        out_shape=[
            jax.ShapeDtypeStruct((rows, lanes), BF16),
            jax.ShapeDtypeStruct((rows, lanes), F32),
            jax.ShapeDtypeStruct((seqs, 2 * pairs, CLIPS * WINDOW, WINDOW), BF16),
        ],
        compiler_params=params(60),
        cost_estimate=cost(10),
    )(table, qkv, qkv, qkv)


def back_window(refs, base, first, last, valid_end, window, pairs, exps, clip, gather):
    queries, keys_ref, values_ref, grads, mixed, inverse, dq, dk, dv = refs
    key_grad, value_grad = gather
    chunk = WINDOW
    single = window == chunk
    low = lane_low(chunk)
    low_keys = lane_low(window)
    extra_keys = None if single else key_extra(window, first, valid_end)
    extra_query = None if single else query_extra(chunk)
    key_rows = pl.ds(base, window)
    one = jnp.ones((window, 128), BF16)

    def one_chunk(offset, row_start):
        rows = pl.ds(row_start, chunk)
        keep = row_mask(chunk, offset, first, last)
        for pair in range(pairs):
            lanes = pl.ds(128 * pair, 128)
            query = queries[rows, lanes]
            keys = keys_ref[key_rows, lanes]
            values = values_ref[key_rows, lanes]
            scaled = jnp.where(keep, grads[rows, lanes].astype(F32) * inverse[rows, lanes], 0.0)
            product = scaled * mixed[rows, lanes].astype(F32)
            turned = pltpu.roll(-product, 64, 1).astype(BF16)
            scaled = scaled.astype(BF16)
            parts = []
            for head in range(2):
                if head == 0:
                    left = jnp.where(low, scaled, turned)
                    right = jnp.where(low_keys, values, one)
                else:
                    left = jnp.where(low, turned, scaled)
                    right = jnp.where(low_keys, one, values)
                if single:
                    weights = exps[0, 2 * pair + head, pl.ds(clip * WINDOW, WINDOW), :]
                else:
                    weights = weights_of(query, keys, extra_query, extra_keys, low, low_keys, head)
                grad_scores = (weights.astype(F32) * dot_nt(left, right)).astype(BF16)
                parts.append(
                    (
                        dot(grad_scores, keys),
                        dot_tn(grad_scores, query),
                        dot_tn(weights, scaled),
                    )
                )
            query_part = jnp.where(low, parts[0][0], parts[1][0]) * 0.125
            key_part = jnp.where(low_keys, parts[0][1], parts[1][1])
            value_part = jnp.where(low_keys, parts[0][2], parts[1][2])
            dq[rows, lanes] = jnp.where(keep, query_part, dq[rows, lanes].astype(F32)).astype(BF16)
            if single:
                dk[rows, lanes] = jnp.where(keep, key_part, dk[rows, lanes].astype(F32)).astype(
                    BF16
                )
                dv[rows, lanes] = jnp.where(keep, value_part, dv[rows, lanes].astype(F32)).astype(
                    BF16
                )
            else:
                key_grad[pl.ds(0, window), lanes] += key_part
                value_grad[pl.ds(0, window), lanes] += value_part

    if single:
        one_chunk(0, base)
        return
    key_grad[...] = jnp.zeros_like(key_grad)
    value_grad[...] = jnp.zeros_like(value_grad)

    def step(index, carry):
        offset = index * chunk
        one_chunk(offset, pl.multiple_of(base + offset, 16))
        return carry

    lax.fori_loop(0, window // chunk, step, 0)
    keep = row_mask(window, 0, first, last)
    for pair in range(pairs):
        lanes = pl.ds(128 * pair, 128)
        for ref, total in ((dk, key_grad), (dv, value_grad)):
            ref[key_rows, lanes] = jnp.where(
                keep, total[pl.ds(0, window), lanes], ref[key_rows, lanes].astype(F32)
            ).astype(BF16)


def back_kernel(
    pairs,
    table,
    queries,
    keys,
    values,
    grads,
    mixed,
    inverse,
    exps,
    dq,
    dk,
    dv,
    key_grad,
    value_grad,
):
    sequence = pl.program_id(0)
    seq_len = queries.shape[0]
    for ref in (dq, dk, dv):
        ref[...] = jnp.zeros_like(ref)
    refs = (queries, keys, values, grads, mixed, inverse, dq, dk, dv)

    gather = (key_grad, value_grad)

    def one_clip(clip, carry):
        base, path, first, last, valid_end = clip_fields(table, sequence, clip)
        for number, window in enumerate((WINDOW, 2 * WINDOW, seq_len)):

            @pl.when(path == number)
            def _():
                back_window(
                    refs, base, first, last, valid_end, window, pairs, exps, clip, gather
                )

        return carry

    def some_clips(index, carry):
        for clip in range(TOGETHER):
            clip = index * TOGETHER + clip
            base, _, first, last, valid_end = clip_fields(table, sequence, clip)
            back_window(refs, base, first, last, valid_end, WINDOW, pairs, exps, clip, gather)
        return carry

    loop_clips(table, sequence, one_clip, some_clips)


def attend_backward(table, qkv, grads, mixed, inverse, exps, seq_len, group, pairs=2):
    rows = mixed.shape[0]
    seqs = rows // seq_len
    lanes = 128 * pairs
    groups = grads.shape[1] // lanes
    block = (seq_len, lanes)
    own = pl.BlockSpec(block, lambda s, t: (s, 0))
    shape = jax.ShapeDtypeStruct((rows, lanes), BF16)
    return pl.pallas_call(
        functools.partial(back_kernel, pairs),
        grid_spec=pltpu.PrefetchScalarGridSpec(
            num_scalar_prefetch=1,
            grid=(seqs,),
            in_specs=[
                pl.BlockSpec(block, lambda s, t: (s, group)),
                pl.BlockSpec(block, lambda s, t: (s, groups + group)),
                pl.BlockSpec(block, lambda s, t: (s, 2 * groups + group)),
                pl.BlockSpec(block, lambda s, t: (s, group)),
                own,
                own,
                pl.BlockSpec((1, 2 * pairs, CLIPS * WINDOW, WINDOW), lambda s, t: (s, 0, 0, 0)),
            ],
            out_specs=[own, own, own],
            scratch_shapes=[pltpu.VMEM(block, F32), pltpu.VMEM(block, F32)],
        ),
        out_shape=[shape, shape, shape],
        compiler_params=params(60),
        cost_estimate=cost(19),
    )(table, qkv, qkv, qkv, grads, mixed, inverse, exps)


def gauss(value):
    cdf = 0.5 + 0.5 * lax.erf(value * 0.7071067811865476)
    tail = jnp.exp2(value * value * (-0.5 * 1.4426950408889634))
    return cdf, value * tail * 0.3989422804014327


def middle_kernel(
    part,
    chips,
    groups,
    place,
    tokens,
    cotangent,
    vecs,
    ebias,
    *refs,
):
    mixed, refs = refs[:groups], refs[groups:]
    owns = (refs[0:3], refs[3:6])
    pieces = (refs[6:10], refs[10:14])
    (
        output,
        grad_middle,
        grad_mixed,
        mine,
        theirs,
        proj,
        expand,
        reduce,
        sum_proj,
        sum_expand,
        sum_reduce,
        sum_ebias,
        sum_vecs,
        middle,
        units,
        scales,
        normed,
        normed_t,
        grad_normed,
        activated,
        grad_hidden,
        small,
        blank,
        in_sems,
        out_sems,
    ) = refs[14:]
    step = pl.program_id(0)
    width, hidden = expand.shape
    block = tokens.shape[0]
    half = block // 2
    own = width // (2 * chips)
    targets = [
        (proj, False, 0),
        (expand, False, width // 2),
        (reduce, True, width // 2 + hidden // 2),
    ]

    @pl.when(step == 0)
    def _():
        made = fetch_copies(place, targets, owns, pieces, chips, in_sems)
        for _, copy in made:
            copy.start()
        sum_proj[...] = jnp.zeros_like(sum_proj)
        sum_expand[...] = jnp.zeros_like(sum_expand)
        sum_reduce[...] = jnp.zeros_like(sum_reduce)
        sum_ebias[...] = jnp.zeros_like(sum_ebias)
        sum_vecs[...] = jnp.zeros_like(sum_vecs)
        for _, copy in made:
            copy.wait()

    def norm_rows(first, count):
        rows = pl.ds(first, count)
        xhat, scale = normalise(middle[rows, :])
        units[rows, :] = xhat
        scales[rows, :] = scale
        normed[rows, :] = (xhat * vecs[5:6, :] + vecs[6:7, :]).astype(BF16)

    def hidden_part(which, start):
        rows = pl.ds(which * half, half)
        cols = pl.ds(start, part)
        into = expand[:, cols]
        back = reduce[cols, :]
        preact = dot(normed[rows, :], into) + ebias[:, cols]
        cdf, slope = gauss(preact)
        active = (preact * cdf).astype(BF16)
        activated[rows, cols] = active
        grad_preact = (dot_nt(cotangent[rows, :], back) * (cdf + slope)).astype(BF16)
        grad_hidden[rows, cols] = grad_preact
        sum_ebias[:, cols] += jnp.sum(grad_preact.astype(F32), axis=0, keepdims=True)
        middle[rows, :] += dot(active, back)
        grad_normed[rows, :] += dot_nt(grad_preact, into)

    def end_rows(first, count):
        rows = pl.ds(first, count)
        upstream = grad_normed[rows, :]
        xhat = units[rows, :]
        output[rows, :] = (middle[rows, :] + vecs[7:8, :]).astype(BF16)
        cot = cotangent[rows, :].astype(F32)
        grads = cot + norm_back(upstream, vecs[5:6, :], xhat, scales[rows, :])
        attended = grads.astype(BF16)
        grad_middle[rows, :] = attended
        sum_vecs[0:1, :] += jnp.sum(attended.astype(F32), axis=0, keepdims=True)
        sum_vecs[1:2, :] += jnp.sum(upstream * xhat, axis=0, keepdims=True)
        sum_vecs[2:3, :] += jnp.sum(upstream, axis=0, keepdims=True)
        sum_vecs[3:4, :] += jnp.sum(cot, axis=0, keepdims=True)

    mixed_rows = jnp.concatenate([ref[...] for ref in mixed], axis=1)
    middle[...] = tokens[...].astype(F32) + dot(mixed_rows, proj[...]) + vecs[4:5, :]
    parts = hidden // part
    piece = half // parts
    grad_normed[...] = jnp.zeros_like(grad_normed)
    norm_rows(0, half)

    def first_half(index, carry):
        hidden_part(0, pl.multiple_of(index * part, part))
        norm_rows(pl.multiple_of(half + index * piece, piece), piece)
        return carry

    lax.fori_loop(0, parts, first_half, 0)
    normed_t[...] = normed[...].T

    def second_half(index, carry):
        start = pl.multiple_of(index * part, part)
        hidden_part(1, start)
        cols = pl.ds(start, part)
        sum_reduce[cols, :] += dot_tn(activated[:, cols], cotangent[...])
        sum_expand[:, cols] += dot(normed_t[...], grad_hidden[:, cols])
        end_rows(pl.multiple_of(index * piece, piece), piece)
        return carry

    lax.fori_loop(0, parts, second_half, 0, unroll=4)
    end_rows(half, half)
    attended = grad_middle[...]
    grad_mixed[...] = dot_nt(attended, proj[...]).astype(BF16)
    sum_proj[...] += dot_tn(mixed_rows, attended)

    @pl.when(step == pl.num_programs(0) - 1)
    def _():
        blank[...] = jnp.zeros_like(blank)
        per = hidden // width

        def rows_of_shard(shard):
            rows = [sum_vecs[0:4, shard * own : (shard + 1) * own]]
            for index in range(per):
                at = (shard * per + index) * own
                rows.append(sum_ebias[0:1, at : at + own])
            return jnp.concatenate(rows, axis=0)

        small_blocks(rows_of_shard, small, 2 * chips, own)
        made = spread_copies(
            place,
            [(proj, False), (expand, False), (reduce, True)],
            small,
            blank,
            mine,
            theirs,
            chips,
            out_sems,
        )
        for number, (low, total) in enumerate(
            ((proj, sum_proj), (expand, sum_expand), (reduce, sum_reduce))
        ):
            low[...] = total[...].astype(BF16)
            for which, copy in made:
                if which == number or (which == 3 and number == 0):
                    copy.start()
        for _, copy in made:
            copy.wait()


def middle_all(
    place, tokens, mixed, cotangent, vecs, ebias, owns, others, pieces, block=512, part=768
):
    rows, width = tokens.shape
    chips = lax.axis_size("fsdp") // 2
    hidden = ebias.shape[1]
    height = width // (4 * chips)
    row_block = pl.BlockSpec((block, width), lambda i, t: (i, 0))
    row_shape = jax.ShapeDtypeStruct((rows, width), BF16)
    packed = (4 * chips * height, width // 2 + hidden // 2 + hidden // 2 + 128)
    packed_shape = jax.ShapeDtypeStruct(packed, BF16)
    sources = [*owns, *others, *pieces[0], *pieces[1]]
    halves = hidden // width // 2
    mixed_block = pl.BlockSpec((block, mixed[0].shape[1]), lambda i, t: (i, 0))
    return pl.pallas_call(
        functools.partial(middle_kernel, part, chips, len(mixed)),
        grid_spec=pltpu.PrefetchScalarGridSpec(
            num_scalar_prefetch=1,
            grid=(rows // block,),
            in_specs=[row_block] * 2
            + [
                pl.BlockSpec(vecs.shape, lambda i, t: (0, 0)),
                pl.BlockSpec(ebias.shape, lambda i, t: (0, 0)),
            ]
            + [mixed_block] * len(mixed)
            + [hbm()] * len(sources),
            out_specs=[row_block] * 3 + [hbm(), hbm()],
            scratch_shapes=[
                pltpu.VMEM((width, width), BF16),
                pltpu.VMEM((width, hidden), BF16),
                pltpu.VMEM((hidden, width), BF16),
                pltpu.VMEM((width, width), F32),
                pltpu.VMEM((width, hidden), F32),
                pltpu.VMEM((hidden, width), F32),
                pltpu.VMEM((1, hidden), F32),
                pltpu.VMEM((8, width), F32),
                pltpu.VMEM((block, width), F32),
                pltpu.VMEM((block, width), F32),
                pltpu.VMEM((block, 1), F32),
                pltpu.VMEM((block, width), BF16),
                pltpu.VMEM((width, block), BF16),
                pltpu.VMEM((block, width), F32),
                pltpu.VMEM((block, hidden), BF16),
                pltpu.VMEM((block, hidden), BF16),
                pltpu.VMEM((2 * chips, height, 128), BF16),
                pltpu.VMEM((height, 128), BF16),
                pltpu.SemaphoreType.DMA((2 * (3 + 4 * (chips - 1) * (2 + halves)),)),
                pltpu.SemaphoreType.DMA((8 * chips * (3 + halves),)),
            ],
        ),
        out_shape=[row_shape, row_shape, row_shape, packed_shape, packed_shape],
        compiler_params=params(63),
        cost_estimate=cost(110),
    )(place, tokens, cotangent, vecs, ebias, *mixed, *sources)


def weight_kernel(chips, offsets, place, unit, vecs, weight, *refs):
    count = len(offsets)
    parts, refs = refs[:count], refs[count:]
    mine, theirs, total, sums, low, small, blank, sems = refs
    step = pl.program_id(0)
    width = unit.shape[1]
    lanes = parts[0].shape[1]
    own = width // (2 * chips)

    @pl.when(step == 0)
    def _():
        total[...] = jnp.zeros_like(total)
        sums[...] = jnp.zeros_like(sums)

    rows_t = unit[...].T
    for index, part in enumerate(parts):
        cols = slice(index * lanes, (index + 1) * lanes)
        total[:, cols] += dot(rows_t, part[...])
        sums[0:1, cols] += jnp.sum(part[...].astype(F32), axis=0, keepdims=True)

    @pl.when(step == pl.num_programs(0) - 1)
    def _():
        columns = vecs[...].T
        gain, shift = columns[:, 0:1], columns[:, 1:2]
        gain_part = jnp.zeros((width, 1), F32)
        shift_part = jnp.zeros((width, 1), F32)
        empty = jnp.zeros((1, lanes), F32)
        biases = [[empty] * (width // lanes) for _ in range(3)]
        for index, offset in enumerate(offsets):
            cols = slice(index * lanes, (index + 1) * lanes)
            raw = total[:, cols]
            sides = weight[:, offset : offset + lanes].astype(F32)
            line = sums[0:1, cols]
            gain_part += jnp.sum(raw * sides, axis=1, keepdims=True)
            shift_part += jnp.sum(line * sides, axis=1, keepdims=True)
            low[:, cols] = (gain * raw + shift * line).astype(BF16)
            biases[offset // width][offset % width // lanes] = line
        pick = lax.broadcasted_iota(jnp.int32, (width, 128), 1)
        both = jnp.where(pick == 0, gain_part, jnp.where(pick == 1, shift_part, 0.0)).T
        query_line = jnp.concatenate(biases[0], axis=1)
        value_line = jnp.concatenate(biases[2], axis=1)
        blank[...] = jnp.zeros_like(blank)

        def rows_of_shard(shard):
            cols = slice(shard * own, (shard + 1) * own)
            return jnp.concatenate([both[0:2, cols], query_line[:, cols], value_line[:, cols]], axis=0)

        small_blocks(rows_of_shard, small, 2 * chips, own)
        run_copies(
            spread_copies(place, [(low, False)], small, blank, mine, theirs, chips, sems)
        )


def qkv_weight_grad(place, unit, vecs, weight, groups, grads, block=512):
    rows, width = unit.shape
    lanes = grads[0][0].shape[1]
    chips = lax.axis_size("fsdp") // 2
    height = width // (4 * chips)
    offsets = tuple(part * width + group * lanes for part in range(3) for group in groups)
    parts = [grad[part] for part in range(3) for grad in grads]
    columns = lanes * len(parts)
    packed = jax.ShapeDtypeStruct((4 * chips * height, columns // 2 + 128), BF16)
    zero = lambda i, t: (0, 0)
    return pl.pallas_call(
        functools.partial(weight_kernel, chips, offsets),
        grid_spec=pltpu.PrefetchScalarGridSpec(
            num_scalar_prefetch=1,
            grid=(rows // block,),
            in_specs=[
                pl.BlockSpec((block, width), lambda i, t: (i, 0)),
                pl.BlockSpec(vecs.shape, zero),
                resident(weight.shape),
            ]
            + [pl.BlockSpec((block, lanes), lambda i, t: (i, 0))] * len(parts),
            out_specs=[hbm(), hbm()],
            scratch_shapes=[
                pltpu.VMEM((width, columns), F32),
                pltpu.VMEM((8, columns), F32),
                pltpu.VMEM((width, columns), BF16),
                pltpu.VMEM((2 * chips, height, 128), BF16),
                pltpu.VMEM((height, 128), BF16),
                pltpu.SemaphoreType.DMA((16 * chips,)),
            ],
        ),
        out_shape=[packed, packed],
        compiler_params=params(60),
        cost_estimate=cost(4 * len(groups)),
    )(place, unit, vecs, weight, *parts)


def input_kernel(count, tokens, grad_middle, vecs, weight, *refs):
    width = tokens.shape[1]
    lanes = width // count
    input_grad = refs[-1]
    xhat, scale = normalise(tokens[...].astype(F32))
    upstream = None
    for part in range(3):
        rows = jnp.concatenate([ref[...] for ref in refs[part * count : (part + 1) * count]], axis=1)
        term = dot_nt(rows, weight[:, part * width : (part + 1) * width])
        upstream = term if upstream is None else upstream + term
    grads = norm_back(upstream, vecs[0:1, :], xhat, scale)
    input_grad[...] = (grad_middle[...].astype(F32) + grads).astype(BF16)


def input_backward(tokens, grad_middle, vecs, weight, grads, first, rows, into=None, block=512):
    width = tokens.shape[1]
    lanes = grads[0][0].shape[1]
    start = first // block
    row_block = pl.BlockSpec((block, width), lambda i: (i + start, 0))
    parts = [grad[part] for part in range(3) for grad in grads]
    inputs = [tokens, grad_middle, vecs, weight, *parts]
    specs = [row_block] * 2 + [resident(vecs.shape), resident(weight.shape)]
    specs += [pl.BlockSpec((block, lanes), lambda i: (i + start, 0))] * len(parts)
    aliases = {}
    if into is not None:
        aliases = {len(inputs): 0}
        inputs.append(into)
        specs.append(hbm())
    return pl.pallas_call(
        functools.partial(input_kernel, len(grads)),
        grid=(rows // block,),
        in_specs=specs,
        out_specs=row_block,
        out_shape=jax.ShapeDtypeStruct(tokens.shape, BF16),
        input_output_aliases=aliases,
        compiler_params=params(60),
        cost_estimate=cost(7),
    )(*inputs)


def local(
    tokens,
    segment_ids,
    valid_mask,
    cotangent,
    norm1_gain,
    norm1_bias,
    qkv_weight,
    query_bias,
    value_bias,
    proj_weight,
    proj_bias,
    norm2_gain,
    norm2_bias,
    expand_weight,
    expand_bias,
    reduce_weight,
    reduce_bias,
):
    seq_len = segment_ids.shape[1]
    own, width = proj_weight.shape
    shards = lax.axis_size("fsdp")
    chips = shards // 2
    height = own // 2
    per = expand_bias.shape[0] // own
    place = place_table()
    row_bit, col_bit = place[2], place[3]

    def tile(weight):
        half = weight.shape[1] // 2
        return lax.dynamic_slice(weight, (row_bit * height, col_bit * half), (height, half))

    small = jnp.stack(
        [
            norm1_gain,
            norm1_bias,
            query_bias,
            value_bias,
            proj_bias,
            norm2_gain,
            norm2_bias,
            reduce_bias,
            *jnp.split(expand_bias, per),
        ]
    )
    block = jnp.pad(small, ((0, height - small.shape[0]), (0, 128 - own)))
    piece = jnp.concatenate([tile(qkv_weight), block], axis=1)
    quarter = lax.dynamic_slice(
        reduce_weight,
        ((row_bit * 2 + col_bit) * (per * own // 4), 0),
        (per * own // 4, width),
    )
    parts = [tile(proj_weight), tile(expand_weight), *jnp.split(quarter, per // 2, axis=0)]
    rest = jnp.concatenate(parts, axis=1)
    table = clip_table(segment_ids, valid_mask)
    owns = (proj_weight, expand_weight, reduce_weight)

    got = shift_all(piece)
    other_qkv, small_other = core_swap(qkv_weight), core_swap(small)
    got, other_qkv, small_other, rest, table = barrier(got, other_qkv, small_other, rest, table)
    along = jnp.concatenate(got, axis=0)
    sides = swap_sides(along)
    odd = shift_all(rest, 1, 2)
    sides, along = barrier(sides, along)
    halves = swap_diagonal(*sides)
    halves, sides, along, odd, rest = barrier(halves, sides, along, odd, rest)
    here = (along, *sides, jnp.concatenate(halves, axis=1))
    qkv_pieces = barrier(here, tuple(core_swap(part) for part in here))

    chip, core = place[0], place[1]
    edge = piece.shape[1] - 128

    def blocks_of(first, along):
        rest = along.reshape(chips - 1, height, -1)[:, : small.shape[0], edge : edge + own]
        return jnp.concatenate([first[None], rest], axis=0)

    both = jnp.stack(
        [blocks_of(small, qkv_pieces[0][0]), blocks_of(small_other, qkv_pieces[1][0])], axis=1
    )
    hops = (chip - jnp.arange(chips)) % chips
    choice = (hops[:, None, None, None] == jnp.arange(chips)[None, None, :, None]) & (
        (jnp.arange(2) ^ core)[None, :, None, None] == jnp.arange(2)[None, None, None, :]
    )
    small = jnp.sum(
        jnp.where(choice[..., None, None], both[None, None].astype(F32), 0.0), axis=(2, 3)
    ).reshape(shards, small.shape[0], own)
    vecs = small[:, :8].swapaxes(0, 1).reshape(8, width)
    ebias = small[:, 8:].reshape(1, width * per)

    qkv, unit, qkv_full = qkv_forward(
        place, tokens, vecs, (qkv_weight, other_qkv), qkv_pieces
    )
    even = shift_all(rest, 2, 2)
    even, qkv, unit, qkv_full = barrier(even, qkv, unit, qkv_full)

    along = jnp.concatenate(
        [(even, odd)[hop % 2][(hop - 1) // 2] for hop in range(1, chips)], axis=0
    )
    along, qkv = barrier(along, qkv)
    sides = swap_sides(along)
    others = [core_swap(weight) for weight in owns]
    forward = [attend_forward(table, qkv, seq_len, 0)]
    forward, now, others = barrier(forward, qkv, others)
    forward.append(attend_forward(table, now, seq_len, 1))
    sides, forward, now, along = barrier(sides, forward, now, along)
    halves = swap_diagonal(*sides)
    swapped = [core_swap(part) for part in (along, *sides)]
    forward.append(attend_forward(table, now, seq_len, 2))
    halves, swapped, forward = barrier(halves, swapped, forward)
    diagonal = jnp.concatenate(halves, axis=1)
    rest_pieces = ((along, *sides, diagonal), (*swapped, core_swap(diagonal)))
    mixed = [result[0] for result in forward]

    output, grad_middle, grad_mixed, mine, theirs = middle_all(
        place, tokens, mixed, cotangent, vecs, ebias, owns, others, rest_pieces
    )

    def back(group, grads):
        return attend_backward(table, qkv, grads, *forward[group], seq_len, group)

    middle_sum = Sum(place, mine, theirs)
    moving = middle_sum.send()
    backward = [back(0, grad_mixed)]
    moving, backward, grad_mixed = barrier(moving, backward, grad_mixed)
    middle_sum.add_first(moving)
    middle_sum.sends, grad_mixed = barrier(middle_sum.sends, grad_mixed)
    moving = middle_sum.send()
    backward.append(back(1, grad_mixed))
    backward, grad_mixed = barrier(backward, grad_mixed)
    backward.append(back(2, grad_mixed))
    moving, backward, unit = barrier(moving, backward, unit)
    middle_sum.add_second(moving)
    middle_sum.sends, unit = barrier(middle_sum.sends, unit)
    moving = middle_sum.send()
    mine, theirs = qkv_weight_grad(place, unit, vecs, qkv_full, (0, 1, 2), backward)
    moving, mine, theirs = barrier(moving, mine, theirs)
    middle_sum.add_third(moving)
    middle_sum.sends, theirs, tokens = barrier(middle_sum.sends, theirs, tokens)
    qkv_sum = Sum(place, mine, theirs)
    moving = middle_sum.send()
    qkv_moving = qkv_sum.send()
    half = seq_len
    input_grad = input_backward(tokens, grad_middle, vecs, qkv_full, backward, 0, half)
    qkv_moving, input_grad, tokens = barrier(qkv_moving, input_grad, tokens)
    qkv_sum.add_first(qkv_moving)
    qkv_sum.sends, tokens = barrier(qkv_sum.sends, tokens)
    qkv_moving = qkv_sum.send()
    input_grad = input_backward(
        tokens, grad_middle, vecs, qkv_full, backward, half, half, input_grad
    )
    qkv_moving, input_grad = barrier(qkv_moving, input_grad)
    qkv_sum.add_second(qkv_moving)
    qkv_moving = qkv_sum.send()
    moving, qkv_moving = barrier(moving, qkv_moving)
    qkv_sum.add_third(qkv_moving)
    qkv_moving = qkv_sum.send()
    middle_sum.add_fourth(moving)
    moving = middle_sum.send()
    qkv_sum.add_fourth(qkv_moving)
    qkv_moving = qkv_sum.send()
    sum_proj, sum_expand, sum_reduce, middle_small = middle_sum.result(
        moving,
        (False, False, True),
        (proj_weight.shape, expand_weight.shape, reduce_weight.shape),
    )
    sum_qkv, qkv_small = qkv_sum.result(qkv_moving, (False,), (qkv_weight.shape,))
    return (
        output,
        input_grad,
        qkv_small[0, :own],
        qkv_small[1, :own],
        sum_qkv,
        qkv_small[2, :own],
        qkv_small[3, :own],
        sum_proj,
        middle_small[0, :own],
        middle_small[1, :own],
        middle_small[2, :own],
        sum_expand,
        middle_small[4 : 4 + per, :own].reshape(-1),
        sum_reduce,
        middle_small[3, :own],
    )


def solution(mesh):
    rows = P(("rep", "fsdp"), None)
    vector = P("fsdp")
    matrix = P("fsdp", None)
    params_specs = (
        vector,
        vector,
        matrix,
        vector,
        vector,
        matrix,
        vector,
        vector,
        vector,
        matrix,
        vector,
        matrix,
        vector,
    )
    return jax.shard_map(
        local,
        mesh=mesh,
        in_specs=(rows, rows, rows, rows) + params_specs,
        out_specs=(rows, rows) + params_specs,
        check_vma=False,
    )
```
